128 devices in a mesh: sample: 16 (over z_lo, y, core), token: 8 (over x, z_hi).
Axes of the slice: x: 4, y: 4, z: 4 (z_hi: 2, z_lo: 2; z = z_hi * 2 + z_lo), core: 2. Of those that a mesh axis runs over, the one named last changes fastest.
Arguments:
- activations: bfloat16 [32, 1024, 768], P('sample', 'token'), may hold values from -100 to 100
- levels: int32 [32], P('sample'), may hold values from 0 to 199
- ada_table: bfloat16 [200, 1536], replicated, may hold values from -1.796875 to 1.796875
- input_weight: bfloat16 [768, 3072], replicated, may hold values from -0.21875 to 0.21875
- output_matrix: bfloat16 [768, 768], replicated, may hold values from -0.21875 to 0.21875
- pair_feats: bfloat16 [1024, 1024, 128], P('token', 'sample'), may hold values from -51 to 51
- pair_weight: bfloat16 [128, 16], replicated, as said below
- cross_bias: float32 [16], replicated, may hold values from -2 to 2
- chains: int32 [1024], replicated, may hold values from 0 to 7, never falling along the last dimension, each value on 1 to 512 neighbouring positions
- cotangent: bfloat16 [32, 1024, 768], P('sample', 'token'), may hold values from -6 to 6
Outputs:
- updated: bfloat16 [32, 1024, 768], P('sample', 'token')
- grad_tokens: bfloat16 [32, 1024, 768], P('sample', 'token')
- grad_pair: bfloat16 [1024, 1024, 128], P('token', 'sample')
- input_weight_grad: float32 [768, 3072], replicated
- output_weight_grad: float32 [768, 768], replicated
- grad_pair_weight: float32 [128, 16], replicated
- grad_cross: float32 [16], replicated
- grad_table: float32 [200, 1536], replicated
The draws below stay inside these ranges and needn't reach their ends.
Inputs may be any that keep to these rules, and one draw needn't show every extreme that they name: `chains`: chain ids never fall along the tokens. `pair_weight`: entries lie within 4 / sqrt(128) of zero.
All inputs are finite; a program needn't handle non-finite values.
Results may differ from the reference program's by a relative error of at most 0.035.
Values may be sent and summed in bfloat16 or wider, within the bound.
No kernel may reach another device: no remote copies, remote signals or barrier semaphores. Data moves between devices by JAX's collectives and lax.ppermute only.
A program may use at most 192 MiB of HBM per device.

```python
import math
import jax
import jax.numpy as jnp
import numpy as np
from jax import lax

MODEL_WIDTH = 768
H = 16
C = 128
LEVELS = 200
CHAINS = 8
N = 1024
S = 32


def shared_weight(key):
    draw_key = jax.random.fold_in(key, 101)
    return jnp.clip(jax.random.normal(draw_key, (C, H), jnp.float32), -4.0, 4.0) / math.sqrt(C)


def draw_pair_weight(key, part):
    weight = shared_weight(key)
    return weight.astype(jnp.bfloat16)


def draw_pair_feats(key, part):
    key = jax.random.fold_in(key, 5)
    entries = jnp.clip(jax.random.normal(key, (N, N, C), jnp.float32), -6.0, 6.0)
    return entries.astype(jnp.bfloat16)


def draw_activations(key, part):
    key = jax.random.fold_in(key, 7)
    entries = jnp.clip(jax.random.normal(key, (S, N, MODEL_WIDTH), jnp.float32), -6.0, 6.0)
    return entries.astype(jnp.bfloat16)


def place_ends(drawn, key, smallest, top_value):
    shape = drawn.shape
    index_at = [jax.random.randint(jax.random.fold_in(key, axis), (), 0, shape[axis]) for axis in range(len(shape))]
    drawn = drawn.at[tuple(index_at)].set(smallest)
    longest = shape.index(max(shape))
    index_at[longest] = (index_at[longest] + 1) % shape[longest]
    return drawn.at[tuple(index_at)].set(top_value)


def steps_of(key, shape, shards, low, top_value):
    factor_of = 1.0
    for position, shards_of in shards:
        heights = jax.random.uniform(jax.random.fold_in(jax.random.fold_in(key, 6), position), (shards_of,), jnp.float32, low / len(shards), top_value / len(shards))
        factor_of = factor_of * jnp.repeat(jnp.exp(heights), shape[position] // shards_of).reshape((-1,) + (1,) * (len(shape) - 1 - position))
    return factor_of


def profile(number_of, total, reach, lean):
    portions = [(1 << 20) // math.isqrt(grade ** lean) + 1 for grade in range(2, number_of + 1)]
    spare, counts = total - reach - (number_of - 1), [1] * (number_of - 1)
    while spare > 0:
        free = [i for i in range(number_of - 1) if counts[i] < reach]
        pool, remaining = sum([portions[i] for i in free]), spare
        for i in free:
            extra = min(reach - counts[i], max(1, remaining * portions[i] // pool), spare)
            counts[i] = counts[i] + extra
            spare = spare - extra
    return np.array([reach] + counts)


def uneven_parts(stream_key, number_of, total, limit, slope):
    if number_of == 2:
        one = jax.random.randint(stream_key, (), max(1, total - limit), min(limit, total - 1) + 1)
        return jnp.stack([one, total - one])
    sizes = jnp.asarray(profile(number_of, total, limit, slope), jnp.int32)
    twos = (number_of - 1) // 2
    donor, taker = sizes[1:1 + 2 * twos:2], sizes[2:2 + 2 * twos:2]
    room = jnp.minimum(donor - 1, limit - taker)
    shifted = jax.random.randint(jax.random.fold_in(stream_key, 1), (twos,), 0, 1 << 20) % (room + 1)
    sizes = sizes.at[1:1 + 2 * twos:2].set(donor - shifted).at[2:2 + 2 * twos:2].set(taker + shifted)
    return sizes[jax.random.permutation(jax.random.fold_in(stream_key, 2), number_of)]


def gaussian(stream_key, shape, scale, limit, cuts=(), kind=jnp.bfloat16):
    gain = steps_of(stream_key, shape, cuts, -0.22, 0.18) if cuts else 1.0
    values = jax.random.normal(stream_key, shape, jnp.float32) * scale * gain
    return jnp.minimum(jnp.maximum(values, -limit), limit).astype(kind)


def setup_inputs(seed: int = 0) -> dict:
    key_list = jax.random.split(jax.random.key(seed), 11)
    activations = draw_activations(jax.random.fold_in(key_list[10], 71), 0)
    levels = place_ends(jax.random.randint(key_list[1], (S,), 0, LEVELS), jax.random.fold_in(key_list[1], 1), 0, LEVELS - 1).astype(jnp.int32)
    ada_table = gaussian(key_list[2], (LEVELS, 2 * MODEL_WIDTH), 0.3, 1.796875)
    input_weight = gaussian(key_list[3], (MODEL_WIDTH, 4 * MODEL_WIDTH), MODEL_WIDTH ** -0.5, 0.21875)
    output_matrix = gaussian(key_list[4], (MODEL_WIDTH, MODEL_WIDTH), MODEL_WIDTH ** -0.5, 0.21875)
    pair_feats = draw_pair_feats(jax.random.fold_in(key_list[10], 71), 0)
    pair_weight = draw_pair_weight(jax.random.fold_in(key_list[10], 71), 0)
    cross_bias = jnp.clip(jax.random.uniform(key_list[7], (H,), jnp.float32, -2.0, 2.0), -2.0, 2.0)
    chains = jnp.searchsorted(jnp.cumsum(uneven_parts(key_list[8], CHAINS, N, N // 2, 1)), jnp.arange(N), side="right").astype(jnp.int32)
    cotangent = gaussian(key_list[9], (S, N, MODEL_WIDTH), 1.0, 6.0, ((0, 16), (1, 8)))
    return {"activations": activations, "levels": levels, "ada_table": ada_table, "input_weight": input_weight, "output_matrix": output_matrix, "pair_feats": pair_feats, "pair_weight": pair_weight, "cross_bias": cross_bias, "chains": chains, "cotangent": cotangent}


norm_epsilon = 1e-05

def broadcast_width(array):
    return array.astype(jnp.float32)

def half_round(array):
    return broadcast_width(lax.optimization_barrier(array.astype(jnp.bfloat16)))

def reference(activations, levels, ada_table, input_weight, output_matrix, pair_feats, pair_weight, cross_bias, chains, cotangent):
    head_size = MODEL_WIDTH // H
    factor = 1.0 / math.sqrt(head_size)
    modulation = broadcast_width(ada_table)[levels]
    ada_scale = 1.0 + modulation[:, None, :MODEL_WIDTH]
    ada_shift = modulation[:, None, MODEL_WIDTH:]
    input_broadcast = broadcast_width(activations)
    row_mean = lax.optimization_barrier(jnp.mean(input_broadcast, axis=2, keepdims=True))
    centred = input_broadcast - row_mean
    inv_std = lax.rsqrt(lax.optimization_barrier(jnp.mean(centred * centred, axis=2, keepdims=True)) + norm_epsilon)
    whitened = centred * inv_std
    layer_normalized = half_round(whitened * ada_scale + ada_shift)
    weight_broadcast = broadcast_width(input_weight)
    projected_rows = jnp.einsum('lou,uw->low', layer_normalized, weight_broadcast)
    query = half_round(projected_rows[..., :MODEL_WIDTH] * factor)
    key_part = half_round(projected_rows[..., MODEL_WIDTH:2 * MODEL_WIDTH])
    value_part = half_round(projected_rows[..., 2 * MODEL_WIDTH:3 * MODEL_WIDTH])
    gate_open = jax.nn.sigmoid(projected_rows[..., 3 * MODEL_WIDTH:])
    pair_wide = broadcast_width(pair_feats)
    pair_bias = jnp.einsum('ijc,ch->hij', pair_wide, broadcast_width(pair_weight))
    differ = broadcast_width(chains[:, None] != chains[None, :])
    fixed_bias = pair_bias + cross_bias[:, None, None] * differ[None]
    grad_gate_applied = jnp.einsum('jxt,ot->jxo', broadcast_width(cotangent), broadcast_width(output_matrix))
    grad_attend = half_round(grad_gate_applied * gate_open)

    def per_sample(bias_total, inputs):
        query_one, key_one, value_one, grad_one = inputs
        query_heads = query_one.reshape(N, H, head_size)
        key_heads = key_one.reshape(N, H, head_size)
        value_heads = value_one.reshape(N, H, head_size)
        grad_heads = grad_one.reshape(N, H, head_size)
        logits = jnp.einsum('ihd,jhd->hij', query_heads, key_heads) + fixed_bias
        row_peak = lax.optimization_barrier(jnp.max(logits, axis=2, keepdims=True))
        exp_terms = jnp.exp(logits - row_peak)
        weights_full = exp_terms / lax.optimization_barrier(jnp.sum(exp_terms, axis=2, keepdims=True))
        weights_half = half_round(weights_full)
        attended = jnp.einsum('hij,jhd->ihd', weights_half, value_heads)
        delta_sum = lax.optimization_barrier(jnp.sum(grad_heads * attended, axis=2))
        grad_weights = jnp.einsum('ihd,jhd->hij', grad_heads, value_heads)
        grad_logits = half_round(weights_full * (grad_weights - jnp.transpose(delta_sum)[:, :, None]))
        query_rows_grad = jnp.einsum('hij,jhd->ihd', grad_logits, key_heads)
        key_rows_grad = jnp.einsum('hij,ihd->jhd', grad_logits, query_heads)
        value_rows_grad = jnp.einsum('hij,ihd->jhd', weights_half, grad_heads)
        outputs = (attended.reshape(N, MODEL_WIDTH), query_rows_grad.reshape(N, MODEL_WIDTH), key_rows_grad.reshape(N, MODEL_WIDTH), value_rows_grad.reshape(N, MODEL_WIDTH))
        return (bias_total + grad_logits, outputs)
    grad_bias, results = lax.scan(per_sample, jnp.zeros((H, N, N), jnp.float32), (query, key_part, value_part, grad_attend))
    attended, query_rows_grad, key_rows_grad, value_rows_grad = results
    query_rows_grad = half_round(query_rows_grad * factor)
    gate_applied = half_round(gate_open * attended)
    updated = (input_broadcast + jnp.einsum('lou,uw->low', gate_applied, broadcast_width(output_matrix))).astype(jnp.bfloat16)
    output_weight_grad = jnp.einsum('faj,fai->ji', gate_applied, broadcast_width(cotangent))
    grad_gate_logits = half_round(grad_gate_applied * attended * gate_open * (1.0 - gate_open))
    normalized_grad = jnp.einsum('jxt,ot->jxo', query_rows_grad, weight_broadcast[:, :MODEL_WIDTH])
    normalized_grad = normalized_grad + jnp.einsum('jxt,ot->jxo', key_rows_grad, weight_broadcast[:, MODEL_WIDTH:2 * MODEL_WIDTH])
    normalized_grad = normalized_grad + jnp.einsum('jxt,ot->jxo', value_rows_grad, weight_broadcast[:, 2 * MODEL_WIDTH:3 * MODEL_WIDTH])
    normalized_grad = normalized_grad + jnp.einsum('jxt,ot->jxo', grad_gate_logits, weight_broadcast[:, 3 * MODEL_WIDTH:])
    input_weight_grad = jnp.concatenate([jnp.einsum('faj,fai->ji', layer_normalized, query_rows_grad), jnp.einsum('faj,fai->ji', layer_normalized, key_rows_grad), jnp.einsum('faj,fai->ji', layer_normalized, value_rows_grad), jnp.einsum('faj,fai->ji', layer_normalized, grad_gate_logits)], axis=1)
    grad_whitened = normalized_grad * ada_scale
    grad_scale = lax.optimization_barrier(jnp.sum(normalized_grad * whitened, axis=1))
    grad_shift = lax.optimization_barrier(jnp.sum(normalized_grad, axis=1))
    onehot = broadcast_width(levels[:, None] == jnp.arange(LEVELS, dtype=jnp.int32)[None, :])
    grad_table = jnp.dot(jnp.transpose(onehot), jnp.concatenate([grad_scale, grad_shift], axis=1), precision=lax.Precision.HIGHEST)
    grad_tokens = (broadcast_width(cotangent) + inv_std * (grad_whitened - lax.optimization_barrier(jnp.mean(grad_whitened, axis=2, keepdims=True)) - whitened * lax.optimization_barrier(jnp.mean(grad_whitened * whitened, axis=2, keepdims=True)))).astype(jnp.bfloat16)
    grad_bias_half = half_round(grad_bias)
    grad_pair = jnp.einsum('hij,ch->ijc', grad_bias_half, broadcast_width(pair_weight)).astype(jnp.bfloat16)
    grad_pair_weight = jnp.einsum('ijc,hij->ch', pair_wide, grad_bias_half)
    grad_cross = lax.optimization_barrier(jnp.sum(grad_bias * differ[None], axis=(1, 2)))
    return (updated, grad_tokens, grad_pair, input_weight_grad, output_weight_grad, grad_pair_weight, grad_cross, grad_table)
```

```python
import functools
import math

import jax
import jax.numpy as jnp
from jax import lax
from jax.experimental import pallas as pl
from jax.experimental.pallas import tpu as pltpu
from jax.sharding import Mesh, PartitionSpec as P

norm_epsilon = 1e-05
bf16 = jnp.bfloat16
f32 = jnp.float32
token_axes = ("x", "z_hi")
head_axes = ("core", "x", "z_hi")
column_axes = ("z_lo", "y")
chip_axes = ("z_lo", "y", "x", "z_hi")


def dot(a, b, dims):
    return lax.dot_general(a, b, (dims, ((), ())), preferred_element_type=f32)


def attend_kernel(
    factor,
    cross_ref,
    chain_col_ref,
    chain_row_ref,
    rows_ref,
    bias_ref,
    out_ref,
    grad_bias_ref,
    bias_full,
    logits,
    exp_half,
    grad_half,
    grad_sum,
):
    blocks, width, lanes = rows_ref.shape
    size = width // 4
    count = blocks * lanes
    chunk = 128
    step = pl.program_id(0)

    @pl.when(step == 0)
    def _():
        cross = cross_ref[0]
        part = bias_ref.shape[3]
        for p in range(count // part):
            at = pl.ds(part * p, part)
            block = jnp.concatenate(
                [bias_ref[p // 2, p % 2, t] for t in range(blocks)], axis=1
            )
            differ = chain_col_ref[at, 0:1] != chain_row_ref[0:1, :]
            bias_full[at, :] = block + jnp.where(differ, cross, 0.0)
            grad_sum[at, :] = jnp.zeros((part, count), f32)

    def take(index):
        return jnp.concatenate(
            [rows_ref[t, index * size : (index + 1) * size, :] for t in range(blocks)], axis=1
        )

    query_t, key_t, value_t, grad_t = take(0), take(1), take(2), take(3)
    key = key_t.T
    value = value_t.T
    peak = jnp.full((1, count), -jnp.inf, f32)
    for p in range(count // chunk):
        at = pl.ds(chunk * p, chunk)
        part = dot(key[chunk * p : chunk * (p + 1)], query_t, ((1,), (0,))) + bias_full[at, :]
        logits[at, :] = part
        peak = jnp.maximum(peak, jnp.max(part, axis=0, keepdims=True))
    for p in range(count // chunk):
        at = pl.ds(chunk * p, chunk)
        exp_half[at, :] = jnp.exp(logits[at, :] - peak).astype(bf16)
    value_ones = jnp.concatenate([value_t, jnp.ones((16, count), bf16)], axis=0)
    summed = dot(value_ones, exp_half[...], ((1,), (0,)))
    inverse = 1.0 / summed[size : size + 1]
    attended_t = summed[:size] * inverse
    scaled_t = (grad_t.astype(f32) * inverse).astype(bf16)
    delta = jnp.sum(scaled_t.astype(f32) * attended_t, axis=0, keepdims=True)
    key_grad = []
    value_grad = []
    for p in range(count // chunk):
        at = pl.ds(chunk * p, chunk)
        weights = dot(value[chunk * p : chunk * (p + 1)], scaled_t, ((1,), (0,)))
        terms = exp_half[at, :]
        grad = terms.astype(f32) * (weights - delta)
        half = grad.astype(bf16)
        grad_half[at, :] = half
        grad_sum[at, :] += grad
        key_grad.append(dot(half, query_t, ((1,), (1,))))
        value_grad.append(dot(terms, scaled_t, ((1,), (1,))))
    query_grad_t = dot(key_t, grad_half[...], ((1,), (0,))) * factor
    key_grad_t = jnp.concatenate(key_grad, axis=0).T
    value_grad_t = jnp.concatenate(value_grad, axis=0).T
    for index, array in enumerate((attended_t, query_grad_t, key_grad_t, value_grad_t)):
        array = array.astype(bf16)
        for t in range(blocks):
            out_ref[t, index * size : (index + 1) * size, :] = array[:, t * lanes : (t + 1) * lanes]

    @pl.when(step == pl.num_programs(0) - 1)
    def _():
        part = grad_bias_ref.shape[3]
        for p in range(count // part):
            for t in range(blocks):
                grad_bias_ref[p // 2, p % 2, t] = grad_sum[
                    pl.ds(part * p, part), t * lanes : (t + 1) * lanes
                ].astype(bf16)


def attend(rows, bias, cross, chains, factor):
    blocks, width, total = rows.shape
    lanes = 128
    samples = total // lanes
    count = blocks * lanes
    chain_col = jnp.broadcast_to(chains[:, None], (count, 128))
    chain_row = jnp.broadcast_to(chains[None, :], (8, count))
    whole = lambda shape: pl.BlockSpec(shape, lambda s: (0,) * len(shape))
    return pl.pallas_call(
        functools.partial(attend_kernel, factor),
        grid=(samples,),
        in_specs=[
            pl.BlockSpec(memory_space=pltpu.SMEM),
            whole(chain_col.shape),
            whole(chain_row.shape),
            pl.BlockSpec((blocks, width, lanes), lambda s: (0, 0, s)),
            whole(bias.shape),
        ],
        out_specs=[
            pl.BlockSpec((blocks, width, lanes), lambda s: (0, 0, s)),
            whole(bias.shape),
        ],
        out_shape=[
            jax.ShapeDtypeStruct(rows.shape, bf16),
            jax.ShapeDtypeStruct(bias.shape, bf16),
        ],
        scratch_shapes=[
            pltpu.VMEM((count, count), f32),
            pltpu.VMEM((count, count), f32),
            pltpu.VMEM((count, count), bf16),
            pltpu.VMEM((count, count), bf16),
            pltpu.VMEM((count, count), f32),
        ],
        compiler_params=pltpu.CompilerParams(vmem_limit_bytes=52 * 1024 * 1024),
        cost_estimate=pl.CostEstimate(
            flops=12 * samples * count * count * 48,
            bytes_accessed=16 * 1024 * 1024,
            transcendentals=samples * count * count,
        ),
    )(cross, chain_col, chain_row, rows, bias)


def swap(array):
    return lax.ppermute(array, "core", [(0, 1), (1, 0)])


def exchange(array, axes):
    return lax.all_to_all(array, axes, 0, 0, tiled=True)


def spread(array, axes, count):
    return exchange(jnp.broadcast_to(array[None], (count,) + array.shape), axes)


def shards(
    activations,
    levels,
    ada_table,
    input_weight,
    output_matrix,
    pair_feats,
    pair_weight,
    cross_bias,
    chains,
    cotangent,
):
    own_samples, row_count, width = activations.shape
    heads = pair_weight.shape[1]
    size = width // heads
    col_count = pair_feats.shape[1]
    level_count = ada_table.shape[0]
    factor = 1.0 / math.sqrt(size)
    core = lax.axis_index("core")
    blocks = lax.axis_size("x") * lax.axis_size("z_hi")
    zy_count = lax.axis_size("z_lo") * lax.axis_size("y")
    chip_count = blocks * zy_count
    token = lax.axis_index(token_axes)
    zy = lax.axis_index(column_axes)
    half = width // 2

    pair_part = jnp.einsum("ijc,ch->hji", pair_feats, pair_weight, preferred_element_type=f32)
    bias_own = exchange(pair_part.astype(jnp.float16), head_axes)
    bias = spread(bias_own, column_axes, zy_count).astype(f32)
    bias = bias.reshape(zy_count, 2, blocks, col_count, row_count)

    rows = own_samples * 2 * row_count
    acts = jnp.concatenate([activations, swap(activations)], axis=0)
    cots = jnp.concatenate([cotangent, swap(cotangent)], axis=0).reshape(rows, width)
    chip_levels = jnp.concatenate([levels, swap(levels)], axis=0)
    onehot = (
        chip_levels[:, None]
        == lax.broadcasted_iota(jnp.int32, (2 * own_samples, level_count), 1)
    ).astype(bf16)
    modulation = jnp.dot(onehot, ada_table, preferred_element_type=f32)
    ada_scale = 1.0 + modulation[:, None, :width]
    ada_shift = modulation[:, None, width:]
    wide = acts.astype(f32)
    row_mean = jnp.mean(wide, axis=2, keepdims=True)
    centred = wide - row_mean
    inv_std = lax.rsqrt(jnp.mean(centred * centred, axis=2, keepdims=True) + norm_epsilon)
    normed = (centred * inv_std * ada_scale + ada_shift).astype(bf16).reshape(rows, width)

    weight = lax.dynamic_slice_in_dim(
        input_weight.reshape(width, 4, 2, half), core, 1, axis=2
    ).reshape(width, 4 * half)
    out_weight = lax.dynamic_slice_in_dim(output_matrix, core * half, half, axis=0)
    projected = dot(weight, normed, ((0,), (1,)))
    query = (projected[:half] * factor).astype(bf16)
    key = projected[half : 2 * half].astype(bf16)
    value = projected[2 * half : 3 * half].astype(bf16)
    gate_open = jax.nn.sigmoid(projected[3 * half :])
    grad_gated = dot(out_weight, cots, ((1,), (1,)))
    grad_attend = (grad_gated * gate_open).astype(bf16)
    by_head = lambda a: a.reshape(blocks, size, rows)
    sent = jnp.concatenate([by_head(a) for a in (query, key, value, grad_attend)], axis=1)
    head_rows = exchange(sent, token_axes)
    own_cross = lax.dynamic_slice_in_dim(cross_bias, core * blocks + token, 1)

    head_grads, grad_bias = attend(head_rows, bias, own_cross, chains, factor)

    back = exchange(head_grads, token_axes).reshape(blocks, 4, size, rows)
    attended = back[:, 0].reshape(half, rows).astype(f32)
    gated = (gate_open * attended).astype(bf16)
    grad_gate = (grad_gated * attended * gate_open * (1.0 - gate_open)).astype(bf16)
    grads = jnp.concatenate(
        [back[:, index].reshape(half, rows) for index in (1, 2, 3)] + [grad_gate], axis=0
    )
    normed_part = dot(grads, weight, ((0,), (1,)))
    updated_part = dot(gated, out_weight, ((0,), (0,)))
    own = rows // 2
    grad_normed = normed_part[:own] + swap(normed_part[own:].astype(bf16)).astype(f32)
    output = updated_part[:own] + swap(updated_part[own:].astype(bf16)).astype(f32)
    own_shape = (own_samples, row_count, width)
    grad_normed = grad_normed.reshape(own_shape)
    updated = (activations.astype(f32) + output.reshape(own_shape)).astype(bf16)

    whitened = centred[:own_samples] * inv_std[:own_samples]
    grad_whitened = grad_normed * ada_scale[:own_samples]
    grad_scale = jnp.sum(grad_normed * whitened, axis=1)
    grad_shift = jnp.sum(grad_normed, axis=1)
    grad_tokens = (
        cotangent.astype(f32)
        + inv_std[:own_samples]
        * (
            grad_whitened
            - jnp.mean(grad_whitened, axis=2, keepdims=True)
            - whitened * jnp.mean(grad_whitened * whitened, axis=2, keepdims=True)
        )
    ).astype(bf16)

    bias_parts = exchange(grad_bias, column_axes)
    bias_sum = jnp.sum(bias_parts.astype(f32), axis=0).astype(bf16)
    grad_bias_half = exchange(bias_sum.reshape(heads, col_count, row_count), head_axes)
    grad_pair = jnp.einsum(
        "hji,ch->ijc", grad_bias_half, pair_weight, preferred_element_type=f32
    ).astype(bf16)
    grad_pair_part = jnp.einsum(
        "ijc,hji->ch", pair_feats, grad_bias_half, preferred_element_type=f32
    )
    col_at = (zy * 2 + core) * col_count
    col_chain = lax.dynamic_slice_in_dim(chains, col_at, col_count)
    row_chain = lax.dynamic_slice_in_dim(chains, token * row_count, row_count)
    differ = col_chain[:, None] != row_chain[None, :]
    grad_cross_part = jnp.sum(
        jnp.where(differ[None], grad_bias_half.astype(f32), 0.0), axis=(1, 2)
    )

    line = 2 * width
    weight_part = dot(normed, grads, ((0,), (1,))).astype(bf16)
    out_part = dot(gated, cots, ((1,), (0,))).astype(bf16)
    at_own = (jnp.arange(zy_count) == zy).astype(f32)[:, None]
    at_first = (jnp.arange(zy_count) == 0).astype(f32)[:, None]
    table_rows = jnp.concatenate([grad_scale, grad_shift], axis=1)
    level_row = jnp.pad(
        levels.astype(f32) * (token == 0).astype(f32), (0, line - own_samples)
    )
    pair_rows = jnp.pad(
        jnp.concatenate([grad_pair_part.reshape(-1), grad_cross_part]),
        (0, 2 * line - grad_pair_part.size - heads),
    ).reshape(2, line)
    small = jnp.stack(
        [
            at_own * table_rows[0],
            at_own * table_rows[1],
            at_first * pair_rows[0],
            at_first * pair_rows[1],
            at_own * level_row,
        ]
        + [jnp.zeros((zy_count, line), f32)] * (blocks - 5),
        axis=1,
    ).reshape(chip_count, 1, line)
    payload = jnp.concatenate(
        [
            weight_part.reshape(chip_count, -1, line),
            out_part.reshape(chip_count, -1, line),
            small.astype(bf16),
        ],
        axis=1,
    )
    parts = exchange(payload, chip_axes)
    summed = jnp.sum(parts.astype(f32), axis=0).astype(bf16)
    gathered = spread(summed, chip_axes, chip_count)
    other = swap(gathered)
    pair_of = jnp.where(core == 0, jnp.stack([gathered, other]), jnp.stack([other, gathered]))
    depth = width // chip_count
    input_weight_grad = (
        pair_of[:, :, :depth]
        .reshape(2, width, 4, half)
        .transpose(1, 2, 0, 3)
        .reshape(width, 4 * width)
        .astype(f32)
    )
    output_weight_grad = pair_of[:, :, depth : depth + depth // 4].reshape(width, width).astype(f32)
    small_all = pair_of[:, :, -1].reshape(2, zy_count, blocks, line).astype(f32)
    table_all = small_all[:, :, :2].transpose(1, 0, 2, 3).reshape(-1, line)
    level_all = small_all[:, :, 4, :own_samples].transpose(1, 0, 2).reshape(-1)
    onehot_all = (
        level_all[None, :] == jnp.arange(level_count, dtype=f32)[:, None]
    ).astype(f32)
    grad_table = jnp.dot(onehot_all, table_all, precision=lax.Precision.HIGHEST)
    pair_flat = jnp.sum(small_all[:, 0, 2:4], axis=0).reshape(-1)
    pair_size = pair_weight.shape[0] * heads
    grad_pair_weight = pair_flat[:pair_size].reshape(pair_weight.shape)
    grad_cross = pair_flat[pair_size : pair_size + heads]
    return (
        updated,
        grad_tokens,
        grad_pair,
        input_weight_grad,
        output_weight_grad,
        grad_pair_weight,
        grad_cross,
        grad_table,
    )


def solution(mesh):
    fine = Mesh(mesh.devices.reshape(2, 4, 2, 4, 2), ("z_lo", "y", "core", "x", "z_hi"))
    sample = ("z_lo", "y", "core")
    token = ("x", "z_hi")
    placed = (
        P(sample, token, None),
        P(sample),
        P(),
        P(),
        P(),
        P(token, sample, None),
        P(),
        P(),
        P(),
        P(sample, token, None),
    )
    return jax.shard_map(
        shards,
        mesh=fine,
        in_specs=placed,
        out_specs=(
            P(sample, token, None),
            P(sample, token, None),
            P(token, sample, None),
            P(),
            P(),
            P(),
            P(),
            P(),
        ),
        check_vma=False,
    )
```

```python
import functools
import math

import jax
import jax.numpy as jnp
from jax import lax
from jax.experimental import pallas as pl
from jax.experimental.pallas import tpu as pltpu
from jax.sharding import Mesh, PartitionSpec as P

norm_epsilon = 1e-05
bf16 = jnp.bfloat16
f32 = jnp.float32
token_axes = ("x", "z_hi")
head_axes = ("core", "x", "z_hi")
column_axes = ("z_lo", "y")
chip_axes = ("z_lo", "y", "x", "z_hi")


def dot(a, b, dims):
    return lax.dot_general(a, b, (dims, ((), ())), preferred_element_type=f32)


def attend_kernel(
    factor,
    cross_ref,
    chain_col_ref,
    chain_row_ref,
    rows_ref,
    bias_ref,
    out_ref,
    grad_bias_ref,
    cross_sum_ref,
    bias_full,
    logits,
    exp_half,
    grad_half,
    grad_sum,
):
    blocks, width, lanes = rows_ref.shape
    size = width // 4
    count = blocks * lanes
    chunk = 128
    step = pl.program_id(0)

    @pl.when(step == 0)
    def _():
        cross = cross_ref[0]
        part = bias_ref.shape[3]
        for p in range(count // part):
            at = pl.ds(part * p, part)
            block = jnp.concatenate(
                [bias_ref[p // 2, p % 2, t] for t in range(blocks)], axis=1
            )
            differ = chain_col_ref[at, 0:1] != chain_row_ref[0:1, :]
            bias_full[at, :] = block + jnp.where(differ, cross, 0.0)
            grad_sum[at, :] = jnp.zeros((part, count), f32)

    def take(index):
        return jnp.concatenate(
            [rows_ref[t, index * size : (index + 1) * size, :] for t in range(blocks)], axis=1
        )

    query_t, key_t, value_t, grad_t = take(0), take(1), take(2), take(3)
    key = key_t.T
    value = value_t.T
    peak = jnp.full((1, count), -jnp.inf, f32)
    for p in range(count // chunk):
        at = pl.ds(chunk * p, chunk)
        part = dot(key[chunk * p : chunk * (p + 1)], query_t, ((1,), (0,))) + bias_full[at, :]
        logits[at, :] = part
        peak = jnp.maximum(peak, jnp.max(part, axis=0, keepdims=True))
    for p in range(count // chunk):
        at = pl.ds(chunk * p, chunk)
        exp_half[at, :] = jnp.exp(logits[at, :] - peak).astype(bf16)
    value_ones = jnp.concatenate([value_t, jnp.ones((16, count), bf16)], axis=0)
    summed = dot(value_ones, exp_half[...], ((1,), (0,)))
    inverse = 1.0 / summed[size : size + 1]
    attended_t = summed[:size] * inverse
    scaled_t = (grad_t.astype(f32) * inverse).astype(bf16)
    delta = jnp.sum(scaled_t.astype(f32) * attended_t, axis=0, keepdims=True)
    key_grad = []
    value_grad = []
    for p in range(count // chunk):
        at = pl.ds(chunk * p, chunk)
        weights = dot(value[chunk * p : chunk * (p + 1)], scaled_t, ((1,), (0,)))
        terms = exp_half[at, :]
        grad = terms.astype(f32) * (weights - delta)
        half = grad.astype(bf16)
        grad_half[at, :] = half
        grad_sum[at, :] += grad
        key_grad.append(dot(half, query_t, ((1,), (1,))))
        value_grad.append(dot(terms, scaled_t, ((1,), (1,))))
    query_grad_t = dot(key_t, grad_half[...], ((1,), (0,))) * factor
    key_grad_t = jnp.concatenate(key_grad, axis=0).T
    value_grad_t = jnp.concatenate(value_grad, axis=0).T
    for index, array in enumerate((attended_t, query_grad_t, key_grad_t, value_grad_t)):
        array = array.astype(bf16)
        for t in range(blocks):
            out_ref[t, index * size : (index + 1) * size, :] = array[:, t * lanes : (t + 1) * lanes]

    @pl.when(step == pl.num_programs(0) - 1)
    def _():
        part = grad_bias_ref.shape[3]
        cross_sum = jnp.zeros((1, count), f32)
        for p in range(count // part):
            at = pl.ds(part * p, part)
            block = grad_sum[at, :]
            differ = chain_col_ref[at, 0:1] != chain_row_ref[0:1, :]
            cross_sum += jnp.sum(jnp.where(differ, block, 0.0), axis=0, keepdims=True)
            half = block.astype(bf16)
            for t in range(blocks):
                grad_bias_ref[p // 2, p % 2, t] = half[:, t * lanes : (t + 1) * lanes]
        cross_sum_ref[...] = jnp.broadcast_to(cross_sum, cross_sum_ref.shape)


def attend(rows, bias, cross, chains, factor):
    blocks, width, total = rows.shape
    lanes = 128
    samples = total // lanes
    count = blocks * lanes
    chain_col = jnp.broadcast_to(chains[:, None], (count, 128))
    chain_row = jnp.broadcast_to(chains[None, :], (8, count))
    whole = lambda shape: pl.BlockSpec(shape, lambda s: (0,) * len(shape))
    return pl.pallas_call(
        functools.partial(attend_kernel, factor),
        grid=(samples,),
        in_specs=[
            pl.BlockSpec(memory_space=pltpu.SMEM),
            whole(chain_col.shape),
            whole(chain_row.shape),
            pl.BlockSpec((blocks, width, lanes), lambda s: (0, 0, s)),
            whole(bias.shape),
        ],
        out_specs=[
            pl.BlockSpec((blocks, width, lanes), lambda s: (0, 0, s)),
            whole(bias.shape),
            whole((8, count)),
        ],
        out_shape=[
            jax.ShapeDtypeStruct(rows.shape, bf16),
            jax.ShapeDtypeStruct(bias.shape, bf16),
            jax.ShapeDtypeStruct((8, count), f32),
        ],
        scratch_shapes=[
            pltpu.VMEM((count, count), f32),
            pltpu.VMEM((count, count), f32),
            pltpu.VMEM((count, count), bf16),
            pltpu.VMEM((count, count), bf16),
            pltpu.VMEM((count, count), f32),
        ],
        compiler_params=pltpu.CompilerParams(vmem_limit_bytes=52 * 1024 * 1024),
        cost_estimate=pl.CostEstimate(
            flops=12 * samples * count * count * 48,
            bytes_accessed=16 * 1024 * 1024,
            transcendentals=samples * count * count,
        ),
    )(cross, chain_col, chain_row, rows, bias)


def before_kernel(factor, core_ref, acts_ref, cots_ref, mod_ref, *refs):
    weight_refs = refs[:4]
    out_weight_ref, sent_ref, gate_ref, grad_gated_ref, normed_ref = refs[4:]
    rows, width = acts_ref.shape
    heads, _, _ = sent_ref.shape
    size = sent_ref.shape[1] // 4
    samples = mod_ref.shape[0]
    part = rows // samples
    for s in range(samples):
        at = slice(s * part, (s + 1) * part)
        wide = acts_ref[at, :].astype(f32)
        centred = wide - jnp.mean(wide, axis=1, keepdims=True)
        inv_std = lax.rsqrt(jnp.mean(centred * centred, axis=1, keepdims=True) + norm_epsilon)
        scale = 1.0 + mod_ref[s : s + 1, :width]
        shift = mod_ref[s : s + 1, width:]
        normed_ref[at, :] = (centred * inv_std * scale + shift).astype(bf16)
    normed = normed_ref[...]

    def put(index, array):
        for h in range(heads):
            sent_ref[h, index * size : (index + 1) * size, :] = array[h * size : (h + 1) * size]

    for index in range(3):
        projected = dot(normed, weight_refs[index][...], ((1,), (0,)))
        if index == 0:
            projected = projected * factor
        put(index, projected.T.astype(bf16))
    gate = jax.nn.sigmoid(dot(normed, weight_refs[3][...], ((1,), (0,)))).T
    gate_ref[...] = gate
    grad_gated = dot(cots_ref[...], out_weight_ref[...], ((1,), (1,))).T
    grad_gated_ref[...] = grad_gated
    put(3, (grad_gated * gate).astype(bf16))


def weight_specs(width, half):
    specs = [
        pl.BlockSpec((width, half), functools.partial(lambda b, i, c: (0, 2 * b + c[0]), b))
        for b in range(4)
    ]
    return specs + [pl.BlockSpec((half, width), lambda i, c: (c[0], 0))]


def spec_of(shape):
    return pl.BlockSpec(shape, lambda i, c: (0,) * len(shape))


def before(core, acts, cots, modulation, input_weight, output_matrix, heads, factor):
    rows, width = acts.shape
    half = width // 2
    size = half // heads
    shapes = [
        ((heads, 4 * size, rows), bf16),
        ((half, rows), f32),
        ((half, rows), f32),
        ((rows, width), bf16),
    ]
    return pl.pallas_call(
        functools.partial(before_kernel, factor),
        grid_spec=pltpu.PrefetchScalarGridSpec(
            num_scalar_prefetch=1,
            grid=(1,),
            in_specs=[spec_of(acts.shape), spec_of(cots.shape), spec_of(modulation.shape)]
            + weight_specs(width, half),
            out_specs=[spec_of(shape) for shape, _ in shapes],
        ),
        out_shape=[jax.ShapeDtypeStruct(shape, kind) for shape, kind in shapes],
        compiler_params=pltpu.CompilerParams(vmem_limit_bytes=48 * 1024 * 1024),
        cost_estimate=pl.CostEstimate(
            flops=2 * rows * width * 5 * half,
            bytes_accessed=8 * 1024 * 1024,
            transcendentals=rows * half,
        ),
    )(core, acts, cots, modulation, *([input_weight] * 4), output_matrix)


def after_kernel(core_ref, back_ref, gate_ref, grad_gated_ref, normed_ref, cots_ref, *refs):
    weight_refs = refs[:4]
    out_weight_ref, own_normed_ref, other_normed_ref, own_out_ref, other_out_ref = refs[4:9]
    payload_ref = refs[9]
    heads = back_ref.shape[0]
    size = back_ref.shape[1] // 4
    own = own_normed_ref.shape[0]
    width = own_normed_ref.shape[1]
    half = heads * size

    def take(index):
        return jnp.concatenate(
            [back_ref[h, index * size : (index + 1) * size, :] for h in range(heads)], axis=0
        )

    attended = take(0).astype(f32)
    gate = gate_ref[...]
    gated_wide = gate * attended
    gated = gated_wide.astype(bf16)
    grad_gate = (grad_gated_ref[...] * gated_wide * (1.0 - gate)).astype(bf16)
    normed_t = normed_ref[...].T
    total = None
    depth = 48
    for index, grad_t in enumerate((take(1), take(2), take(3), grad_gate)):
        grad = grad_t.T
        part = dot(grad, weight_refs[index][...], ((1,), (1,)))
        total = part if total is None else total + part
        weight_grad = dot(normed_t, grad, ((1,), (0,))).astype(bf16)
        for a in range(width // depth):
            payload_ref[4 * a + index, :depth, :] = weight_grad[depth * a : depth * (a + 1)]
    own_normed_ref[...] = total[:own]
    other_normed_ref[...] = total[own:].astype(bf16)
    output = dot(gated.T, out_weight_ref[...], ((1,), (0,)))
    own_out_ref[...] = output[:own]
    other_out_ref[...] = output[own:].astype(bf16)
    out_grad = dot(gated, cots_ref[...], ((1,), (0,))).astype(bf16)
    for d in range(payload_ref.shape[0]):
        if d < half // 8:
            block = out_grad[16 * (d // 2) : 16 * (d // 2 + 1), half * (d % 2) : half * (d % 2 + 1)]
        else:
            block = jnp.zeros((16, half), bf16)
        payload_ref[d, depth:, :] = block


def after(core, back, gate, grad_gated, normed, cots, input_weight, output_matrix):
    rows, width = normed.shape
    half = width // 2
    own = rows // 2
    shapes = [
        ((own, width), f32),
        ((own, width), bf16),
        ((own, width), f32),
        ((own, width), bf16),
        ((64, 64, half), bf16),
    ]
    operands = (back, gate, grad_gated, normed, cots)
    return pl.pallas_call(
        after_kernel,
        grid_spec=pltpu.PrefetchScalarGridSpec(
            num_scalar_prefetch=1,
            grid=(1,),
            in_specs=[spec_of(a.shape) for a in operands] + weight_specs(width, half),
            out_specs=[spec_of(shape) for shape, _ in shapes],
        ),
        out_shape=[jax.ShapeDtypeStruct(shape, kind) for shape, kind in shapes],
        compiler_params=pltpu.CompilerParams(vmem_limit_bytes=48 * 1024 * 1024),
        cost_estimate=pl.CostEstimate(
            flops=4 * rows * width * 5 * half,
            bytes_accessed=12 * 1024 * 1024,
            transcendentals=0,
        ),
    )(core, *operands, *([input_weight] * 4), output_matrix)


def assemble_kernel(core_ref, mine_ref, other_ref, input_ref, output_ref):
    step = pl.program_id(0)
    half = mine_ref.shape[2]
    depth = input_ref.shape[0]

    def write(position, ref):
        for b in range(4):
            at = (2 * b + position) * half
            input_ref[:, at : at + half] = ref[b, :depth, :].astype(f32)

        @pl.when(step < 12)
        def _():
            for b in range(4):
                output_ref[
                    position, 16 * (b // 2) : 16 * (b // 2 + 1), half * (b % 2) : half * (b % 2 + 1)
                ] = ref[b, depth : depth + 16, :].astype(f32)

    @pl.when(core_ref[0] == 0)
    def _():
        write(0, mine_ref)
        write(1, other_ref)

    @pl.when(core_ref[0] == 1)
    def _():
        write(1, mine_ref)
        write(0, other_ref)


def assemble(core, mine, other):
    chips, depth, half = mine.shape
    width = 2 * half
    block = pl.BlockSpec((4, depth, half), lambda a, c: (a, 0, 0))
    return pl.pallas_call(
        assemble_kernel,
        grid_spec=pltpu.PrefetchScalarGridSpec(
            num_scalar_prefetch=1,
            grid=(16,),
            in_specs=[block, block],
            out_specs=[
                pl.BlockSpec((width // 16, 4 * width), lambda a, c: (a, 0)),
                pl.BlockSpec((2, 32, width), lambda a, c: (0, jnp.minimum(a, 11), 0)),
            ],
        ),
        out_shape=[
            jax.ShapeDtypeStruct((width, 4 * width), f32),
            jax.ShapeDtypeStruct((2, half, width), f32),
        ],
        compiler_params=pltpu.CompilerParams(vmem_limit_bytes=32 * 1024 * 1024),
        cost_estimate=pl.CostEstimate(
            flops=0, bytes_accessed=20 * 1024 * 1024, transcendentals=0
        ),
    )(core, mine, other)


def swap(array):
    return lax.ppermute(array, "core", [(0, 1), (1, 0)])


def exchange(array, axes):
    return lax.all_to_all(array, axes, 0, 0, tiled=True)


def spread(array, axes, count):
    return exchange(jnp.broadcast_to(array[None], (count,) + array.shape), axes)


def shards(
    activations,
    levels,
    ada_table,
    input_weight,
    output_matrix,
    pair_feats,
    pair_weight,
    cross_bias,
    chains,
    cotangent,
):
    own_samples, row_count, width = activations.shape
    heads = pair_weight.shape[1]
    size = width // heads
    col_count = pair_feats.shape[1]
    level_count = ada_table.shape[0]
    factor = 1.0 / math.sqrt(size)
    core = lax.axis_index("core")
    blocks = lax.axis_size("x") * lax.axis_size("z_hi")
    zy_count = lax.axis_size("z_lo") * lax.axis_size("y")
    chip_count = blocks * zy_count
    token = lax.axis_index(token_axes)
    half = width // 2

    pair_part = jnp.einsum("ijc,ch->hji", pair_feats, pair_weight, preferred_element_type=f32)
    bias_own = exchange(pair_part.astype(jnp.float16), head_axes)
    bias = spread(bias_own, column_axes, zy_count).astype(f32)
    bias = bias.reshape(zy_count, 2, blocks, col_count, row_count)

    rows = own_samples * 2 * row_count
    core_at = jnp.reshape(core, (1,)).astype(jnp.int32)
    acts = jnp.concatenate([activations, swap(activations)], axis=0).reshape(rows, width)
    cots = jnp.concatenate([cotangent, swap(cotangent)], axis=0).reshape(rows, width)
    chip_levels = jnp.concatenate([levels, swap(levels)], axis=0)
    onehot = (
        chip_levels[:, None]
        == lax.broadcasted_iota(jnp.int32, (2 * own_samples, level_count), 1)
    ).astype(bf16)
    modulation = jnp.dot(onehot, ada_table, preferred_element_type=f32)
    sent, gate_open, grad_gated, normed = before(
        core_at, acts, cots, modulation, input_weight, output_matrix, blocks, factor
    )
    head_rows = exchange(sent, token_axes)
    own_cross = lax.dynamic_slice_in_dim(cross_bias, core * blocks + token, 1)
    head_grads, grad_bias, cross_sum = attend(head_rows, bias, own_cross, chains, factor)

    back = exchange(head_grads, token_axes)
    own_normed, other_normed, own_output, other_output, payload = after(
        core_at, back, gate_open, grad_gated, normed, cots, input_weight, output_matrix
    )
    own_shape = (own_samples, row_count, width)
    grad_normed = (own_normed + swap(other_normed).astype(f32)).reshape(own_shape)
    output = (own_output + swap(other_output).astype(f32)).reshape(own_shape)
    wide = activations.astype(f32)
    updated = (wide + output).astype(bf16)
    centred = wide - jnp.mean(wide, axis=2, keepdims=True)
    inv_std = lax.rsqrt(jnp.mean(centred * centred, axis=2, keepdims=True) + norm_epsilon)
    whitened = centred * inv_std
    grad_whitened = grad_normed * (1.0 + modulation[:own_samples, None, :width])
    grad_scale = jnp.sum(grad_normed * whitened, axis=1)
    grad_shift = jnp.sum(grad_normed, axis=1)
    grad_tokens = (
        cotangent.astype(f32)
        + inv_std
        * (
            grad_whitened
            - jnp.mean(grad_whitened, axis=2, keepdims=True)
            - whitened * jnp.mean(grad_whitened * whitened, axis=2, keepdims=True)
        )
    ).astype(bf16)

    bias_parts = exchange(grad_bias, column_axes)
    bias_sum = jnp.sum(bias_parts.astype(f32), axis=0).astype(bf16)
    grad_bias_half = exchange(bias_sum.reshape(heads, col_count, row_count), head_axes)
    grad_pair = jnp.einsum(
        "hji,ch->ijc", grad_bias_half, pair_weight, preferred_element_type=f32
    ).astype(bf16)
    grad_pair_part = jnp.einsum(
        "ijc,hji->ch", pair_feats, grad_bias_half, preferred_element_type=f32
    )

    parts = exchange(payload, chip_axes)
    summed = jnp.sum(parts.astype(f32), axis=0).astype(bf16)
    pair_size = pair_weight.shape[0] * heads
    cross_part = jnp.sum(cross_sum[0])
    cross_high = cross_part.astype(bf16).astype(f32)
    last = jnp.concatenate(
        [jnp.stack([cross_high, cross_part - cross_high]), levels.astype(f32)]
    )
    flat = jnp.concatenate([grad_scale, grad_shift], axis=1).reshape(-1)
    flat = jnp.concatenate([flat, grad_pair_part.reshape(-1), last])
    small_depth = 16
    small = jnp.pad(flat, (0, small_depth * half - flat.size)).reshape(small_depth, half)
    block = jnp.concatenate([summed, small.astype(bf16)], axis=0)
    gathered = spread(block, chip_axes, chip_count)
    other = swap(gathered)
    input_weight_grad, output_weight_grad = assemble(core_at, gathered, other)
    output_weight_grad = output_weight_grad.reshape(width, width)
    mine_small = gathered[:, -small_depth:].reshape(zy_count, blocks, small_depth * half)
    other_small = other[:, -small_depth:].reshape(zy_count, blocks, small_depth * half)
    small_all = jnp.where(
        core == 0, jnp.stack([mine_small, other_small]), jnp.stack([other_small, mine_small])
    ).astype(f32)
    line = 2 * width
    table_all = jnp.sum(small_all[..., : own_samples * line], axis=2)
    table_all = table_all.reshape(2, zy_count, own_samples, line)
    table_all = table_all.transpose(1, 0, 2, 3).reshape(-1, line)
    at = own_samples * line
    grad_pair_weight = jnp.sum(small_all[..., at : at + pair_size], axis=(0, 1, 2)).reshape(
        pair_weight.shape
    )
    at = at + pair_size
    grad_cross = jnp.sum(small_all[..., at : at + 2], axis=(1, 3)).reshape(-1)
    level_all = small_all[:, :, 0, at + 2 : at + 2 + own_samples].transpose(1, 0, 2).reshape(-1)
    onehot_all = (
        level_all[None, :] == jnp.arange(level_count, dtype=f32)[:, None]
    ).astype(f32)
    grad_table = jnp.dot(onehot_all, table_all, precision=lax.Precision.HIGHEST)
    return (
        updated,
        grad_tokens,
        grad_pair,
        input_weight_grad,
        output_weight_grad,
        grad_pair_weight,
        grad_cross,
        grad_table,
    )


def solution(mesh):
    fine = Mesh(mesh.devices.reshape(2, 4, 2, 4, 2), ("z_lo", "y", "core", "x", "z_hi"))
    sample = ("z_lo", "y", "core")
    token = ("x", "z_hi")
    placed = (
        P(sample, token, None),
        P(sample),
        P(),
        P(),
        P(),
        P(token, sample, None),
        P(),
        P(),
        P(),
        P(sample, token, None),
    )
    return jax.shard_map(
        shards,
        mesh=fine,
        in_specs=placed,
        out_specs=(
            P(sample, token, None),
            P(sample, token, None),
            P(token, sample, None),
            P(),
            P(),
            P(),
            P(),
            P(),
        ),
        check_vma=False,
    )
```

```python
import functools
import math

import jax
import jax.numpy as jnp
from jax import lax
from jax.experimental import pallas as pl
from jax.experimental.pallas import tpu as pltpu
from jax.sharding import Mesh, PartitionSpec as P

norm_epsilon = 1e-05
bf16 = jnp.bfloat16
f32 = jnp.float32
token_axes = ("x", "z_hi")
head_axes = ("core", "x", "z_hi")
column_axes = ("z_lo", "y")
chip_axes = ("z_lo", "y", "x", "z_hi")


def dot(a, b, dims):
    return lax.dot_general(a, b, (dims, ((), ())), preferred_element_type=f32)


def bias_block(refs, place, part):
    dz, dy = place // 4, place % 4
    if dy == 2:
        return refs[5 * dz + 3 + part], 0
    return refs[5 * dz + (0, 1, None, 2)[dy]], part


def attend_kernel(factor, base_ref, cross_ref, chain_col_ref, chain_row_ref, rows_ref, *refs):
    bias_refs, out_ref, grad_bias_refs = refs[:10], refs[10], refs[11:19]
    cross_sum_ref, bias_full, logits, exp_half, grad_half, grad_sum = refs[19:]
    blocks, width, lanes = rows_ref.shape
    size = width // 4
    count = blocks * lanes
    chunk = 128
    step = pl.program_id(0)

    @pl.when(step == 0)
    def _():
        cross = cross_ref[0]
        part = (bias_refs[0].shape[1] - 16) // blocks
        for p in range(count // part):
            at = pl.ds(pl.multiple_of(base_ref[p // 2] * (2 * part), 2 * part) + part * (p % 2), part)
            ref, first = bias_block(bias_refs, p // 2, p % 2)
            moved = jnp.concatenate(
                [ref[first, part * t : part * (t + 1), :].astype(f32) for t in range(blocks)], axis=1
            )
            shifts = ref[first, part * blocks :, :].astype(f32)
            shift = jnp.concatenate([shifts[t : t + 1] for t in range(blocks)], axis=1)
            differ = chain_col_ref[at, 0:1] != chain_row_ref[0:1, :]
            bias_full[at, :] = (moved + shift) + jnp.where(differ, cross, 0.0)
            grad_sum[at, :] = jnp.zeros((part, count), f32)

    def take(index):
        return jnp.concatenate(
            [rows_ref[t, index * size : (index + 1) * size, :] for t in range(blocks)], axis=1
        )

    query_t, key_t, value_t, grad_t = take(0), take(1), take(2), take(3)
    key = key_t.T
    value = value_t.T
    peak = jnp.full((1, count), -jnp.inf, f32)
    for p in range(count // chunk):
        at = pl.ds(chunk * p, chunk)
        part = dot(key[chunk * p : chunk * (p + 1)], query_t, ((1,), (0,))) + bias_full[at, :]
        logits[at, :] = part
        peak = jnp.maximum(peak, jnp.max(part, axis=0, keepdims=True))
    for p in range(count // chunk):
        at = pl.ds(chunk * p, chunk)
        exp_half[at, :] = jnp.exp(logits[at, :] - peak).astype(bf16)
    value_ones = jnp.concatenate([value_t, jnp.ones((16, count), bf16)], axis=0)
    summed = dot(value_ones, exp_half[...], ((1,), (0,)))
    inverse = 1.0 / summed[size : size + 1]
    attended_t = summed[:size] * inverse
    scaled_t = (grad_t.astype(f32) * inverse).astype(bf16)
    delta = jnp.sum(scaled_t.astype(f32) * attended_t, axis=0, keepdims=True)
    key_grad = []
    value_grad = []
    for p in range(count // chunk):
        at = pl.ds(chunk * p, chunk)
        weights = dot(value[chunk * p : chunk * (p + 1)], scaled_t, ((1,), (0,)))
        terms = exp_half[at, :]
        grad = terms.astype(f32) * (weights - delta)
        half = grad.astype(bf16)
        grad_half[at, :] = half
        grad_sum[at, :] += grad
        key_grad.append(dot(half, query_t, ((1,), (1,))))
        value_grad.append(dot(terms, scaled_t, ((1,), (1,))))
    query_grad_t = dot(key_t, grad_half[...], ((1,), (0,))) * factor
    key_grad_t = jnp.concatenate(key_grad, axis=0).T
    value_grad_t = jnp.concatenate(value_grad, axis=0).T
    for index, array in enumerate((attended_t, query_grad_t, key_grad_t, value_grad_t)):
        array = array.astype(bf16)
        for t in range(blocks):
            out_ref[t, index * size : (index + 1) * size, :] = array[:, t * lanes : (t + 1) * lanes]

    @pl.when(step == pl.num_programs(0) - 1)
    def _():
        part = grad_bias_refs[0].shape[2]
        cross_sum = jnp.zeros((1, count), f32)
        for p in range(count // part):
            at = pl.ds(pl.multiple_of(base_ref[p // 2] * (2 * part), 2 * part) + part * (p % 2), part)
            block = grad_sum[at, :]
            differ = chain_col_ref[at, 0:1] != chain_row_ref[0:1, :]
            cross_sum += jnp.sum(jnp.where(differ, block, 0.0), axis=0, keepdims=True)
            half = block.astype(bf16)
            for t in range(blocks):
                grad_bias_refs[p // 2][p % 2, t] = half[:, t * lanes : (t + 1) * lanes]
        cross_sum_ref[...] = jnp.broadcast_to(cross_sum, cross_sum_ref.shape)


def attend(base, rows, biases, cross, chains, factor):
    blocks, width, total = rows.shape
    lanes = 128
    samples = total // lanes
    count = blocks * lanes
    chain_col = jnp.broadcast_to(chains[:, None], (count, 128))
    chain_row = jnp.broadcast_to(chains[None, :], (8, count))
    whole = lambda shape: pl.BlockSpec(shape, lambda s: (0,) * len(shape))
    block_shape = (2, blocks, (biases[0].shape[1] - 16) // blocks, lanes)
    once = lambda shape: pl.BlockSpec(
        shape, lambda s: (0,) * len(shape), pipeline_mode=pl.Buffered(1)
    )
    return pl.pallas_call(
        functools.partial(attend_kernel, factor),
        grid=(samples,),
        in_specs=[
            pl.BlockSpec(memory_space=pltpu.SMEM),
            pl.BlockSpec(memory_space=pltpu.SMEM),
            whole(chain_col.shape),
            whole(chain_row.shape),
            pl.BlockSpec((blocks, width, lanes), lambda s: (0, 0, s)),
        ]
        + [once(bias.shape) for bias in biases],
        out_specs=[pl.BlockSpec((blocks, width, lanes), lambda s: (0, 0, s))]
        + [whole(block_shape)] * 8
        + [whole((8, count))],
        out_shape=[jax.ShapeDtypeStruct(rows.shape, bf16)]
        + [jax.ShapeDtypeStruct(block_shape, bf16)] * 8
        + [jax.ShapeDtypeStruct((8, count), f32)],
        scratch_shapes=[
            pltpu.VMEM((count, count), f32),
            pltpu.VMEM((count, count), f32),
            pltpu.VMEM((count, count), bf16),
            pltpu.VMEM((count, count), bf16),
            pltpu.VMEM((count, count), f32),
        ],
        compiler_params=pltpu.CompilerParams(vmem_limit_bytes=48 * 1024 * 1024),
        cost_estimate=pl.CostEstimate(
            flops=12 * samples * count * count * 48,
            bytes_accessed=16 * 1024 * 1024,
            transcendentals=samples * count * count,
        ),
    )(base, cross, chain_col, chain_row, rows, *biases)


def before_kernel(factor, core_ref, acts_ref, cots_ref, mod_ref, *refs):
    weight_refs = refs[:4]
    out_weight_ref, sent_ref, gate_ref, grad_gated_ref, normed_ref = refs[4:]
    rows, width = acts_ref.shape
    heads, _, _ = sent_ref.shape
    size = sent_ref.shape[1] // 4
    samples = mod_ref.shape[0]
    part = rows // samples
    for s in range(samples):
        at = slice(s * part, (s + 1) * part)
        wide = acts_ref[at, :].astype(f32)
        centred = wide - jnp.mean(wide, axis=1, keepdims=True)
        inv_std = lax.rsqrt(jnp.mean(centred * centred, axis=1, keepdims=True) + norm_epsilon)
        scale = 1.0 + mod_ref[s : s + 1, :width]
        shift = mod_ref[s : s + 1, width:]
        normed_ref[at, :] = (centred * inv_std * scale + shift).astype(bf16)
    normed = normed_ref[...]

    def put(index, array):
        for h in range(heads):
            sent_ref[h, index * size : (index + 1) * size, :] = array[h * size : (h + 1) * size]

    for index in range(3):
        projected = dot(normed, weight_refs[index][...], ((1,), (0,)))
        if index == 0:
            projected = projected * factor
        put(index, projected.T.astype(bf16))
    gate = jax.nn.sigmoid(dot(normed, weight_refs[3][...], ((1,), (0,)))).T
    gate_ref[...] = gate
    grad_gated = dot(cots_ref[...], out_weight_ref[...], ((1,), (1,))).T
    grad_gated_ref[...] = grad_gated
    put(3, (grad_gated * gate).astype(bf16))


def weight_specs(width, half):
    specs = [
        pl.BlockSpec((width, half), functools.partial(lambda b, i, c: (0, 2 * b + c[0]), b))
        for b in range(4)
    ]
    return specs + [pl.BlockSpec((half, width), lambda i, c: (c[0], 0))]


def spec_of(shape):
    return pl.BlockSpec(shape, lambda i, c: (0,) * len(shape))


def before(core, acts, cots, modulation, input_weight, output_matrix, heads, factor):
    rows, width = acts.shape
    half = width // 2
    size = half // heads
    shapes = [
        ((heads, 4 * size, rows), bf16),
        ((half, rows), f32),
        ((half, rows), f32),
        ((rows, width), bf16),
    ]
    return pl.pallas_call(
        functools.partial(before_kernel, factor),
        grid_spec=pltpu.PrefetchScalarGridSpec(
            num_scalar_prefetch=1,
            grid=(1,),
            in_specs=[spec_of(acts.shape), spec_of(cots.shape), spec_of(modulation.shape)]
            + weight_specs(width, half),
            out_specs=[spec_of(shape) for shape, _ in shapes],
        ),
        out_shape=[jax.ShapeDtypeStruct(shape, kind) for shape, kind in shapes],
        compiler_params=pltpu.CompilerParams(vmem_limit_bytes=48 * 1024 * 1024),
        cost_estimate=pl.CostEstimate(
            flops=2 * rows * width * 5 * half,
            bytes_accessed=8 * 1024 * 1024,
            transcendentals=rows * half,
        ),
    )(core, acts, cots, modulation, *([input_weight] * 4), output_matrix)


def after_kernel(core_ref, back_ref, gate_ref, grad_gated_ref, normed_ref, cots_ref, *refs):
    weight_refs = refs[:4]
    out_weight_ref, own_normed_ref, other_normed_ref, own_out_ref, other_out_ref = refs[4:9]
    payload_ref = refs[9]
    heads = back_ref.shape[0]
    size = back_ref.shape[1] // 4
    own = own_normed_ref.shape[0]
    width = own_normed_ref.shape[1]
    half = heads * size

    def take(index):
        return jnp.concatenate(
            [back_ref[h, index * size : (index + 1) * size, :] for h in range(heads)], axis=0
        )

    attended = take(0).astype(f32)
    gate = gate_ref[...]
    gated_wide = gate * attended
    gated = gated_wide.astype(bf16)
    grad_gate = (grad_gated_ref[...] * gated_wide * (1.0 - gate)).astype(bf16)
    normed_t = normed_ref[...].T
    total = None
    depth = 48
    for index, grad_t in enumerate((take(1), take(2), take(3), grad_gate)):
        grad = grad_t.T
        part = dot(grad, weight_refs[index][...], ((1,), (1,)))
        total = part if total is None else total + part
        weight_grad = dot(normed_t, grad, ((1,), (0,))).astype(bf16)
        for a in range(width // depth):
            payload_ref[4 * a + index, :depth, :] = weight_grad[depth * a : depth * (a + 1)]
    own_normed_ref[...] = total[:own]
    other_normed_ref[...] = total[own:].astype(bf16)
    output = dot(gated.T, out_weight_ref[...], ((1,), (0,)))
    own_out_ref[...] = output[:own]
    other_out_ref[...] = output[own:].astype(bf16)
    out_grad = dot(gated, cots_ref[...], ((1,), (0,))).astype(bf16)
    for d in range(payload_ref.shape[0]):
        if d < half // 8:
            block = out_grad[16 * (d // 2) : 16 * (d // 2 + 1), half * (d % 2) : half * (d % 2 + 1)]
        else:
            block = jnp.zeros((16, half), bf16)
        payload_ref[d, depth:, :] = block


def after(core, back, gate, grad_gated, normed, cots, input_weight, output_matrix):
    rows, width = normed.shape
    half = width // 2
    own = rows // 2
    shapes = [
        ((own, width), f32),
        ((own, width), bf16),
        ((own, width), f32),
        ((own, width), bf16),
        ((64, 64, half), bf16),
    ]
    operands = (back, gate, grad_gated, normed, cots)
    return pl.pallas_call(
        after_kernel,
        grid_spec=pltpu.PrefetchScalarGridSpec(
            num_scalar_prefetch=1,
            grid=(1,),
            in_specs=[spec_of(a.shape) for a in operands] + weight_specs(width, half),
            out_specs=[spec_of(shape) for shape, _ in shapes],
        ),
        out_shape=[jax.ShapeDtypeStruct(shape, kind) for shape, kind in shapes],
        compiler_params=pltpu.CompilerParams(vmem_limit_bytes=48 * 1024 * 1024),
        cost_estimate=pl.CostEstimate(
            flops=4 * rows * width * 5 * half,
            bytes_accessed=12 * 1024 * 1024,
            transcendentals=0,
        ),
    )(core, *operands, *([input_weight] * 4), output_matrix)


def assemble_kernel(place_ref, block_ref, *refs):
    input_ref, output_ref, stage, stage_out, sems = refs[-5:]
    half = block_ref.shape[2]
    depth = 48
    place = place_ref[0]
    copies = []
    for b in range(4):
        for group in range(2):
            for a in range(8 * group, 8 * group + 8):
                stage[b, depth * a : depth * (a + 1), :] = block_ref[4 * a + b, :depth, :].astype(f32)
            rows = slice(8 * depth * group, 8 * depth * (group + 1))
            at = pl.multiple_of((2 * b + place) * half, 128)
            copies.append(
                pltpu.make_async_copy(
                    stage.at[b, rows, :],
                    input_ref.at[rows, pl.ds(at, half)],
                    sems.at[len(copies)],
                )
            )
            copies[-1].start()
    for d in range(half // 8):
        stage_out[16 * (d // 2) : 16 * (d // 2 + 1), half * (d % 2) : half * (d % 2 + 1)] = block_ref[
            d, depth : depth + 16, :
        ].astype(f32)
    copies.append(pltpu.make_async_copy(stage_out, output_ref.at[place], sems.at[len(copies)]))
    copies[-1].start()
    for copy in copies:
        copy.wait()


def assemble(place, gathered, earlier):
    chips, depth, half = gathered.shape
    width = 2 * half
    anywhere = pl.BlockSpec(memory_space=pl.ANY)
    return pl.pallas_call(
        assemble_kernel,
        in_specs=[
            pl.BlockSpec(memory_space=pltpu.SMEM),
            pl.BlockSpec(memory_space=pltpu.VMEM),
        ]
        + [anywhere] * len(earlier),
        out_specs=[anywhere, anywhere],
        out_shape=[
            jax.ShapeDtypeStruct((width, 4 * width), f32),
            jax.ShapeDtypeStruct((2, half, width), f32),
        ],
        scratch_shapes=[
            pltpu.VMEM((4, width, half), f32),
            pltpu.VMEM((half, width), f32),
            pltpu.SemaphoreType.DMA((9,)),
        ],
        input_output_aliases={2 + k: k for k in range(len(earlier))},
        compiler_params=pltpu.CompilerParams(vmem_limit_bytes=24 * 1024 * 1024),
        cost_estimate=pl.CostEstimate(
            flops=0, bytes_accessed=10 * 1024 * 1024, transcendentals=0
        ),
    )(place, gathered, *earlier)


def gather_small_kernel(block_ref, out_ref):
    zy, rows, half = out_ref.shape
    blocks = block_ref.shape[0] // zy
    for p in range(zy):
        total = block_ref[blocks * p].astype(f32)
        for t in range(1, blocks):
            total = total + block_ref[blocks * p + t].astype(f32)
        out_ref[p] = total


def gather_small(gathered, zy, small_depth):
    chips, depth, half = gathered.shape
    return pl.pallas_call(
        gather_small_kernel,
        grid=(1,),
        in_specs=[
            pl.BlockSpec((chips, small_depth, half), lambda i: (0, depth // small_depth - 1, 0))
        ],
        out_specs=pl.BlockSpec((zy, small_depth, half), lambda i: (0, 0, 0)),
        out_shape=jax.ShapeDtypeStruct((zy, small_depth, half), f32),
        cost_estimate=pl.CostEstimate(flops=0, bytes_accessed=1 << 20, transcendentals=0),
    )(gathered)


def finish_small_kernel(tokens, mine_ref, other_ref, table_ref, sums_ref):
    zy, rows, half = mine_ref.shape
    levels = table_ref.shape[0]
    for r in range(4):
        total = jnp.zeros((levels, half), f32)
        for ref in (mine_ref, other_ref):
            row = lax.broadcasted_iota(jnp.int32, (rows, 1), 0)
            hot = []
            for p in range(zy):
                first = ref[p, 13:14, 144:145] * (1.0 / tokens)
                second = ref[p, 13:14, 145:146] * (1.0 / tokens)
                level = jnp.where(row < 4, first, second)
                kept = (row < 8) & (row % 4 == r)
                at = lax.broadcasted_iota(jnp.int32, (rows, levels), 1).astype(f32)
                hot.append(jnp.where((level == at) & kept, 1.0, 0.0))
            total += lax.dot_general(
                jnp.concatenate(hot, axis=0),
                ref[...].reshape(zy * rows, half),
                (((0,), (0,)), ((), ())),
                precision=lax.Precision.HIGHEST,
                preferred_element_type=f32,
            )
        table_ref[:, r * half : (r + 1) * half] = total
    sums_ref[0] = jnp.sum(mine_ref[...], axis=0)
    sums_ref[1] = jnp.sum(other_ref[...], axis=0)


def finish_small(mine, other, levels, tokens):
    zy, rows, half = mine.shape
    return pl.pallas_call(
        functools.partial(finish_small_kernel, tokens),
        out_shape=[
            jax.ShapeDtypeStruct((levels, 4 * half), f32),
            jax.ShapeDtypeStruct((2, rows, half), f32),
        ],
        cost_estimate=pl.CostEstimate(flops=0, bytes_accessed=2 << 20, transcendentals=0),
    )(mine, other)


def ring(array, shift):
    return lax.ppermute(array, "y", [(i, (i + shift) % 4) for i in range(4)])


def other_z(array):
    return lax.ppermute(array, "z_lo", [(0, 1), (1, 0)])


def spread_bias(own, far):
    result = []
    for block in (own, far):
        above = ring(block, 3)
        below = ring(block, 1)
        result += [block, above, below, ring(below[:1], 1), ring(above[1:], 3)]
    return result


def sum_bias(parts):
    add = lambda *arrays: sum(a.astype(f32) for a in arrays)
    ends = []
    for dz in (1, 0):
        near, above, far, below = parts[4 * dz : 4 * dz + 4]
        from_below = ring(far[:1], 1)
        from_above = ring(far[1:], 3)
        above = jnp.concatenate([add(above[:1], from_below).astype(bf16), above[1:]], axis=0)
        below = jnp.concatenate([below[:1], add(below[1:], from_above).astype(bf16)], axis=0)
        total = add(near, ring(above, 1), ring(below, 3))
        ends.append(total)
    far, near = ends
    return near + other_z(far.astype(bf16)).astype(f32)


def swap(array):
    return lax.ppermute(array, "core", [(0, 1), (1, 0)])


def exchange(array, axes):
    return lax.all_to_all(array, axes, 0, 0, tiled=True)


def spread(array, axes, count):
    return exchange(jnp.broadcast_to(array[None], (count,) + array.shape), axes)


def shards(
    activations,
    levels,
    ada_table,
    input_weight,
    output_matrix,
    pair_feats,
    pair_weight,
    cross_bias,
    chains,
    cotangent,
):
    own_samples, row_count, width = activations.shape
    heads = pair_weight.shape[1]
    size = width // heads
    col_count = pair_feats.shape[1]
    level_count = ada_table.shape[0]
    factor = 1.0 / math.sqrt(size)
    core = lax.axis_index("core")
    blocks = lax.axis_size("x") * lax.axis_size("z_hi")
    zy_count = lax.axis_size("z_lo") * lax.axis_size("y")
    chip_count = blocks * zy_count
    token = lax.axis_index(token_axes)
    half = width // 2

    pair_part = jnp.einsum("ijc,ch->hji", pair_feats, pair_weight, preferred_element_type=f32)
    shift = jnp.max(pair_part, axis=1, keepdims=True).astype(bf16)
    moved = (pair_part - shift.astype(f32)).astype(bf16)
    bias_sent = jnp.concatenate(
        [moved, jnp.broadcast_to(shift, (heads, 16, row_count))], axis=1
    )
    bias_got = exchange(bias_sent, head_axes)
    bias_own = jnp.concatenate(
        [
            bias_got[:, :col_count].reshape(2, blocks * col_count, row_count),
            bias_got[:, col_count].reshape(2, blocks, row_count),
            bias_got[:, col_count].reshape(2, blocks, row_count),
        ],
        axis=1,
    )
    bias_own = lax.optimization_barrier(bias_own)
    bias_far = other_z(bias_own)

    rows = own_samples * 2 * row_count
    core_at = jnp.reshape(core, (1,)).astype(jnp.int32)
    acts = jnp.concatenate([activations, swap(activations)], axis=0).reshape(rows, width)
    cots = jnp.concatenate([cotangent, swap(cotangent)], axis=0).reshape(rows, width)
    chip_levels = jnp.concatenate([levels, swap(levels)], axis=0)
    onehot = (
        chip_levels[:, None]
        == lax.broadcasted_iota(jnp.int32, (2 * own_samples, level_count), 1)
    ).astype(bf16)
    modulation = jnp.dot(onehot, ada_table, preferred_element_type=f32)
    sent, gate_open, grad_gated, normed = before(
        core_at, acts, cots, modulation, input_weight, output_matrix, blocks, factor
    )
    sent, bias_own, bias_far = lax.optimization_barrier((sent, bias_own, bias_far))
    biases = spread_bias(bias_own, bias_far)
    head_rows = exchange(sent, token_axes)
    z_at, y_at = lax.axis_index("z_lo"), lax.axis_index("y")
    base = jnp.stack(
        [((z_at + p // 4) % 2) * 4 + (y_at + p % 4) % 4 for p in range(8)]
    ).astype(jnp.int32)
    own_cross = lax.dynamic_slice_in_dim(cross_bias, core * blocks + token, 1)
    head_grads, *grad_biases, cross_sum = attend(
        base, head_rows, biases, own_cross, chains, factor
    )

    back = exchange(head_grads, token_axes)
    own_normed, other_normed, own_output, other_output, payload = after(
        core_at, back, gate_open, grad_gated, normed, cots, input_weight, output_matrix
    )
    own_shape = (own_samples, row_count, width)
    grad_normed = (own_normed + swap(other_normed).astype(f32)).reshape(own_shape)
    output = (own_output + swap(other_output).astype(f32)).reshape(own_shape)
    wide = activations.astype(f32)
    updated = (wide + output).astype(bf16)
    centred = wide - jnp.mean(wide, axis=2, keepdims=True)
    inv_std = lax.rsqrt(jnp.mean(centred * centred, axis=2, keepdims=True) + norm_epsilon)
    whitened = centred * inv_std
    grad_whitened = grad_normed * (1.0 + modulation[:own_samples, None, :width])
    grad_scale = jnp.sum(grad_normed * whitened, axis=1)
    grad_shift = jnp.sum(grad_normed, axis=1)
    grad_tokens = (
        cotangent.astype(f32)
        + inv_std
        * (
            grad_whitened
            - jnp.mean(grad_whitened, axis=2, keepdims=True)
            - whitened * jnp.mean(grad_whitened * whitened, axis=2, keepdims=True)
        )
    ).astype(bf16)

    bias_sum = sum_bias(grad_biases).astype(bf16)
    grad_bias_half = exchange(bias_sum.reshape(heads, col_count, row_count), head_axes)
    grad_pair = jnp.einsum(
        "hji,ch->ijc", grad_bias_half, pair_weight, preferred_element_type=f32
    ).astype(bf16)
    grad_pair_part = jnp.einsum(
        "ijc,hji->ch", pair_feats, grad_bias_half, preferred_element_type=f32
    )

    parts = exchange(payload, chip_axes)
    summed = jnp.sum(parts.astype(f32), axis=0).astype(bf16)
    pair_size = pair_weight.shape[0] * heads
    cross_part = jnp.sum(cross_sum[0])
    cross_high = cross_part.astype(bf16).astype(f32)
    at_token = (jnp.arange(blocks) == token).astype(f32)
    last = jnp.concatenate(
        [at_token * cross_high, at_token * (cross_part - cross_high), levels.astype(f32)]
    )
    flat = jnp.concatenate([grad_scale, grad_shift], axis=1).reshape(-1)
    flat = jnp.concatenate([flat, grad_pair_part.reshape(-1), last])
    small_depth = 16
    small = jnp.pad(flat, (0, small_depth * half - flat.size)).reshape(small_depth, half)
    block = jnp.concatenate([summed, small.astype(bf16)], axis=0)
    gathered = spread(block, chip_axes, chip_count)
    pair_shape = grad_pair.shape
    gathered, updated, grad_tokens, grad_pair = lax.optimization_barrier(
        (gathered, updated, grad_tokens, grad_pair.reshape(-1, pair_shape[2]))
    )
    grad_pair = grad_pair.reshape(pair_shape)
    mine_small = gather_small(gathered, zy_count, small_depth)
    other = swap(gathered)
    other_small = swap(mine_small)
    earlier = assemble(core_at, gathered, ())
    input_weight_grad, output_weight_grad = assemble(1 - core_at, other, earlier)
    output_weight_grad = output_weight_grad.reshape(width, width)
    grad_table, sums = finish_small(mine_small, other_small, level_count, blocks)
    pair_rows = (sums[0] + sums[1])[8:].reshape(-1)
    grad_pair_weight = pair_rows[:pair_size].reshape(pair_weight.shape)
    crosses = sums[:, 13, 128:144].reshape(2, 2, blocks).sum(axis=1)
    grad_cross = jnp.where(core == 0, crosses, crosses[::-1]).reshape(-1)
    return (
        updated,
        grad_tokens,
        grad_pair,
        input_weight_grad,
        output_weight_grad,
        grad_pair_weight,
        grad_cross,
        grad_table,
    )


def solution(mesh):
    fine = Mesh(mesh.devices.reshape(2, 4, 2, 4, 2), ("z_lo", "y", "core", "x", "z_hi"))
    sample = ("z_lo", "y", "core")
    token = ("x", "z_hi")
    placed = (
        P(sample, token, None),
        P(sample),
        P(),
        P(),
        P(),
        P(token, sample, None),
        P(),
        P(),
        P(),
        P(sample, token, None),
    )
    return jax.shard_map(
        shards,
        mesh=fine,
        in_specs=placed,
        out_specs=(
            P(sample, token, None),
            P(sample, token, None),
            P(token, sample, None),
            P(),
            P(),
            P(),
            P(),
            P(),
        ),
        check_vma=False,
    )
```

```python
import functools
import math

import jax
import jax.numpy as jnp
from jax import lax
from jax.experimental import pallas as pl
from jax.experimental.pallas import tpu as pltpu
from jax.sharding import Mesh, PartitionSpec as P

norm_epsilon = 1e-05
bf16 = jnp.bfloat16
f32 = jnp.float32
token_axes = ("x", "z_hi")
head_axes = ("z_lo", "x", "z_hi")
column_axes = ("z_lo", "y")
chip_axes = ("z_lo", "y", "x", "z_hi")
vmem_bytes = 60 * 1024 * 1024


def dot(a, b, dims):
    return lax.dot_general(a, b, (dims, ((), ())), preferred_element_type=f32)


def attend_places(refs):
    near, above, below, first, second = refs

    def find(place, part):
        dcore, dy = place // 4, place % 4
        if dy == 2:
            return (first, second)[part], (dcore, 0)
        return (near, above, None, below)[dy], (dcore, part)

    return find


def rows_of(base_ref, index, part):
    return pl.ds(pl.multiple_of(base_ref[index] * part, part), part)


def attend_kernel(factor, part, base_ref, cross_ref, chain_col_ref, chain_row_ref, rows_ref, *refs):
    bias_at, out_ref, grad_sum = attend_places(refs[:5]), refs[5], refs[6]
    bias_full, logits, exp_half, grad_half = refs[7:]
    blocks, width, lanes = rows_ref.shape
    size = width // 4
    count = blocks * lanes
    chunk = 128

    @pl.when(pl.program_id(0) == 0)
    def _():
        cross = cross_ref[0]
        for p in range(count // part):
            at = rows_of(base_ref, p, part)
            ref, lead = bias_at(p // 2, p % 2)
            moved = jnp.concatenate(
                [ref[(*lead, slice(part * t, part * (t + 1)))].astype(f32) for t in range(blocks)], axis=1
            )
            shifts = ref[(*lead, slice(part * blocks, part * blocks + 16))].astype(f32)
            shift = jnp.concatenate([shifts[t : t + 1] for t in range(blocks)], axis=1)
            differ = chain_col_ref[at, 0:1] != chain_row_ref[0:1, :]
            bias_full[at, :] = (moved + shift) + jnp.where(differ, cross, 0.0)
            grad_sum[at, :] = jnp.zeros((part, count), f32)

    def take(index):
        return jnp.concatenate(
            [rows_ref[t, index * size : (index + 1) * size, :] for t in range(blocks)], axis=1
        )

    query_t, key_t, value_t, grad_t = take(0), take(1), take(2), take(3)
    key = key_t.T
    value = value_t.T
    peak = jnp.full((1, count), -jnp.inf, f32)
    for p in range(count // chunk):
        at = pl.ds(chunk * p, chunk)
        scores = dot(key[chunk * p : chunk * (p + 1)], query_t, ((1,), (0,))) + bias_full[at, :]
        logits[at, :] = scores
        peak = jnp.maximum(peak, jnp.max(scores, axis=0, keepdims=True))
    for p in range(count // chunk):
        at = pl.ds(chunk * p, chunk)
        exp_half[at, :] = jnp.exp(logits[at, :] - peak).astype(bf16)
    value_ones = jnp.concatenate([value_t, jnp.ones((16, count), bf16)], axis=0)
    summed = dot(value_ones, exp_half[...], ((1,), (0,)))
    inverse = 1.0 / summed[size : size + 1]
    attended_t = summed[:size] * inverse
    scaled_t = (grad_t.astype(f32) * inverse).astype(bf16)
    delta = jnp.sum(scaled_t.astype(f32) * attended_t, axis=0, keepdims=True)
    key_grad = []
    value_grad = []
    for p in range(count // chunk):
        at = pl.ds(chunk * p, chunk)
        weights = dot(value[chunk * p : chunk * (p + 1)], scaled_t, ((1,), (0,)))
        terms = exp_half[at, :]
        grad = terms.astype(f32) * (weights - delta)
        half = grad.astype(bf16)
        grad_half[at, :] = half
        grad_sum[at, :] += grad
        key_grad.append(dot(half, query_t, ((1,), (1,))))
        value_grad.append(dot(terms, scaled_t, ((1,), (1,))))
    query_grad_t = dot(key_t, grad_half[...], ((1,), (0,))) * factor
    key_grad_t = jnp.concatenate(key_grad, axis=0).T
    value_grad_t = jnp.concatenate(value_grad, axis=0).T
    for index, array in enumerate((attended_t, query_grad_t, key_grad_t, value_grad_t)):
        array = array.astype(bf16)
        for t in range(blocks):
            out_ref[t, index * size : (index + 1) * size, :] = array[:, t * lanes : (t + 1) * lanes]


def pack_kernel(part, base_ref, chain_col_ref, chain_row_ref, sum_ref, *refs):
    grad_at, cross_ref = attend_places(refs[:5]), refs[5]
    count = sum_ref.shape[0]
    lanes = refs[0].shape[4]
    cross = jnp.zeros((1, count), f32)
    for p in range(count // part):
        at = rows_of(base_ref, p, part)
        block = sum_ref[at, :]
        differ = chain_col_ref[at, 0:1] != chain_row_ref[0:1, :]
        cross += jnp.sum(jnp.where(differ, block, 0.0), axis=0, keepdims=True)
        half = block.astype(bf16)
        ref, lead = grad_at(p // 2, p % 2)
        for t in range(count // lanes):
            ref[(*lead, t)] = half[:, t * lanes : (t + 1) * lanes]
    cross_ref[...] = jnp.broadcast_to(cross, cross_ref.shape)


def attend(base, rows, biases, cross, chains, factor):
    sources, width, total = rows.shape
    lanes = 128
    blocks = sources // 2
    own = total // lanes
    samples = 2 * own
    count = blocks * lanes
    chain_col = jnp.broadcast_to(chains[:, None], (count, 128))
    chain_row = jnp.broadcast_to(chains[None, :], (8, count))
    part = (biases[0].shape[2] - 16) // blocks
    once = lambda shape: pl.BlockSpec(
        shape, lambda s: (0,) * len(shape), pipeline_mode=pl.Buffered(1)
    )
    smem = pl.BlockSpec(memory_space=pltpu.SMEM)
    by_sample = pl.BlockSpec((blocks, width, lanes), lambda s: (s // own, 0, s % own))
    head_grads, grad_sum = pl.pallas_call(
        functools.partial(attend_kernel, factor, part),
        grid=(samples,),
        in_specs=[smem, smem, once(chain_col.shape), once(chain_row.shape), by_sample]
        + [once(bias.shape) for bias in biases],
        out_specs=[by_sample, once((count, count))],
        out_shape=[
            jax.ShapeDtypeStruct(rows.shape, bf16),
            jax.ShapeDtypeStruct((count, count), f32),
        ],
        scratch_shapes=[
            pltpu.VMEM((count, count), f32),
            pltpu.VMEM((count, count), f32),
            pltpu.VMEM((count, count), bf16),
            pltpu.VMEM((count, count), bf16),
        ],
        compiler_params=pltpu.CompilerParams(vmem_limit_bytes=vmem_bytes),
        cost_estimate=pl.CostEstimate(
            flops=12 * samples * count * count * 48,
            bytes_accessed=16 * 1024 * 1024,
            transcendentals=samples * count * count,
        ),
    )(base, cross, chain_col, chain_row, rows, *biases)
    whole_block = (2, 2, blocks, part, lanes)
    half_block = (2, 1, blocks, part, lanes)
    block_shapes = [whole_block] * 3 + [half_block] * 2
    vmem = pl.BlockSpec(memory_space=pltpu.VMEM)
    packed = pl.pallas_call(
        functools.partial(pack_kernel, part),
        in_specs=[smem, vmem, vmem, vmem],
        out_specs=[vmem] * 6,
        out_shape=[jax.ShapeDtypeStruct(shape, bf16) for shape in block_shapes]
        + [jax.ShapeDtypeStruct((8, count), f32)],
        compiler_params=pltpu.CompilerParams(vmem_limit_bytes=vmem_bytes),
        cost_estimate=pl.CostEstimate(
            flops=2 * count * count, bytes_accessed=8 * 1024 * 1024, transcendentals=0
        ),
    )(base, chain_col, chain_row, grad_sum)
    return head_grads, packed[:5], packed[5]


def norm_parts(wide):
    centred = wide - jnp.mean(wide, axis=1, keepdims=True)
    inv_std = lax.rsqrt(jnp.mean(centred * centred, axis=1, keepdims=True) + norm_epsilon)
    return centred * inv_std, inv_std


def before_kernel(
    factor,
    acts_ref,
    cots_ref,
    mod_ref,
    weight_ref,
    out_weight_ref,
    sent_ref,
    gate_ref,
    grad_gated_ref,
    normed_ref,
):
    rows, width = acts_ref.shape
    heads = sent_ref.shape[0]
    size = sent_ref.shape[1] // 4
    samples = mod_ref.shape[0]
    part = rows // samples
    for s in range(samples):
        at = slice(s * part, (s + 1) * part)
        whitened, _ = norm_parts(acts_ref[at, :].astype(f32))
        scale = 1.0 + mod_ref[s : s + 1, :width]
        shift = mod_ref[s : s + 1, width:]
        normed_ref[at, :] = (whitened * scale + shift).astype(bf16)
    normed = normed_ref[...]

    def project(index):
        return dot(normed, weight_ref[:, index * width : (index + 1) * width], ((1,), (0,)))

    def put(index, array):
        for h in range(heads):
            sent_ref[h, index * size : (index + 1) * size, :] = array[h * size : (h + 1) * size]

    put(0, (project(0) * factor).T.astype(bf16))
    put(1, project(1).T.astype(bf16))
    put(2, project(2).T.astype(bf16))
    gate = jax.nn.sigmoid(project(3)).T
    gate_ref[...] = gate
    grad_gated = dot(cots_ref[...], out_weight_ref[...], ((1,), (1,))).T
    grad_gated_ref[...] = grad_gated
    put(3, (grad_gated * gate).astype(bf16))


def in_vmem(kernel, shapes, operands, flops, smem=0):
    vmem = pl.BlockSpec(memory_space=pltpu.VMEM)
    scalars = [pl.BlockSpec(memory_space=pltpu.SMEM)] * smem
    size = sum(a.size * a.dtype.itemsize for a in operands)
    return pl.pallas_call(
        kernel,
        in_specs=scalars + [vmem] * (len(operands) - smem),
        out_specs=[vmem] * len(shapes),
        out_shape=[jax.ShapeDtypeStruct(shape, kind) for shape, kind in shapes],
        compiler_params=pltpu.CompilerParams(vmem_limit_bytes=vmem_bytes),
        cost_estimate=pl.CostEstimate(flops=flops, bytes_accessed=size, transcendentals=0),
    )(*operands)


def before(acts, cots, modulation, input_weight, output_matrix, heads, factor):
    rows, width = acts.shape
    shapes = [
        ((heads, 4 * width // heads, rows), bf16),
        ((width, rows), f32),
        ((width, rows), f32),
        ((rows, width), bf16),
    ]
    return in_vmem(
        functools.partial(before_kernel, factor),
        shapes,
        (acts, cots, modulation, input_weight, output_matrix),
        10 * rows * width * width,
    )


def gate_kernel(core_ref, back_ref, gate_ref, grad_gated_ref, keep_ref, send_ref):
    heads = back_ref.shape[0]
    size = back_ref.shape[1] // 4
    half = heads * size // 2

    def take(index, side):
        return jnp.concatenate(
            [
                back_ref[h, index * size : (index + 1) * size, :]
                for h in range(side * heads // 2, (side + 1) * heads // 2)
            ],
            axis=0,
        )

    def write(side, ref):
        at = slice(side * half, (side + 1) * half)
        gate = gate_ref[at, :]
        gated = gate * take(0, side).astype(f32)
        ref[0] = gated.astype(bf16)
        for index in (1, 2, 3):
            ref[index] = take(index, side)
        ref[4] = (grad_gated_ref[at, :] * gated * (1.0 - gate)).astype(bf16)

    @pl.when(core_ref[0] == 0)
    def _():
        write(0, keep_ref)
        write(1, send_ref)

    @pl.when(core_ref[0] == 1)
    def _():
        write(1, keep_ref)
        write(0, send_ref)


def rows_kernel(
    core_ref,
    keep_ref,
    send_ref,
    acts_ref,
    cots_ref,
    mod_ref,
    weight_ref,
    out_weight_ref,
    updated_ref,
    grad_ref,
    table_ref,
):
    rows, width = acts_ref.shape
    half = width // 2
    samples = mod_ref.shape[0]
    part = rows // samples
    grad_normed = None
    output = None
    for side, ref in ((core_ref[0], keep_ref), (1 - core_ref[0], send_ref)):
        for index in range(4):
            at = pl.multiple_of((2 * index + side) * half, 128)
            term = dot(ref[index + 1].T, weight_ref[:, pl.ds(at, half)], ((1,), (1,)))
            grad_normed = term if grad_normed is None else grad_normed + term
        at = pl.multiple_of(side * half, 128)
        term = dot(ref[0].T, out_weight_ref[pl.ds(at, half), :], ((1,), (0,)))
        output = term if output is None else output + term
    for s in range(samples):
        at = slice(s * part, (s + 1) * part)
        wide = acts_ref[at, :].astype(f32)
        updated_ref[at, :] = (wide + output[at]).astype(bf16)
        whitened, inv_std = norm_parts(wide)
        grad = grad_normed[at]
        products = grad * whitened
        scaled = grad * (1.0 + mod_ref[s : s + 1, :width])
        moved = scaled - jnp.mean(scaled, axis=1, keepdims=True)
        moved = moved - whitened * jnp.mean(scaled * whitened, axis=1, keepdims=True)
        grad_ref[at, :] = (cots_ref[at, :].astype(f32) + inv_std * moved).astype(bf16)
        for index, array in enumerate((products, grad)):
            total = jnp.sum(array, axis=0, keepdims=True)
            for k in range(2):
                row = 4 * s + 2 * index + k
                table_ref[row : row + 1, :] = total[:, k * half : (k + 1) * half]


def weights_kernel(keep_ref, got_ref, own_normed_ref, other_normed_ref, own_cots_ref, other_cots_ref, payload_ref):
    width = own_normed_ref.shape[1]
    half = width // 2
    depth = 48
    normed_t = jnp.concatenate([own_normed_ref[...], other_normed_ref[...]], axis=0).T
    for index in range(4):
        grad = jnp.concatenate([keep_ref[index + 1], got_ref[index + 1]], axis=1).T
        weight_grad = dot(normed_t, grad, ((1,), (0,))).astype(bf16)
        for a in range(width // depth):
            payload_ref[4 * a + index, :depth, :] = weight_grad[depth * a : depth * (a + 1)]
    gated = jnp.concatenate([keep_ref[0], got_ref[0]], axis=1)
    cots = jnp.concatenate([own_cots_ref[...], other_cots_ref[...]], axis=0)
    out_grad = dot(gated, cots, ((1,), (0,))).astype(bf16)
    for d in range(payload_ref.shape[0]):
        if d < half // 8:
            block = out_grad[16 * (d // 2) : 16 * (d // 2 + 1), half * (d % 2) : half * (d % 2 + 1)]
        else:
            block = jnp.zeros((16, half), bf16)
        payload_ref[d, depth:, :] = block


def assemble_kernel(place_ref, block_ref, *refs):
    input_ref, output_ref, stage, stage_out, sems = refs[-5:]
    half = block_ref.shape[2]
    depth = 48
    place = place_ref[0]
    copies = []
    for b in range(4):
        for group in range(2):
            for a in range(8 * group, 8 * group + 8):
                stage[b, depth * a : depth * (a + 1), :] = block_ref[4 * a + b, :depth, :].astype(f32)
            rows = slice(8 * depth * group, 8 * depth * (group + 1))
            at = pl.multiple_of((2 * b + place) * half, 128)
            copies.append(
                pltpu.make_async_copy(
                    stage.at[b, rows, :],
                    input_ref.at[rows, pl.ds(at, half)],
                    sems.at[len(copies)],
                )
            )
            copies[-1].start()
    for d in range(half // 8):
        stage_out[16 * (d // 2) : 16 * (d // 2 + 1), half * (d % 2) : half * (d % 2 + 1)] = block_ref[
            d, depth : depth + 16, :
        ].astype(f32)
    copies.append(pltpu.make_async_copy(stage_out, output_ref.at[place], sems.at[len(copies)]))
    copies[-1].start()
    for copy in copies:
        copy.wait()


def assemble(place, gathered, earlier):
    chips, depth, half = gathered.shape
    width = 2 * half
    anywhere = pl.BlockSpec(memory_space=pl.ANY)
    return pl.pallas_call(
        assemble_kernel,
        in_specs=[
            pl.BlockSpec(memory_space=pltpu.SMEM),
            pl.BlockSpec(memory_space=pltpu.VMEM),
        ]
        + [anywhere] * len(earlier),
        out_specs=[anywhere, anywhere],
        out_shape=[
            jax.ShapeDtypeStruct((width, 4 * width), f32),
            jax.ShapeDtypeStruct((2, half, width), f32),
        ],
        scratch_shapes=[
            pltpu.VMEM((4, width, half), f32),
            pltpu.VMEM((half, width), f32),
            pltpu.SemaphoreType.DMA((9,)),
        ],
        input_output_aliases={2 + k: k for k in range(len(earlier))},
        compiler_params=pltpu.CompilerParams(vmem_limit_bytes=vmem_bytes),
        cost_estimate=pl.CostEstimate(
            flops=0, bytes_accessed=10 * 1024 * 1024, transcendentals=0
        ),
    )(place, gathered, *earlier)


def gather_small_kernel(block_ref, out_ref):
    zy, rows, half = out_ref.shape
    blocks = block_ref.shape[0] // zy
    for p in range(zy):
        total = block_ref[blocks * p].astype(f32)
        for t in range(1, blocks):
            total = total + block_ref[blocks * p + t].astype(f32)
        out_ref[p] = total


def gather_small(gathered, zy, small_depth):
    chips, depth, half = gathered.shape
    return pl.pallas_call(
        gather_small_kernel,
        grid=(1,),
        in_specs=[
            pl.BlockSpec((chips, small_depth, half), lambda i: (0, depth // small_depth - 1, 0))
        ],
        out_specs=pl.BlockSpec((zy, small_depth, half), lambda i: (0, 0, 0)),
        out_shape=jax.ShapeDtypeStruct((zy, small_depth, half), f32),
        cost_estimate=pl.CostEstimate(flops=0, bytes_accessed=1 << 20, transcendentals=0),
    )(gathered)


def finish_small_kernel(tokens, mine_ref, other_ref, table_ref, sums_ref):
    zy, rows, half = mine_ref.shape
    levels = table_ref.shape[0]
    refs = (mine_ref, other_ref)
    values = jnp.concatenate([ref[...].reshape(zy * rows, half) for ref in refs], axis=0)
    high = values.astype(bf16)
    low = (values - high.astype(f32)).astype(bf16)
    row = lax.broadcasted_iota(jnp.int32, (rows, 1), 0)
    at = lax.broadcasted_iota(jnp.int32, (rows, levels), 1).astype(f32)
    same = []
    for ref in refs:
        for p in range(zy):
            first = ref[p, 13:14, 160:161] * (1.0 / tokens)
            second = ref[p, 13:14, 161:162] * (1.0 / tokens)
            same.append(jnp.where(row < 4, first, second) == at)
    for r in range(4):
        kept = (row < 8) & (row % 4 == r)
        hot = jnp.concatenate([jnp.where(s & kept, 1.0, 0.0) for s in same], axis=0).astype(bf16)
        table_ref[:, r * half : (r + 1) * half] = dot(hot, high, ((0,), (0,))) + dot(
            hot, low, ((0,), (0,))
        )
    sums_ref[0] = jnp.sum(mine_ref[...], axis=0)
    sums_ref[1] = jnp.sum(other_ref[...], axis=0)


def finish_small(mine, other, levels, tokens):
    zy, rows, half = mine.shape
    return pl.pallas_call(
        functools.partial(finish_small_kernel, tokens),
        out_shape=[
            jax.ShapeDtypeStruct((levels, 4 * half), f32),
            jax.ShapeDtypeStruct((2, rows, half), f32),
        ],
        cost_estimate=pl.CostEstimate(flops=0, bytes_accessed=2 << 20, transcendentals=0),
    )(mine, other)


def ring(array, shift):
    return lax.ppermute(array, "y", [(i, (i + shift) % 4) for i in range(4)])


def spread_bias(near):
    above = ring(near, 3)
    below = ring(near, 1)
    return [near, above, below, ring(below[:, :1], 1), ring(above[:, 1:], 3)]


def sum_bias(near, above, below, first, second):
    add = lambda *arrays: sum(a.astype(f32) for a in arrays)
    from_below = ring(first, 1)
    from_above = ring(second, 3)
    above = jnp.concatenate([add(above[:, :1], from_below).astype(bf16), above[:, 1:]], axis=1)
    below = jnp.concatenate([below[:, :1], add(below[:, 1:], from_above).astype(bf16)], axis=1)
    total = add(near, ring(above, 1), ring(below, 3))
    return total[0] + swap(total[1].astype(bf16)).astype(f32)


def swap(array):
    return lax.ppermute(array, "core", [(0, 1), (1, 0)])


def exchange(array, axes):
    return lax.all_to_all(array, axes, 0, 0, tiled=True)


def spread(array, axes, count):
    return exchange(jnp.broadcast_to(array[None], (count,) + array.shape), axes)


def shards(
    activations,
    levels,
    ada_table,
    input_weight,
    output_matrix,
    pair_feats,
    pair_weight,
    cross_bias,
    chains,
    cotangent,
):
    own_samples, row_count, width = activations.shape
    heads = pair_weight.shape[1]
    size = width // heads
    col_count = pair_feats.shape[1]
    level_count = ada_table.shape[0]
    factor = 1.0 / math.sqrt(size)
    core = lax.axis_index("core")
    blocks = lax.axis_size("x") * lax.axis_size("z_hi")
    zy_count = lax.axis_size("z_lo") * lax.axis_size("y")
    chip_count = blocks * zy_count
    half = width // 2

    pair_part = jnp.einsum("ijc,ch->hji", pair_feats, pair_weight, preferred_element_type=f32)
    shift = jnp.max(pair_part, axis=1, keepdims=True).astype(bf16)
    moved = (pair_part - shift.astype(f32)).astype(bf16)
    bias_sent = jnp.concatenate(
        [moved, jnp.broadcast_to(shift, (heads, 16, row_count))], axis=1
    )
    bias_got = exchange(bias_sent, head_axes)

    core_at = jnp.reshape(core, (1,)).astype(jnp.int32)
    acts = activations.reshape(-1, width)
    cots = cotangent.reshape(-1, width)
    onehot = (
        levels[:, None] == lax.broadcasted_iota(jnp.int32, (own_samples, level_count), 1)
    ).astype(bf16)
    modulation = jnp.dot(onehot, ada_table, preferred_element_type=f32)
    sent, gate_open, grad_gated, normed = before(
        acts, cots, modulation, input_weight, output_matrix, heads, factor
    )
    sent, bias_got = lax.optimization_barrier((sent, bias_got))
    bias_own = jnp.concatenate(
        [
            bias_got[:, :col_count].reshape(2, blocks * col_count, row_count),
            bias_got[:, col_count].reshape(2, blocks, row_count),
            bias_got[:, col_count].reshape(2, blocks, row_count),
        ],
        axis=1,
    )
    near = jnp.stack([bias_own, swap(bias_own)])
    sent, near = lax.optimization_barrier((sent, near))
    biases = spread_bias(near)
    head_rows = exchange(sent, head_axes)
    y_at = lax.axis_index("y")
    base = jnp.stack(
        [
            ((p % 2) * 4 + (y_at + p // 2) % 4) * 2 + (core + p // 8) % 2
            for p in range(16)
        ]
    ).astype(jnp.int32)
    head = lax.axis_index(head_axes)
    own_cross = lax.dynamic_slice_in_dim(cross_bias, head, 1)
    other_normed = swap(normed)
    other_cots = swap(cots)
    head_grads, grad_biases, cross_sum = attend(
        base, head_rows, biases, own_cross, chains, factor
    )

    back = exchange(head_grads, head_axes)
    half_shape = ((5, half, acts.shape[0]), bf16)
    keep, send = in_vmem(
        gate_kernel, [half_shape] * 2, (core_at, back, gate_open, grad_gated), 0, 1
    )
    got = swap(send)
    updated, grad_tokens, table_rows = in_vmem(
        rows_kernel,
        [(acts.shape, bf16), (acts.shape, bf16), ((8, half), f32)],
        (core_at, keep, send, acts, cots, modulation, input_weight, output_matrix),
        10 * acts.size * width,
        1,
    )
    updated = updated.reshape(activations.shape)
    grad_tokens = grad_tokens.reshape(activations.shape)
    (payload,) = in_vmem(
        weights_kernel,
        [((chip_count, 64, half), bf16)],
        (keep, got, normed, other_normed, cots, other_cots),
        10 * acts.size * width,
    )

    bias_sum = sum_bias(*grad_biases).astype(bf16)
    grad_bias_half = exchange(bias_sum.reshape(heads, col_count, row_count), head_axes)
    grad_pair = jnp.einsum(
        "hji,ch->ijc", grad_bias_half, pair_weight, preferred_element_type=f32
    ).astype(bf16)
    grad_pair_part = jnp.einsum(
        "ijc,hji->ch", pair_feats, grad_bias_half, preferred_element_type=f32
    )

    parts = exchange(payload, chip_axes)
    summed = jnp.sum(parts.astype(f32), axis=0).astype(bf16)
    pair_size = pair_weight.shape[0] * heads
    cross_part = jnp.sum(cross_sum[0])
    cross_high = cross_part.astype(bf16).astype(f32)
    at_head = (jnp.arange(heads) == head).astype(f32)
    last = jnp.concatenate(
        [at_head * cross_high, at_head * (cross_part - cross_high), levels.astype(f32)]
    )
    flat = jnp.concatenate([table_rows.reshape(-1), grad_pair_part.reshape(-1), last])
    small_depth = 16
    small = jnp.pad(flat, (0, small_depth * half - flat.size)).reshape(small_depth, half)
    block = jnp.concatenate([summed, small.astype(bf16)], axis=0)
    gathered = spread(block, chip_axes, chip_count)
    pair_shape = grad_pair.shape
    gathered, updated, grad_tokens, grad_pair = lax.optimization_barrier(
        (gathered, updated, grad_tokens, grad_pair.reshape(-1, pair_shape[2]))
    )
    grad_pair = grad_pair.reshape(pair_shape)
    mine_small = gather_small(gathered, zy_count, small_depth)
    other = swap(gathered)
    other_small = swap(mine_small)
    earlier = assemble(core_at, gathered, ())
    input_weight_grad, output_weight_grad = assemble(1 - core_at, other, earlier)
    output_weight_grad = output_weight_grad.reshape(width, width)
    grad_table, sums = finish_small(mine_small, other_small, level_count, blocks)
    pair_rows = (sums[0] + sums[1])[8:].reshape(-1)
    grad_pair_weight = pair_rows[:pair_size].reshape(pair_weight.shape)
    crosses = sums[0, 13] + sums[1, 13]
    grad_cross = crosses[128:144] + crosses[144:160]
    return (
        updated,
        grad_tokens,
        grad_pair,
        input_weight_grad,
        output_weight_grad,
        grad_pair_weight,
        grad_cross,
        grad_table,
    )


def solution(mesh):
    fine = Mesh(mesh.devices.reshape(2, 4, 2, 4, 2), ("z_lo", "y", "core", "x", "z_hi"))
    sample = ("z_lo", "y", "core")
    token = ("x", "z_hi")
    placed = (
        P(sample, token, None),
        P(sample),
        P(),
        P(),
        P(),
        P(token, sample, None),
        P(),
        P(),
        P(),
        P(sample, token, None),
    )
    return jax.shard_map(
        shards,
        mesh=fine,
        in_specs=placed,
        out_specs=(
            P(sample, token, None),
            P(sample, token, None),
            P(token, sample, None),
            P(),
            P(),
            P(),
            P(),
            P(),
        ),
        check_vma=False,
    )
```

```python
import functools
import math

import jax
import jax.numpy as jnp
from jax import lax
from jax.experimental import pallas as pl
from jax.experimental.pallas import tpu as pltpu
from jax.sharding import Mesh, PartitionSpec as P

norm_epsilon = 1e-05
bf16 = jnp.bfloat16
f32 = jnp.float32
token_axes = ("x", "z_hi")
head_axes = ("z_lo", "x", "z_hi")
column_axes = ("z_lo", "y")
chip_axes = ("z_lo", "y", "x", "z_hi")
vmem_bytes = 60 * 1024 * 1024


def dot(a, b, dims):
    return lax.dot_general(a, b, (dims, ((), ())), preferred_element_type=f32)


def attend_places(refs):
    near, above, below, first, second = refs

    def find(place, part):
        dcore, dy = place // 4, place % 4
        if dy == 2:
            return (first, second)[part], (dcore, 0)
        return (near, above, None, below)[dy], (dcore, part)

    return find


def rows_of(base_ref, index, part):
    return pl.ds(pl.multiple_of(base_ref[index] * part, part), part)


def attend_kernel(factor, part, base_ref, cross_ref, chain_col_ref, chain_row_ref, rows_ref, *refs):
    bias_at, out_ref, grad_refs, cross_sum_ref = attend_places(refs[:5]), refs[5], refs[6:10], refs[10]
    bias_full, logits, exp_half, grad_half, grad_sum = refs[11:]
    blocks, width, lanes = rows_ref.shape
    size = width // 4
    count = blocks * lanes
    chunk = 256

    @pl.when(pl.program_id(0) == 0)
    def _():
        cross = cross_ref[0]
        for p in range(count // part):
            at = rows_of(base_ref, p, part)
            ref, lead = bias_at(p // 2, p % 2)
            moved = jnp.concatenate(
                [ref[(*lead, slice(part * t, part * (t + 1)))].astype(f32) for t in range(blocks)], axis=1
            )
            shifts = ref[(*lead, slice(part * blocks, part * blocks + 16))].astype(f32)
            shift = jnp.concatenate([shifts[t : t + 1] for t in range(blocks)], axis=1)
            differ = chain_col_ref[at, 0:1] != chain_row_ref[0:1, :]
            bias_full[at, :] = (moved + shift) + jnp.where(differ, cross, 0.0)
            grad_sum[at, :] = jnp.zeros((part, count), f32)

    def take(index):
        return jnp.concatenate(
            [rows_ref[t, index * size : (index + 1) * size, :] for t in range(blocks)], axis=1
        )

    query_t, key_t, value_t, grad_t = take(0), take(1), take(2), take(3)
    key = key_t.T
    value = value_t.T
    query = query_t.T
    peak = jnp.full((1, count), -jnp.inf, f32)
    for p in range(count // chunk):
        at = pl.ds(chunk * p, chunk)
        scores = dot(key[chunk * p : chunk * (p + 1)], query_t, ((1,), (0,))) + bias_full[at, :]
        logits[at, :] = scores
        peak = jnp.maximum(peak, jnp.max(scores, axis=0, keepdims=True))
    for p in range(count // chunk):
        at = pl.ds(chunk * p, chunk)
        exp_half[at, :] = jnp.exp(logits[at, :] - peak).astype(bf16)
    value_ones = jnp.concatenate([value_t, jnp.ones((16, count), bf16)], axis=0)
    summed = dot(value_ones, exp_half[...], ((1,), (0,)))
    inverse = 1.0 / summed[size : size + 1]
    attended_t = summed[:size] * inverse
    scaled_t = (grad_t.astype(f32) * inverse).astype(bf16)
    scaled = scaled_t.T
    delta = jnp.sum(scaled_t.astype(f32) * attended_t, axis=0, keepdims=True)
    key_grad = []
    value_grad = []
    for p in range(count // chunk):
        at = pl.ds(chunk * p, chunk)
        weights = dot(value[chunk * p : chunk * (p + 1)], scaled_t, ((1,), (0,)))
        terms = exp_half[at, :]
        grad = terms.astype(f32) * (weights - delta)
        half = grad.astype(bf16)
        grad_half[at, :] = half
        grad_sum[at, :] += grad
        key_grad.append(dot(half, query, ((1,), (0,))))
        value_grad.append(dot(terms, scaled, ((1,), (0,))))
    query_grad_t = dot(key_t, grad_half[...], ((1,), (0,))) * factor
    key_grad_t = jnp.concatenate(key_grad, axis=0).T
    value_grad_t = jnp.concatenate(value_grad, axis=0).T
    for index, array in enumerate((attended_t, query_grad_t, key_grad_t, value_grad_t)):
        array = array.astype(bf16)
        for t in range(blocks):
            out_ref[t, index * size : (index + 1) * size, :] = array[:, t * lanes : (t + 1) * lanes]

    @pl.when(pl.program_id(0) == pl.num_programs(0) - 1)
    def _():
        cross_sum = jnp.zeros((1, count), f32)
        for p in range(count // part):
            at = rows_of(base_ref, p, part)
            block = grad_sum[at, :]
            differ = chain_col_ref[at, 0:1] != chain_row_ref[0:1, :]
            cross_sum += jnp.sum(jnp.where(differ, block, 0.0), axis=0, keepdims=True)
            half = block.astype(bf16)
            for t in range(blocks):
                grad_refs[p // 2 % 4][p // 8, p % 2, t] = half[:, t * lanes : (t + 1) * lanes]
        cross_sum_ref[...] = jnp.broadcast_to(cross_sum, cross_sum_ref.shape)


def attend(base, rows, biases, cross, chains, factor):
    sources, width, total = rows.shape
    lanes = 128
    blocks = sources // 2
    own = total // lanes
    samples = 2 * own
    count = blocks * lanes
    chain_col = jnp.broadcast_to(chains[:, None], (count, 128))
    chain_row = jnp.broadcast_to(chains[None, :], (8, count))
    part = (biases[0].shape[2] - 16) // blocks
    once = lambda shape: pl.BlockSpec(
        shape, lambda s: (0,) * len(shape), pipeline_mode=pl.Buffered(1)
    )
    smem = pl.BlockSpec(memory_space=pltpu.SMEM)
    by_sample = pl.BlockSpec((blocks, width, lanes), lambda s: (s // own, 0, s % own))
    block_shape = (2, 2, blocks, part, lanes)
    head_grads, *grad_biases, cross_sum = pl.pallas_call(
        functools.partial(attend_kernel, factor, part),
        grid=(samples,),
        in_specs=[smem, smem, once(chain_col.shape), once(chain_row.shape), by_sample]
        + [once(bias.shape) for bias in biases],
        out_specs=[by_sample] + [once(block_shape)] * 4 + [once((8, count))],
        out_shape=[jax.ShapeDtypeStruct(rows.shape, bf16)]
        + [jax.ShapeDtypeStruct(block_shape, bf16)] * 4
        + [jax.ShapeDtypeStruct((8, count), f32)],
        scratch_shapes=[
            pltpu.VMEM((count, count), f32),
            pltpu.VMEM((count, count), f32),
            pltpu.VMEM((count, count), bf16),
            pltpu.VMEM((count, count), bf16),
            pltpu.VMEM((count, count), f32),
        ],
        compiler_params=pltpu.CompilerParams(vmem_limit_bytes=vmem_bytes),
        cost_estimate=pl.CostEstimate(
            flops=12 * samples * count * count * 48,
            bytes_accessed=16 * 1024 * 1024,
            transcendentals=samples * count * count,
        ),
    )(base, cross, chain_col, chain_row, rows, *biases)
    return head_grads, grad_biases, cross_sum


def norm_parts(wide):
    centred = wide - jnp.mean(wide, axis=1, keepdims=True)
    inv_std = lax.rsqrt(jnp.mean(centred * centred, axis=1, keepdims=True) + norm_epsilon)
    return centred * inv_std, inv_std


def before_kernel(
    factor,
    acts_ref,
    cots_ref,
    mod_ref,
    weight_ref,
    out_weight_ref,
    sent_ref,
    gate_ref,
    grad_gated_ref,
    normed_ref,
):
    rows, width = acts_ref.shape
    heads = sent_ref.shape[0]
    size = sent_ref.shape[1] // 4
    samples = mod_ref.shape[0]
    part = rows // samples
    for s in range(samples):
        at = slice(s * part, (s + 1) * part)
        whitened, _ = norm_parts(acts_ref[at, :].astype(f32))
        scale = 1.0 + mod_ref[s : s + 1, :width]
        shift = mod_ref[s : s + 1, width:]
        normed_ref[at, :] = (whitened * scale + shift).astype(bf16)
    normed = normed_ref[...]

    def project(index):
        return dot(normed, weight_ref[:, index * width : (index + 1) * width], ((1,), (0,)))

    def put(index, array):
        for h in range(heads):
            sent_ref[h, index * size : (index + 1) * size, :] = array[h * size : (h + 1) * size]

    put(0, (project(0) * factor).T.astype(bf16))
    put(1, project(1).T.astype(bf16))
    put(2, project(2).T.astype(bf16))
    gate = jax.nn.sigmoid(project(3)).T
    gate_ref[...] = gate
    grad_gated = dot(cots_ref[...], out_weight_ref[...], ((1,), (1,))).T
    grad_gated_ref[...] = grad_gated
    put(3, (grad_gated * gate).astype(bf16))


def in_vmem(kernel, shapes, operands, flops, smem=0):
    vmem = pl.BlockSpec(memory_space=pltpu.VMEM)
    scalars = [pl.BlockSpec(memory_space=pltpu.SMEM)] * smem
    size = sum(a.size * a.dtype.itemsize for a in operands)
    return pl.pallas_call(
        kernel,
        in_specs=scalars + [vmem] * (len(operands) - smem),
        out_specs=[vmem] * len(shapes),
        out_shape=[jax.ShapeDtypeStruct(shape, kind) for shape, kind in shapes],
        compiler_params=pltpu.CompilerParams(vmem_limit_bytes=vmem_bytes),
        cost_estimate=pl.CostEstimate(flops=flops, bytes_accessed=size, transcendentals=0),
    )(*operands)


def before(acts, cots, modulation, input_weight, output_matrix, heads, factor):
    rows, width = acts.shape
    shapes = [
        ((heads, 4 * width // heads, rows), bf16),
        ((width, rows), f32),
        ((width, rows), f32),
        ((rows, width), bf16),
    ]
    return in_vmem(
        functools.partial(before_kernel, factor),
        shapes,
        (acts, cots, modulation, input_weight, output_matrix),
        10 * rows * width * width,
    )


def gate_kernel(core_ref, back_ref, gate_ref, grad_gated_ref, keep_ref, send_ref):
    heads = back_ref.shape[0]
    size = back_ref.shape[1] // 4
    half = heads * size // 2

    def take(index, side):
        return jnp.concatenate(
            [
                back_ref[h, index * size : (index + 1) * size, :]
                for h in range(side * heads // 2, (side + 1) * heads // 2)
            ],
            axis=0,
        )

    def write(side, ref):
        at = slice(side * half, (side + 1) * half)
        gate = gate_ref[at, :]
        gated = gate * take(0, side).astype(f32)
        ref[0] = gated.astype(bf16)
        for index in (1, 2, 3):
            ref[index] = take(index, side)
        ref[4] = (grad_gated_ref[at, :] * gated * (1.0 - gate)).astype(bf16)

    @pl.when(core_ref[0] == 0)
    def _():
        write(0, keep_ref)
        write(1, send_ref)

    @pl.when(core_ref[0] == 1)
    def _():
        write(1, keep_ref)
        write(0, send_ref)


def rows_kernel(
    core_ref,
    keep_ref,
    send_ref,
    acts_ref,
    cots_ref,
    mod_ref,
    weight_ref,
    out_weight_ref,
    updated_ref,
    grad_ref,
    table_ref,
):
    rows, width = acts_ref.shape
    half = width // 2
    samples = mod_ref.shape[0]
    part = rows // samples
    grad_normed = None
    output = None
    for side, ref in ((core_ref[0], keep_ref), (1 - core_ref[0], send_ref)):
        for index in range(4):
            at = pl.multiple_of((2 * index + side) * half, 128)
            term = dot(ref[index + 1].T, weight_ref[:, pl.ds(at, half)], ((1,), (1,)))
            grad_normed = term if grad_normed is None else grad_normed + term
        at = pl.multiple_of(side * half, 128)
        term = dot(ref[0].T, out_weight_ref[pl.ds(at, half), :], ((1,), (0,)))
        output = term if output is None else output + term
    for s in range(samples):
        at = slice(s * part, (s + 1) * part)
        wide = acts_ref[at, :].astype(f32)
        updated_ref[at, :] = (wide + output[at]).astype(bf16)
        whitened, inv_std = norm_parts(wide)
        grad = grad_normed[at]
        products = grad * whitened
        scaled = grad * (1.0 + mod_ref[s : s + 1, :width])
        moved = scaled - jnp.mean(scaled, axis=1, keepdims=True)
        moved = moved - whitened * jnp.mean(scaled * whitened, axis=1, keepdims=True)
        grad_ref[at, :] = (cots_ref[at, :].astype(f32) + inv_std * moved).astype(bf16)
        for index, array in enumerate((products, grad)):
            total = jnp.sum(array, axis=0, keepdims=True)
            for k in range(2):
                row = 4 * s + 2 * index + k
                table_ref[row : row + 1, :] = total[:, k * half : (k + 1) * half]


def weights_kernel(keep_ref, got_ref, own_normed_ref, other_normed_ref, own_cots_ref, other_cots_ref, payload_ref):
    width = own_normed_ref.shape[1]
    half = width // 2
    depth = 48
    normed_t = jnp.concatenate([own_normed_ref[...], other_normed_ref[...]], axis=0).T
    for index in range(4):
        grad = jnp.concatenate([keep_ref[index + 1], got_ref[index + 1]], axis=1).T
        weight_grad = dot(normed_t, grad, ((1,), (0,))).astype(bf16)
        for a in range(width // depth):
            payload_ref[4 * a + index, :depth, :] = weight_grad[depth * a : depth * (a + 1)]
    gated = jnp.concatenate([keep_ref[0], got_ref[0]], axis=1)
    cots = jnp.concatenate([own_cots_ref[...], other_cots_ref[...]], axis=0)
    out_grad = dot(gated, cots, ((1,), (0,))).astype(bf16)
    for d in range(payload_ref.shape[0]):
        if d < half // 8:
            block = out_grad[16 * (d // 2) : 16 * (d // 2 + 1), half * (d % 2) : half * (d % 2 + 1)]
        else:
            block = jnp.zeros((16, half), bf16)
        payload_ref[d, depth:, :] = block


def assemble_kernel(place_ref, block_ref, *refs):
    input_ref, output_ref, blocks, stage, stage_out, in_sems, sems = refs[-7:]
    half = blocks.shape[2]
    depth = 48
    groups = in_sems.shape[0]
    chips = blocks.shape[0]
    size = chips // groups
    place = place_ref[0]
    arrivals = []
    for g in range(groups):
        at = slice(size * g, size * (g + 1))
        arrivals.append(pltpu.make_async_copy(block_ref.at[at], blocks.at[at], in_sems.at[g]))
        arrivals[-1].start()
    copies = []
    for g in range(groups):
        arrivals[g].wait()
        for b in range(4):
            for a in range(size // 4 * g, size // 4 * (g + 1)):
                stage[b, depth * a : depth * (a + 1), :] = blocks[4 * a + b, :depth, :].astype(f32)
            rows = slice(size // 4 * depth * g, size // 4 * depth * (g + 1))
            at = pl.multiple_of((2 * b + place) * half, 128)
            copies.append(
                pltpu.make_async_copy(
                    stage.at[b, rows, :],
                    input_ref.at[rows, pl.ds(at, half)],
                    sems.at[len(copies)],
                )
            )
            copies[-1].start()
    for d in range(half // 8):
        stage_out[16 * (d // 2) : 16 * (d // 2 + 1), half * (d % 2) : half * (d % 2 + 1)] = blocks[
            d, depth : depth + 16, :
        ].astype(f32)
    copies.append(pltpu.make_async_copy(stage_out, output_ref.at[place], sems.at[len(copies)]))
    copies[-1].start()
    for copy in copies:
        copy.wait()


def assemble(place, gathered, earlier):
    chips, depth, half = gathered.shape
    width = 2 * half
    groups = 4
    anywhere = pl.BlockSpec(memory_space=pl.ANY)
    return pl.pallas_call(
        assemble_kernel,
        in_specs=[pl.BlockSpec(memory_space=pltpu.SMEM), anywhere] + [anywhere] * len(earlier),
        out_specs=[anywhere, anywhere],
        out_shape=[
            jax.ShapeDtypeStruct((width, 4 * width), f32),
            jax.ShapeDtypeStruct((2, half, width), f32),
        ],
        scratch_shapes=[
            pltpu.VMEM((chips, depth, half), bf16),
            pltpu.VMEM((4, width, half), f32),
            pltpu.VMEM((half, width), f32),
            pltpu.SemaphoreType.DMA((groups,)),
            pltpu.SemaphoreType.DMA((4 * groups + 1,)),
        ],
        input_output_aliases={2 + k: k for k in range(len(earlier))},
        compiler_params=pltpu.CompilerParams(vmem_limit_bytes=vmem_bytes),
        cost_estimate=pl.CostEstimate(
            flops=0, bytes_accessed=10 * 1024 * 1024, transcendentals=0
        ),
    )(place, gathered, *earlier)


def total_kernel(parts_ref, small_ref, out_ref):
    chips, depth, _ = parts_ref.shape
    total = parts_ref[0].astype(f32)
    for p in range(1, chips):
        total = total + parts_ref[p].astype(f32)
    total = total.astype(bf16)
    small = small_ref[...].astype(bf16)
    for p in range(out_ref.shape[0]):
        out_ref[p, :depth, :] = total
        out_ref[p, depth:, :] = small


def gather_small_kernel(block_ref, out_ref):
    zy, rows, half = out_ref.shape
    blocks = block_ref.shape[0] // zy
    for p in range(zy):
        total = block_ref[blocks * p].astype(f32)
        for t in range(1, blocks):
            total = total + block_ref[blocks * p + t].astype(f32)
        out_ref[p] = total


def gather_small(gathered, zy, small_depth):
    chips, depth, half = gathered.shape
    return pl.pallas_call(
        gather_small_kernel,
        grid=(1,),
        in_specs=[
            pl.BlockSpec((chips, small_depth, half), lambda i: (0, depth // small_depth - 1, 0))
        ],
        out_specs=pl.BlockSpec((zy, small_depth, half), lambda i: (0, 0, 0)),
        out_shape=jax.ShapeDtypeStruct((zy, small_depth, half), f32),
        cost_estimate=pl.CostEstimate(flops=0, bytes_accessed=1 << 20, transcendentals=0),
    )(gathered)


def finish_small_kernel(tokens, mine_ref, other_ref, table_ref, pair_ref, cross_ref):
    zy, rows, half = mine_ref.shape
    levels = table_ref.shape[0]
    refs = (mine_ref, other_ref)
    values = jnp.concatenate([ref[...].reshape(zy * rows, half) for ref in refs], axis=0)
    high = values.astype(bf16)
    low = (values - high.astype(f32)).astype(bf16)
    row = lax.broadcasted_iota(jnp.int32, (rows, 1), 0)
    at = lax.broadcasted_iota(jnp.int32, (rows, levels), 1).astype(f32)
    same = []
    for ref in refs:
        for p in range(zy):
            first = ref[p, 13:14, 160:161] * (1.0 / tokens)
            second = ref[p, 13:14, 161:162] * (1.0 / tokens)
            same.append(jnp.where(row < 4, first, second) == at)
    for r in range(4):
        kept = (row < 8) & (row % 4 == r)
        hot = jnp.concatenate([jnp.where(s & kept, 1.0, 0.0) for s in same], axis=0).astype(bf16)
        table_ref[:, r * half : (r + 1) * half] = dot(hot, high, ((0,), (0,))) + dot(
            hot, low, ((0,), (0,))
        )
    sums = jnp.sum(mine_ref[...], axis=0) + jnp.sum(other_ref[...], axis=0)
    heads, lanes = pair_ref.shape
    per_row = half // lanes
    pair = [
        sums[8 + h // per_row : 9 + h // per_row, h % per_row * lanes : (h % per_row + 1) * lanes]
        for h in range(heads)
    ]
    pair_ref[...] = jnp.concatenate(pair, axis=0)
    last = sums[13:14, lanes : 2 * lanes]
    cross_ref[...] = last[:, :heads] + last[:, heads : 2 * heads]


def ring(array, shift):
    return lax.ppermute(array, "y", [(i, (i + shift) % 4) for i in range(4)])


def spread_bias(near):
    above = ring(near, 3)
    below = ring(near, 1)
    return [near, above, below, ring(below[:, :1], 1), ring(above[:, 1:], 3)]


def sum_bias(near, above, far, below):
    arrived = [near, ring(above, 1), ring(far, 2), ring(below, 3)]
    total = sum(a.astype(f32) for a in arrived)
    return total[0] + swap(total[1].astype(bf16)).astype(f32)


def swap(array):
    return lax.ppermute(array, "core", [(0, 1), (1, 0)])


def exchange(array, axes):
    return lax.all_to_all(array, axes, 0, 0, tiled=True)


def shards(
    activations,
    levels,
    ada_table,
    input_weight,
    output_matrix,
    pair_feats,
    pair_weight,
    cross_bias,
    chains,
    cotangent,
):
    own_samples, row_count, width = activations.shape
    heads = pair_weight.shape[1]
    size = width // heads
    col_count = pair_feats.shape[1]
    level_count = ada_table.shape[0]
    factor = 1.0 / math.sqrt(size)
    core = lax.axis_index("core")
    blocks = lax.axis_size("x") * lax.axis_size("z_hi")
    zy_count = lax.axis_size("z_lo") * lax.axis_size("y")
    chip_count = blocks * zy_count
    half = width // 2

    pair_part = jnp.einsum("ijc,ch->hji", pair_feats, pair_weight, preferred_element_type=f32)
    shift = jnp.max(pair_part, axis=1, keepdims=True).astype(bf16)
    moved = (pair_part - shift.astype(f32)).astype(bf16)
    bias_sent = jnp.concatenate(
        [moved, jnp.broadcast_to(shift, (heads, 16, row_count))], axis=1
    )
    bias_got = exchange(bias_sent, head_axes)

    core_at = jnp.reshape(core, (1,)).astype(jnp.int32)
    acts = activations.reshape(-1, width)
    cots = cotangent.reshape(-1, width)
    onehot = (
        levels[:, None] == lax.broadcasted_iota(jnp.int32, (own_samples, level_count), 1)
    ).astype(bf16)
    modulation = jnp.dot(onehot, ada_table, preferred_element_type=f32)
    sent, gate_open, grad_gated, normed = before(
        acts, cots, modulation, input_weight, output_matrix, heads, factor
    )
    sent, bias_got = lax.optimization_barrier((sent, bias_got))
    bias_own = jnp.concatenate(
        [
            bias_got[:, :col_count].reshape(2, blocks * col_count, row_count),
            bias_got[:, col_count].reshape(2, blocks, row_count),
            bias_got[:, col_count].reshape(2, blocks, row_count),
        ],
        axis=1,
    )
    near = jnp.stack([bias_own, swap(bias_own)])
    sent, near = lax.optimization_barrier((sent, near))
    biases = spread_bias(near)
    head_rows = exchange(sent, head_axes)
    y_at = lax.axis_index("y")
    base = jnp.stack(
        [
            ((p % 2) * 4 + (y_at + p // 2) % 4) * 2 + (core + p // 8) % 2
            for p in range(16)
        ]
    ).astype(jnp.int32)
    head = lax.axis_index(head_axes)
    own_cross = lax.dynamic_slice_in_dim(cross_bias, head, 1)
    other_normed = swap(normed)
    other_cots = swap(cots)
    head_grads, grad_biases, cross_sum = attend(
        base, head_rows, biases, own_cross, chains, factor
    )

    back = exchange(head_grads, head_axes)
    half_shape = ((5, half, acts.shape[0]), bf16)
    keep, send = in_vmem(
        gate_kernel, [half_shape] * 2, (core_at, back, gate_open, grad_gated), 0, 1
    )
    got = swap(send)
    updated, grad_tokens, table_rows = in_vmem(
        rows_kernel,
        [(acts.shape, bf16), (acts.shape, bf16), ((8, half), f32)],
        (core_at, keep, send, acts, cots, modulation, input_weight, output_matrix),
        10 * acts.size * width,
        1,
    )
    updated = updated.reshape(activations.shape)
    grad_tokens = grad_tokens.reshape(activations.shape)
    (payload,) = in_vmem(
        weights_kernel,
        [((chip_count, 64, half), bf16)],
        (keep, got, normed, other_normed, cots, other_cots),
        10 * acts.size * width,
    )

    bias_sum = sum_bias(*grad_biases).astype(bf16)
    grad_bias_half = exchange(bias_sum.reshape(heads, col_count, row_count), head_axes)
    grad_pair = jnp.einsum(
        "hji,ch->ijc", grad_bias_half, pair_weight, preferred_element_type=f32
    ).astype(bf16)
    grad_pair_part = jnp.einsum(
        "ijc,hji->hc", pair_feats, grad_bias_half, preferred_element_type=f32
    )

    parts = exchange(payload, chip_axes)
    cross_part = jnp.sum(cross_sum[0])
    cross_high = cross_part.astype(bf16).astype(f32)
    at_head = (jnp.arange(heads) == head).astype(f32)
    last = jnp.concatenate(
        [at_head * cross_high, at_head * (cross_part - cross_high), levels.astype(f32)]
    )
    flat = jnp.concatenate([table_rows.reshape(-1), grad_pair_part.reshape(-1), last])
    small_depth = 16
    small = jnp.pad(flat, (0, small_depth * half - flat.size)).reshape(small_depth, half)
    (block,) = in_vmem(
        total_kernel,
        [((chip_count, parts.shape[1] + small_depth, half), bf16)],
        (parts, small),
        parts.size,
    )
    gathered = exchange(block, chip_axes)
    pair_shape = grad_pair.shape
    gathered, updated, grad_tokens, grad_pair = lax.optimization_barrier(
        (gathered, updated, grad_tokens, grad_pair.reshape(-1, pair_shape[2]))
    )
    grad_pair = grad_pair.reshape(pair_shape)
    mine_small = gather_small(gathered, zy_count, small_depth)
    other = swap(gathered)
    other_small = swap(mine_small)
    earlier = assemble(core_at, gathered, ())
    input_weight_grad, output_weight_grad = assemble(1 - core_at, other, earlier)
    output_weight_grad = output_weight_grad.reshape(width, width)
    grad_table, grad_pair_weight, grad_cross = in_vmem(
        functools.partial(finish_small_kernel, blocks),
        [((level_count, 4 * half), f32), (pair_weight.shape[::-1], f32), ((1, heads), f32)],
        (mine_small, other_small),
        0,
    )
    grad_pair_weight = grad_pair_weight.T
    grad_cross = grad_cross.reshape(heads)
    return (
        updated,
        grad_tokens,
        grad_pair,
        input_weight_grad,
        output_weight_grad,
        grad_pair_weight,
        grad_cross,
        grad_table,
    )


def solution(mesh):
    fine = Mesh(mesh.devices.reshape(2, 4, 2, 4, 2), ("z_lo", "y", "core", "x", "z_hi"))
    sample = ("z_lo", "y", "core")
    token = ("x", "z_hi")
    placed = (
        P(sample, token, None),
        P(sample),
        P(),
        P(),
        P(),
        P(token, sample, None),
        P(),
        P(),
        P(),
        P(sample, token, None),
    )
    return jax.shard_map(
        shards,
        mesh=fine,
        in_specs=placed,
        out_specs=(
            P(sample, token, None),
            P(sample, token, None),
            P(token, sample, None),
            P(),
            P(),
            P(),
            P(),
            P(),
        ),
        check_vma=False,
    )
```

```python
import functools
import math

import jax
import jax.numpy as jnp
from jax import lax
from jax.experimental import pallas as pl
from jax.experimental.pallas import tpu as pltpu
from jax.sharding import Mesh, PartitionSpec as P

norm_epsilon = 1e-05
bf16 = jnp.bfloat16
f32 = jnp.float32
token_axes = ("x", "z_hi")
head_axes = ("z_lo", "x", "z_hi")
column_axes = ("z_lo", "y")
chip_axes = ("z_lo", "y", "x", "z_hi")
vmem_bytes = 60 * 1024 * 1024


def dot(a, b, dims):
    return lax.dot_general(a, b, (dims, ((), ())), preferred_element_type=f32)


def attend_places(refs):
    near, above, below, first, second = refs

    def find(place, part):
        dcore, dy = place // 4, place % 4
        if dy == 2:
            return (first, second)[part], (dcore, 0)
        return (near, above, None, below)[dy], (dcore, part)

    return find


def rows_of(base_ref, index, part):
    return pl.ds(pl.multiple_of(base_ref[index] * part, part), part)


def attend_kernel(factor, part, base_ref, cross_ref, chain_col_ref, chain_row_ref, rows_ref, *refs):
    bias_at, out_ref, grad_refs, cross_sum_ref = attend_places(refs[:5]), refs[5], refs[6:10], refs[10]
    bias_full, logits, exp_half, grad_half, grad_sum = refs[11:]
    blocks, width, lanes = rows_ref.shape
    size = width // 4
    count = blocks * lanes
    chunk = 256

    @pl.when(pl.program_id(0) == 0)
    def _():
        cross = cross_ref[0]
        for p in range(count // part):
            at = rows_of(base_ref, p, part)
            ref, lead = bias_at(p // 2, p % 2)
            moved = jnp.concatenate(
                [ref[(*lead, slice(part * t, part * (t + 1)))].astype(f32) for t in range(blocks)], axis=1
            )
            shifts = ref[(*lead, slice(part * blocks, part * blocks + 16))].astype(f32)
            shift = jnp.concatenate([shifts[t : t + 1] for t in range(blocks)], axis=1)
            differ = chain_col_ref[at, 0:1] != chain_row_ref[0:1, :]
            bias_full[at, :] = (moved + shift) + jnp.where(differ, cross, 0.0)
            grad_sum[at, :] = jnp.zeros((part, count), f32)

    def take(index):
        return jnp.concatenate(
            [rows_ref[t, index * size : (index + 1) * size, :] for t in range(blocks)], axis=1
        )

    query_t, key_t, value_t, grad_t = take(0), take(1), take(2), take(3)
    key = key_t.T
    value = value_t.T
    query = query_t.T
    peak = jnp.full((1, count), -jnp.inf, f32)
    for p in range(count // chunk):
        at = pl.ds(chunk * p, chunk)
        scores = dot(key[chunk * p : chunk * (p + 1)], query_t, ((1,), (0,))) + bias_full[at, :]
        logits[at, :] = scores
        peak = jnp.maximum(peak, jnp.max(scores, axis=0, keepdims=True))
    for p in range(count // chunk):
        at = pl.ds(chunk * p, chunk)
        exp_half[at, :] = jnp.exp(logits[at, :] - peak).astype(bf16)
    value_ones = jnp.concatenate([value_t, jnp.ones((16, count), bf16)], axis=0)
    summed = dot(value_ones, exp_half[...], ((1,), (0,)))
    inverse = 1.0 / summed[size : size + 1]
    attended_t = summed[:size] * inverse
    scaled_t = (grad_t.astype(f32) * inverse).astype(bf16)
    scaled = scaled_t.T
    delta = jnp.sum(scaled_t.astype(f32) * attended_t, axis=0, keepdims=True)
    key_grad = []
    value_grad = []
    for p in range(count // chunk):
        at = pl.ds(chunk * p, chunk)
        weights = dot(value[chunk * p : chunk * (p + 1)], scaled_t, ((1,), (0,)))
        terms = exp_half[at, :]
        grad = terms.astype(f32) * (weights - delta)
        half = grad.astype(bf16)
        grad_half[at, :] = half
        grad_sum[at, :] += grad
        key_grad.append(dot(half, query, ((1,), (0,))))
        value_grad.append(dot(terms, scaled, ((1,), (0,))))
    query_grad_t = dot(key_t, grad_half[...], ((1,), (0,))) * factor
    key_grad_t = jnp.concatenate(key_grad, axis=0).T
    value_grad_t = jnp.concatenate(value_grad, axis=0).T
    for index, array in enumerate((attended_t, query_grad_t, key_grad_t, value_grad_t)):
        array = array.astype(bf16)
        for t in range(blocks):
            out_ref[t, index * size : (index + 1) * size, :] = array[:, t * lanes : (t + 1) * lanes]

    @pl.when(pl.program_id(0) == pl.num_programs(0) - 1)
    def _():
        cross_sum = jnp.zeros((1, count), f32)
        for p in range(count // part):
            at = rows_of(base_ref, p, part)
            block = grad_sum[at, :]
            differ = chain_col_ref[at, 0:1] != chain_row_ref[0:1, :]
            cross_sum += jnp.sum(jnp.where(differ, block, 0.0), axis=0, keepdims=True)
            half = block.astype(bf16)
            for t in range(blocks):
                grad_refs[p // 2 % 4][p // 8, p % 2, t] = half[:, t * lanes : (t + 1) * lanes]
        cross_sum_ref[...] = jnp.broadcast_to(cross_sum, cross_sum_ref.shape)


def attend(base, rows, biases, cross, chains, factor):
    sources, width, total = rows.shape
    lanes = 128
    blocks = sources // 2
    own = total // lanes
    samples = 2 * own
    count = blocks * lanes
    chain_col, chain_row = chains
    part = (biases[0].shape[2] - 16) // blocks
    once = lambda shape: pl.BlockSpec(
        shape, lambda s: (0,) * len(shape), pipeline_mode=pl.Buffered(1)
    )
    smem = pl.BlockSpec(memory_space=pltpu.SMEM)
    by_sample = pl.BlockSpec((blocks, width, lanes), lambda s: (s // own, 0, s % own))
    block_shape = (2, 2, blocks, part, lanes)
    head_grads, *grad_biases, cross_sum = pl.pallas_call(
        functools.partial(attend_kernel, factor, part),
        grid=(samples,),
        in_specs=[smem, smem, once(chain_col.shape), once(chain_row.shape), by_sample]
        + [once(bias.shape) for bias in biases],
        out_specs=[by_sample] + [once(block_shape)] * 4 + [once((8, count))],
        out_shape=[jax.ShapeDtypeStruct(rows.shape, bf16)]
        + [jax.ShapeDtypeStruct(block_shape, bf16)] * 4
        + [jax.ShapeDtypeStruct((8, count), f32)],
        scratch_shapes=[
            pltpu.VMEM((count, count), f32),
            pltpu.VMEM((count, count), f32),
            pltpu.VMEM((count, count), bf16),
            pltpu.VMEM((count, count), bf16),
            pltpu.VMEM((count, count), f32),
        ],
        compiler_params=pltpu.CompilerParams(vmem_limit_bytes=vmem_bytes),
        cost_estimate=pl.CostEstimate(
            flops=12 * samples * count * count * 48,
            bytes_accessed=16 * 1024 * 1024,
            transcendentals=samples * count * count,
        ),
    )(base, cross, chain_col, chain_row, rows, *biases)
    return head_grads, grad_biases, cross_sum


def norm_parts(wide):
    centred = wide - jnp.mean(wide, axis=1, keepdims=True)
    inv_std = lax.rsqrt(jnp.mean(centred * centred, axis=1, keepdims=True) + norm_epsilon)
    return centred * inv_std, inv_std


def before_kernel(
    factor,
    acts_ref,
    cots_ref,
    mod_ref,
    weight_ref,
    out_weight_ref,
    sent_ref,
    gate_ref,
    grad_gated_ref,
    normed_ref,
):
    rows, width = acts_ref.shape
    heads = sent_ref.shape[0]
    size = sent_ref.shape[1] // 4
    samples = mod_ref.shape[0]
    part = rows // samples
    for s in range(samples):
        at = slice(s * part, (s + 1) * part)
        whitened, _ = norm_parts(acts_ref[at, :].astype(f32))
        scale = 1.0 + mod_ref[s : s + 1, :width]
        shift = mod_ref[s : s + 1, width:]
        normed_ref[at, :] = (whitened * scale + shift).astype(bf16)
    normed = normed_ref[...]

    def project(index):
        return dot(normed, weight_ref[:, index * width : (index + 1) * width], ((1,), (0,)))

    def put(index, array):
        for h in range(heads):
            sent_ref[h, index * size : (index + 1) * size, :] = array[h * size : (h + 1) * size]

    put(0, (project(0) * factor).T.astype(bf16))
    put(1, project(1).T.astype(bf16))
    put(2, project(2).T.astype(bf16))
    gate = jax.nn.sigmoid(project(3)).T
    gate_ref[...] = gate
    grad_gated = dot(cots_ref[...], out_weight_ref[...], ((1,), (1,))).T
    grad_gated_ref[...] = grad_gated
    put(3, (grad_gated * gate).astype(bf16))


def in_vmem(kernel, shapes, operands, flops, smem=0):
    vmem = pl.BlockSpec(memory_space=pltpu.VMEM)
    scalars = [pl.BlockSpec(memory_space=pltpu.SMEM)] * smem
    size = sum(a.size * a.dtype.itemsize for a in operands)
    return pl.pallas_call(
        kernel,
        in_specs=scalars + [vmem] * (len(operands) - smem),
        out_specs=[vmem] * len(shapes),
        out_shape=[jax.ShapeDtypeStruct(shape, kind) for shape, kind in shapes],
        compiler_params=pltpu.CompilerParams(vmem_limit_bytes=vmem_bytes),
        cost_estimate=pl.CostEstimate(flops=flops, bytes_accessed=size, transcendentals=0),
    )(*operands)


def before(acts, cots, modulation, input_weight, output_matrix, heads, factor):
    rows, width = acts.shape
    shapes = [
        ((heads, 4 * width // heads, rows), bf16),
        ((width, rows), f32),
        ((width, rows), f32),
        ((rows, width), bf16),
    ]
    return in_vmem(
        functools.partial(before_kernel, factor),
        shapes,
        (acts, cots, modulation, input_weight, output_matrix),
        10 * rows * width * width,
    )


def gate_kernel(core_ref, back_ref, gate_ref, grad_gated_ref, keep_ref, send_ref):
    heads = back_ref.shape[0]
    size = back_ref.shape[1] // 4
    half = heads * size // 2

    def take(index, side):
        return jnp.concatenate(
            [
                back_ref[h, index * size : (index + 1) * size, :]
                for h in range(side * heads // 2, (side + 1) * heads // 2)
            ],
            axis=0,
        )

    def write(side, ref):
        at = slice(side * half, (side + 1) * half)
        gate = gate_ref[at, :]
        gated = gate * take(0, side).astype(f32)
        ref[0] = gated.astype(bf16)
        for index in (1, 2, 3):
            ref[index] = take(index, side)
        ref[4] = (grad_gated_ref[at, :] * gated * (1.0 - gate)).astype(bf16)

    @pl.when(core_ref[0] == 0)
    def _():
        write(0, keep_ref)
        write(1, send_ref)

    @pl.when(core_ref[0] == 1)
    def _():
        write(1, keep_ref)
        write(0, send_ref)


def rows_kernel(
    core_ref,
    keep_ref,
    send_ref,
    acts_ref,
    cots_ref,
    mod_ref,
    weight_ref,
    out_weight_ref,
    updated_ref,
    grad_ref,
    table_ref,
):
    rows, width = acts_ref.shape
    half = width // 2
    samples = mod_ref.shape[0]
    part = rows // samples
    grad_normed = None
    output = None
    for side, ref in ((core_ref[0], keep_ref), (1 - core_ref[0], send_ref)):
        for index in range(4):
            at = pl.multiple_of((2 * index + side) * half, 128)
            term = dot(ref[index + 1].T, weight_ref[:, pl.ds(at, half)], ((1,), (1,)))
            grad_normed = term if grad_normed is None else grad_normed + term
        at = pl.multiple_of(side * half, 128)
        term = dot(ref[0].T, out_weight_ref[pl.ds(at, half), :], ((1,), (0,)))
        output = term if output is None else output + term
    for s in range(samples):
        at = slice(s * part, (s + 1) * part)
        wide = acts_ref[at, :].astype(f32)
        updated_ref[at, :] = (wide + output[at]).astype(bf16)
        whitened, inv_std = norm_parts(wide)
        grad = grad_normed[at]
        products = grad * whitened
        scaled = grad * (1.0 + mod_ref[s : s + 1, :width])
        moved = scaled - jnp.mean(scaled, axis=1, keepdims=True)
        moved = moved - whitened * jnp.mean(scaled * whitened, axis=1, keepdims=True)
        grad_ref[at, :] = (cots_ref[at, :].astype(f32) + inv_std * moved).astype(bf16)
        for index, array in enumerate((products, grad)):
            total = jnp.sum(array, axis=0, keepdims=True)
            for k in range(2):
                row = 4 * s + 2 * index + k
                table_ref[row : row + 1, :] = total[:, k * half : (k + 1) * half]


def weights_kernel(keep_ref, got_ref, own_normed_ref, other_normed_ref, own_cots_ref, other_cots_ref, payload_ref):
    width = own_normed_ref.shape[1]
    half = width // 2
    depth = 48
    normed_t = jnp.concatenate([own_normed_ref[...], other_normed_ref[...]], axis=0).T
    for index in range(4):
        grad = jnp.concatenate([keep_ref[index + 1], got_ref[index + 1]], axis=1).T
        weight_grad = dot(normed_t, grad, ((1,), (0,))).astype(bf16)
        for a in range(width // depth):
            payload_ref[4 * a + index, :depth, :] = weight_grad[depth * a : depth * (a + 1)]
    gated = jnp.concatenate([keep_ref[0], got_ref[0]], axis=1)
    cots = jnp.concatenate([own_cots_ref[...], other_cots_ref[...]], axis=0)
    out_grad = dot(gated, cots, ((1,), (0,))).astype(bf16)
    for d in range(payload_ref.shape[0]):
        if d < half // 8:
            block = out_grad[16 * (d // 2) : 16 * (d // 2 + 1), half * (d % 2) : half * (d % 2 + 1)]
        else:
            block = jnp.zeros((16, half), bf16)
        payload_ref[d, depth:, :] = block


def assemble_kernel(place_ref, block_ref, *refs):
    input_ref, output_ref, blocks, stage, stage_out, in_sems, sems = refs[-7:]
    half = blocks.shape[2]
    depth = 48
    groups = in_sems.shape[0]
    chips = blocks.shape[0]
    size = chips // groups
    place = place_ref[0]
    arrivals = []
    for g in range(groups):
        at = slice(size * g, size * (g + 1))
        arrivals.append(pltpu.make_async_copy(block_ref.at[at], blocks.at[at], in_sems.at[g]))
        arrivals[-1].start()
    copies = []
    for g in range(groups):
        arrivals[g].wait()
        for b in range(4):
            for a in range(size // 4 * g, size // 4 * (g + 1)):
                stage[b, depth * a : depth * (a + 1), :] = blocks[4 * a + b, :depth, :].astype(f32)
            rows = slice(size // 4 * depth * g, size // 4 * depth * (g + 1))
            at = pl.multiple_of((2 * b + place) * half, 128)
            copies.append(
                pltpu.make_async_copy(
                    stage.at[b, rows, :],
                    input_ref.at[rows, pl.ds(at, half)],
                    sems.at[len(copies)],
                )
            )
            copies[-1].start()
    for d in range(half // 8):
        stage_out[16 * (d // 2) : 16 * (d // 2 + 1), half * (d % 2) : half * (d % 2 + 1)] = blocks[
            d, depth : depth + 16, :
        ].astype(f32)
    copies.append(pltpu.make_async_copy(stage_out, output_ref.at[place], sems.at[len(copies)]))
    copies[-1].start()
    for copy in copies:
        copy.wait()


def assemble(place, gathered, earlier):
    chips, depth, half = gathered.shape
    width = 2 * half
    groups = 4
    anywhere = pl.BlockSpec(memory_space=pl.ANY)
    return pl.pallas_call(
        assemble_kernel,
        in_specs=[pl.BlockSpec(memory_space=pltpu.SMEM), anywhere] + [anywhere] * len(earlier),
        out_specs=[anywhere, anywhere],
        out_shape=[
            jax.ShapeDtypeStruct((width, 4 * width), f32),
            jax.ShapeDtypeStruct((2, half, width), f32),
        ],
        scratch_shapes=[
            pltpu.VMEM((chips, depth, half), bf16),
            pltpu.VMEM((4, width, half), f32),
            pltpu.VMEM((half, width), f32),
            pltpu.SemaphoreType.DMA((groups,)),
            pltpu.SemaphoreType.DMA((4 * groups + 1,)),
        ],
        input_output_aliases={2 + k: k for k in range(len(earlier))},
        compiler_params=pltpu.CompilerParams(vmem_limit_bytes=vmem_bytes),
        cost_estimate=pl.CostEstimate(
            flops=0, bytes_accessed=10 * 1024 * 1024, transcendentals=0
        ),
    )(place, gathered, *earlier)


def total_kernel(parts_ref, small_ref, out_ref):
    chips, depth, _ = parts_ref.shape
    total = parts_ref[0].astype(f32)
    for p in range(1, chips):
        total = total + parts_ref[p].astype(f32)
    total = total.astype(bf16)
    small = small_ref[...].astype(bf16)
    for p in range(out_ref.shape[0]):
        out_ref[p, :depth, :] = total
        out_ref[p, depth:, :] = small


def gather_small_kernel(block_ref, out_ref):
    zy = out_ref.shape[0]
    blocks = block_ref.shape[0] // zy
    for p in range(zy):
        for parity in range(2):
            total = None
            for t in range(blocks):
                if t // 2 % 2 == parity:
                    term = block_ref[blocks * p + t]
                    total = term if total is None else total + term
            out_ref[p, parity] = total


def finish_small_kernel(sharers, mine_ref, other_ref, table_ref, pair_ref, cross_ref):
    zy, _, rows, half = mine_ref.shape
    levels = table_ref.shape[0]
    heads, lanes = pair_ref.shape
    refs = (mine_ref, other_ref)
    values = jnp.concatenate([ref[...].reshape(zy * 2 * rows, half) for ref in refs], axis=0)
    high = values.astype(bf16)
    low = (values - high.astype(f32)).astype(bf16)
    row = lax.broadcasted_iota(jnp.int32, (rows, 1), 0)
    at = lax.broadcasted_iota(jnp.int32, (rows, levels), 1).astype(f32)
    same = []
    for ref in refs:
        for p in range(zy):
            for parity in range(2):
                lane = 2 * lanes + 2 * heads + parity
                level = ref[p, parity, 6:7, lane : lane + 1] * (1.0 / sharers)
                same.append(level == at)
    for r in range(4):
        hot = jnp.concatenate([jnp.where(s & (row == r), 1.0, 0.0) for s in same], axis=0)
        hot = hot.astype(bf16)
        table_ref[:, r * half : (r + 1) * half] = dot(hot, high, ((0,), (0,))) + dot(
            hot, low, ((0,), (0,))
        )
    sums = jnp.sum(mine_ref[...], axis=0) + jnp.sum(other_ref[...], axis=0)
    per_row = half // lanes
    pair = []
    for h in range(heads):
        parity, j = h // (heads // 2), h % (heads // 2)
        at_row, at_lane = 4 + j // per_row, j % per_row * lanes
        pair.append(sums[parity, at_row : at_row + 1, at_lane : at_lane + lanes])
    pair_ref[...] = jnp.concatenate(pair, axis=0)
    last = sums[0, 6:7, 2 * lanes :] + sums[1, 6:7, 2 * lanes :]
    cross_ref[...] = last[:, :heads] + last[:, heads : 2 * heads]


def ring(array, shift):
    return lax.ppermute(array, "y", [(i, (i + shift) % 4) for i in range(4)])


def spread_bias(near):
    above = ring(near, 3)
    below = ring(near, 1)
    return [near, above, below, ring(below[:, :1], 1), ring(above[:, 1:], 3)]


def sum_bias(near, above, far, below):
    arrived = [near, ring(above, 1), ring(far, 2), ring(below, 3)]
    total = sum(a.astype(f32) for a in arrived)
    return total[0] + swap(total[1].astype(bf16)).astype(f32)


def swap(array):
    return lax.ppermute(array, "core", [(0, 1), (1, 0)])


def exchange(array, axes):
    return lax.all_to_all(array, axes, 0, 0, tiled=True)


def shards(
    activations,
    levels,
    ada_table,
    input_weight,
    output_matrix,
    pair_feats,
    pair_weight,
    cross_bias,
    chains,
    cotangent,
):
    own_samples, row_count, width = activations.shape
    heads = pair_weight.shape[1]
    size = width // heads
    col_count = pair_feats.shape[1]
    level_count = ada_table.shape[0]
    factor = 1.0 / math.sqrt(size)
    core = lax.axis_index("core")
    blocks = lax.axis_size("x") * lax.axis_size("z_hi")
    zy_count = lax.axis_size("z_lo") * lax.axis_size("y")
    chip_count = blocks * zy_count
    half = width // 2

    pair_part = jnp.einsum("ijc,ch->hji", pair_feats, pair_weight, preferred_element_type=f32)
    shift = jnp.max(pair_part, axis=1, keepdims=True).astype(bf16)
    moved = (pair_part - shift.astype(f32)).astype(bf16)
    bias_sent = jnp.concatenate(
        [moved, jnp.broadcast_to(shift, (heads, 16, row_count))], axis=1
    )
    bias_got = exchange(bias_sent, head_axes)

    core_at = jnp.reshape(core, (1,)).astype(jnp.int32)
    acts = activations.reshape(-1, width)
    cots = cotangent.reshape(-1, width)
    onehot = (
        levels[:, None] == lax.broadcasted_iota(jnp.int32, (own_samples, level_count), 1)
    ).astype(bf16)
    modulation = jnp.dot(onehot, ada_table, preferred_element_type=f32)
    sent, gate_open, grad_gated, normed = before(
        acts, cots, modulation, input_weight, output_matrix, heads, factor
    )
    count = chains.shape[0]
    chain_col = jnp.broadcast_to(chains[:, None], (count, 128))
    chain_row = jnp.broadcast_to(chains[None, :], (8, count))
    sent, bias_got, chain_col, chain_row = lax.optimization_barrier(
        (sent, bias_got, chain_col, chain_row)
    )
    bias_own = jnp.concatenate(
        [
            bias_got[:, :col_count].reshape(2, blocks * col_count, row_count),
            bias_got[:, col_count].reshape(2, blocks, row_count),
            bias_got[:, col_count].reshape(2, blocks, row_count),
        ],
        axis=1,
    )
    near = jnp.stack([bias_own, swap(bias_own)])
    sent, near = lax.optimization_barrier((sent, near))
    biases = spread_bias(near)
    head_rows = exchange(sent, head_axes)
    y_at = lax.axis_index("y")
    base = jnp.stack(
        [
            ((p % 2) * 4 + (y_at + p // 2) % 4) * 2 + (core + p // 8) % 2
            for p in range(16)
        ]
    ).astype(jnp.int32)
    head = lax.axis_index(head_axes)
    own_cross = lax.dynamic_slice_in_dim(cross_bias, head, 1)
    other_normed = swap(normed)
    other_cots = swap(cots)
    head_grads, grad_biases, cross_sum = attend(
        base, head_rows, biases, own_cross, (chain_col, chain_row), factor
    )

    back = exchange(head_grads, head_axes)
    half_shape = ((5, half, acts.shape[0]), bf16)
    keep, send = in_vmem(
        gate_kernel, [half_shape] * 2, (core_at, back, gate_open, grad_gated), 0, 1
    )
    got = swap(send)
    updated, grad_tokens, table_rows = in_vmem(
        rows_kernel,
        [(acts.shape, bf16), (acts.shape, bf16), ((8, half), f32)],
        (core_at, keep, send, acts, cots, modulation, input_weight, output_matrix),
        10 * acts.size * width,
        1,
    )
    updated = updated.reshape(activations.shape)
    grad_tokens = grad_tokens.reshape(activations.shape)
    (payload,) = in_vmem(
        weights_kernel,
        [((chip_count, 64, half), bf16)],
        (keep, got, normed, other_normed, cots, other_cots),
        10 * acts.size * width,
    )

    bias_sum = sum_bias(*grad_biases).astype(bf16)
    grad_bias_half = exchange(bias_sum.reshape(heads, col_count, row_count), head_axes)
    grad_pair = jnp.einsum(
        "hji,ch->ijc", grad_bias_half, pair_weight, preferred_element_type=f32
    ).astype(bf16)
    grad_pair_part = jnp.einsum(
        "ijc,hji->hc", pair_feats, grad_bias_half, preferred_element_type=f32
    )

    parts = exchange(payload, chip_axes)
    cross_part = jnp.sum(cross_sum[0])
    cross_high = cross_part.astype(bf16).astype(f32)
    at_head = (jnp.arange(heads) == head).astype(f32)
    last = jnp.concatenate(
        [at_head * cross_high, at_head * (cross_part - cross_high), levels.astype(f32)]
    )
    halves = jnp.concatenate(
        [table_rows.reshape(2, -1), grad_pair_part.reshape(2, -1)], axis=1
    )
    odd = lax.axis_index("x") % 2
    pick = lambda index: lax.dynamic_index_in_dim(halves, index, 0, keepdims=False)
    shared = pick(odd) + lax.ppermute(pick(1 - odd), "x", [(i, i ^ 1) for i in range(4)])
    flat = jnp.concatenate([shared, last])
    small_depth = 8
    small = jnp.pad(flat, (0, small_depth * half - flat.size)).reshape(small_depth, half)
    (block,) = in_vmem(
        total_kernel,
        [((chip_count, parts.shape[1] + small_depth, half), bf16)],
        (parts, small),
        parts.size,
    )
    gathered = exchange(block, chip_axes)
    pair_shape = grad_pair.shape
    gathered, updated, grad_tokens, grad_pair = lax.optimization_barrier(
        (gathered, updated, grad_tokens, grad_pair.reshape(-1, pair_shape[2]))
    )
    grad_pair = grad_pair.reshape(pair_shape)
    (mine_small,) = in_vmem(
        gather_small_kernel,
        [((zy_count, 2, small_depth, half), f32)],
        (gathered[:, -small_depth:].astype(f32),),
        0,
    )
    other = swap(gathered)
    other_small = swap(mine_small)
    earlier = assemble(core_at, gathered, ())
    input_weight_grad, output_weight_grad = assemble(1 - core_at, other, earlier)
    output_weight_grad = output_weight_grad.reshape(width, width)
    grad_table, grad_pair_weight, grad_cross = in_vmem(
        functools.partial(finish_small_kernel, blocks // 2),
        [((level_count, 4 * half), f32), (pair_weight.shape[::-1], f32), ((1, heads), f32)],
        (mine_small, other_small),
        0,
    )
    grad_pair_weight = grad_pair_weight.T
    grad_cross = grad_cross.reshape(heads)
    return (
        updated,
        grad_tokens,
        grad_pair,
        input_weight_grad,
        output_weight_grad,
        grad_pair_weight,
        grad_cross,
        grad_table,
    )


def solution(mesh):
    fine = Mesh(mesh.devices.reshape(2, 4, 2, 4, 2), ("z_lo", "y", "core", "x", "z_hi"))
    sample = ("z_lo", "y", "core")
    token = ("x", "z_hi")
    placed = (
        P(sample, token, None),
        P(sample),
        P(),
        P(),
        P(),
        P(token, sample, None),
        P(),
        P(),
        P(),
        P(sample, token, None),
    )
    return jax.shard_map(
        shards,
        mesh=fine,
        in_specs=placed,
        out_specs=(
            P(sample, token, None),
            P(sample, token, None),
            P(token, sample, None),
            P(),
            P(),
            P(),
            P(),
            P(),
        ),
        check_vma=False,
    )
```

```python
import functools
import math

import jax
import jax.numpy as jnp
from jax import lax
from jax.experimental import pallas as pl
from jax.experimental.pallas import tpu as pltpu
from jax.sharding import Mesh, PartitionSpec as P

norm_epsilon = 1e-05
bf16 = jnp.bfloat16
f32 = jnp.float32
token_axes = ("x", "z_hi")
head_axes = ("z_lo", "x", "z_hi")
column_axes = ("z_lo", "y")
chip_axes = ("z_lo", "y", "x", "z_hi")
vmem_bytes = 60 * 1024 * 1024


def dot(a, b, dims):
    return lax.dot_general(a, b, (dims, ((), ())), preferred_element_type=f32)


def attend_places(refs):
    near, above, below, first, second = refs

    def find(place, part):
        dcore, dy = place // 4, place % 4
        if dy == 2:
            return (first, second)[part], (dcore, 0)
        return (near, above, None, below)[dy], (dcore, part)

    return find


def rows_of(base_ref, index, part):
    return pl.ds(pl.multiple_of(base_ref[index] * part, part), part)


def attend_kernel(factor, part, base_ref, cross_ref, chain_col_ref, chain_row_ref, rows_ref, *refs):
    bias_at, out_ref, grad_refs, cross_sum_ref = attend_places(refs[:5]), refs[5], refs[6:10], refs[10]
    bias_full, logits, exp_half, grad_half, grad_sum = refs[11:]
    blocks, width, lanes = rows_ref.shape
    size = width // 4
    count = blocks * lanes
    chunk = 256

    @pl.when(pl.program_id(0) == 0)
    def _():
        cross = cross_ref[0]
        for p in range(count // part):
            at = rows_of(base_ref, p, part)
            ref, lead = bias_at(p // 2, p % 2)
            moved = jnp.concatenate(
                [ref[(*lead, slice(part * t, part * (t + 1)))].astype(f32) for t in range(blocks)], axis=1
            )
            shifts = ref[(*lead, slice(part * blocks, part * blocks + 16))].astype(f32)
            shift = jnp.concatenate([shifts[t : t + 1] for t in range(blocks)], axis=1)
            differ = chain_col_ref[at, 0:1] != chain_row_ref[0:1, :]
            bias_full[at, :] = (moved + shift) + jnp.where(differ, cross, 0.0)
            grad_sum[at, :] = jnp.zeros((part, count), f32)

    def take(index):
        return jnp.concatenate(
            [rows_ref[t, index * size : (index + 1) * size, :] for t in range(blocks)], axis=1
        )

    query_t, key_t, value_t, grad_t = take(0), take(1), take(2), take(3)
    key = key_t.T
    value = value_t.T
    query = query_t.T
    peak = jnp.full((1, count), -jnp.inf, f32)
    for p in range(count // chunk):
        at = pl.ds(chunk * p, chunk)
        scores = dot(key[chunk * p : chunk * (p + 1)], query_t, ((1,), (0,))) + bias_full[at, :]
        logits[at, :] = scores
        peak = jnp.maximum(peak, jnp.max(scores, axis=0, keepdims=True))
    for p in range(count // chunk):
        at = pl.ds(chunk * p, chunk)
        exp_half[at, :] = jnp.exp(logits[at, :] - peak).astype(bf16)
    value_ones = jnp.concatenate([value_t, jnp.ones((16, count), bf16)], axis=0)
    summed = dot(value_ones, exp_half[...], ((1,), (0,)))
    inverse = 1.0 / summed[size : size + 1]
    attended_t = summed[:size] * inverse
    scaled_t = (grad_t.astype(f32) * inverse).astype(bf16)
    scaled = scaled_t.T
    delta = jnp.sum(scaled_t.astype(f32) * attended_t, axis=0, keepdims=True)
    key_grad = []
    value_grad = []
    for p in range(count // chunk):
        at = pl.ds(chunk * p, chunk)
        weights = dot(value[chunk * p : chunk * (p + 1)], scaled_t, ((1,), (0,)))
        terms = exp_half[at, :]
        grad = terms.astype(f32) * (weights - delta)
        half = grad.astype(bf16)
        grad_half[at, :] = half
        grad_sum[at, :] += grad
        key_grad.append(dot(half, query, ((1,), (0,))))
        value_grad.append(dot(terms, scaled, ((1,), (0,))))
    query_grad_t = dot(key_t, grad_half[...], ((1,), (0,))) * factor
    key_grad_t = jnp.concatenate(key_grad, axis=0).T
    value_grad_t = jnp.concatenate(value_grad, axis=0).T
    for index, array in enumerate((attended_t, query_grad_t, key_grad_t, value_grad_t)):
        array = array.astype(bf16)
        for t in range(blocks):
            out_ref[t, index * size : (index + 1) * size, :] = array[:, t * lanes : (t + 1) * lanes]

    @pl.when(pl.program_id(0) == pl.num_programs(0) - 1)
    def _():
        cross_sum = jnp.zeros((1, count), f32)
        for p in range(count // part):
            at = rows_of(base_ref, p, part)
            block = grad_sum[at, :]
            differ = chain_col_ref[at, 0:1] != chain_row_ref[0:1, :]
            cross_sum += jnp.sum(jnp.where(differ, block, 0.0), axis=0, keepdims=True)
            half = block.astype(bf16)
            for t in range(blocks):
                grad_refs[p // 2 % 4][p // 8, p % 2, t] = half[:, t * lanes : (t + 1) * lanes]
        cross_sum_ref[...] = jnp.broadcast_to(cross_sum, cross_sum_ref.shape)


def attend(base, rows, biases, cross, chains, factor):
    sources, width, total = rows.shape
    lanes = 128
    blocks = sources // 2
    own = total // lanes
    samples = 2 * own
    count = blocks * lanes
    chain_col, chain_row = chains
    part = (biases[0].shape[2] - 16) // blocks
    once = lambda shape: pl.BlockSpec(
        shape, lambda s: (0,) * len(shape), pipeline_mode=pl.Buffered(1)
    )
    smem = pl.BlockSpec(memory_space=pltpu.SMEM)
    by_sample = pl.BlockSpec((blocks, width, lanes), lambda s: (s // own, 0, s % own))
    block_shape = (2, 2, blocks, part, lanes)
    head_grads, *grad_biases, cross_sum = pl.pallas_call(
        functools.partial(attend_kernel, factor, part),
        grid=(samples,),
        in_specs=[smem, smem, once(chain_col.shape), once(chain_row.shape), by_sample]
        + [once(bias.shape) for bias in biases],
        out_specs=[by_sample] + [once(block_shape)] * 4 + [once((8, count))],
        out_shape=[jax.ShapeDtypeStruct(rows.shape, bf16)]
        + [jax.ShapeDtypeStruct(block_shape, bf16)] * 4
        + [jax.ShapeDtypeStruct((8, count), f32)],
        scratch_shapes=[
            pltpu.VMEM((count, count), f32),
            pltpu.VMEM((count, count), f32),
            pltpu.VMEM((count, count), bf16),
            pltpu.VMEM((count, count), bf16),
            pltpu.VMEM((count, count), f32),
        ],
        compiler_params=pltpu.CompilerParams(vmem_limit_bytes=vmem_bytes),
        cost_estimate=pl.CostEstimate(
            flops=12 * samples * count * count * 48,
            bytes_accessed=16 * 1024 * 1024,
            transcendentals=samples * count * count,
        ),
    )(base, cross, chain_col, chain_row, rows, *biases)
    return head_grads, grad_biases, cross_sum


def norm_parts(wide):
    centred = wide - jnp.mean(wide, axis=1, keepdims=True)
    inv_std = lax.rsqrt(jnp.mean(centred * centred, axis=1, keepdims=True) + norm_epsilon)
    return centred * inv_std, inv_std


def before_kernel(
    factor,
    acts_ref,
    cots_ref,
    mod_ref,
    weight_ref,
    out_weight_ref,
    sent_ref,
    gate_ref,
    grad_gated_ref,
    normed_ref,
):
    rows, width = acts_ref.shape
    heads = sent_ref.shape[0]
    size = sent_ref.shape[1] // 4
    samples = mod_ref.shape[0]
    part = rows // samples
    for s in range(samples):
        at = slice(s * part, (s + 1) * part)
        whitened, _ = norm_parts(acts_ref[at, :].astype(f32))
        scale = 1.0 + mod_ref[s : s + 1, :width]
        shift = mod_ref[s : s + 1, width:]
        normed_ref[at, :] = (whitened * scale + shift).astype(bf16)
    normed = normed_ref[...]

    def project(index):
        return dot(normed, weight_ref[:, index * width : (index + 1) * width], ((1,), (0,)))

    def put(index, array):
        for h in range(heads):
            sent_ref[h, index * size : (index + 1) * size, :] = array[h * size : (h + 1) * size]

    put(0, (project(0) * factor).T.astype(bf16))
    put(1, project(1).T.astype(bf16))
    put(2, project(2).T.astype(bf16))
    gate = jax.nn.sigmoid(project(3)).T
    gate_ref[...] = gate
    grad_gated = dot(cots_ref[...], out_weight_ref[...], ((1,), (1,))).T
    grad_gated_ref[...] = grad_gated
    put(3, (grad_gated * gate).astype(bf16))


def in_vmem(kernel, shapes, operands, flops, smem=0):
    vmem = pl.BlockSpec(memory_space=pltpu.VMEM)
    scalars = [pl.BlockSpec(memory_space=pltpu.SMEM)] * smem
    size = sum(a.size * a.dtype.itemsize for a in operands)
    return pl.pallas_call(
        kernel,
        in_specs=scalars + [vmem] * (len(operands) - smem),
        out_specs=[vmem] * len(shapes),
        out_shape=[jax.ShapeDtypeStruct(shape, kind) for shape, kind in shapes],
        compiler_params=pltpu.CompilerParams(vmem_limit_bytes=vmem_bytes),
        cost_estimate=pl.CostEstimate(flops=flops, bytes_accessed=size, transcendentals=0),
    )(*operands)


def before(acts, cots, modulation, input_weight, output_matrix, heads, factor):
    rows, width = acts.shape
    shapes = [
        ((heads, 4 * width // heads, rows), bf16),
        ((width, rows), f32),
        ((width, rows), f32),
        ((rows, width), bf16),
    ]
    return in_vmem(
        functools.partial(before_kernel, factor),
        shapes,
        (acts, cots, modulation, input_weight, output_matrix),
        10 * rows * width * width,
    )


def gate_kernel(core_ref, back_ref, gate_ref, grad_gated_ref, keep_ref, send_ref):
    heads = back_ref.shape[0]
    size = back_ref.shape[1] // 4
    half = heads * size // 2

    def take(index, side):
        return jnp.concatenate(
            [
                back_ref[h, index * size : (index + 1) * size, :]
                for h in range(side * heads // 2, (side + 1) * heads // 2)
            ],
            axis=0,
        )

    def write(side, ref):
        at = slice(side * half, (side + 1) * half)
        gate = gate_ref[at, :]
        gated = gate * take(0, side).astype(f32)
        ref[0] = gated.astype(bf16)
        for index in (1, 2, 3):
            ref[index] = take(index, side)
        ref[4] = (grad_gated_ref[at, :] * gated * (1.0 - gate)).astype(bf16)

    @pl.when(core_ref[0] == 0)
    def _():
        write(0, keep_ref)
        write(1, send_ref)

    @pl.when(core_ref[0] == 1)
    def _():
        write(1, keep_ref)
        write(0, send_ref)


def rows_kernel(
    core_ref,
    keep_ref,
    send_ref,
    acts_ref,
    cots_ref,
    mod_ref,
    weight_ref,
    out_weight_ref,
    updated_ref,
    grad_ref,
    table_ref,
):
    rows, width = acts_ref.shape
    half = width // 2
    samples = mod_ref.shape[0]
    part = rows // samples
    grad_normed = None
    output = None
    for side, ref in ((core_ref[0], keep_ref), (1 - core_ref[0], send_ref)):
        for index in range(4):
            at = pl.multiple_of((2 * index + side) * half, 128)
            term = dot(ref[index + 1].T, weight_ref[:, pl.ds(at, half)], ((1,), (1,)))
            grad_normed = term if grad_normed is None else grad_normed + term
        at = pl.multiple_of(side * half, 128)
        term = dot(ref[0].T, out_weight_ref[pl.ds(at, half), :], ((1,), (0,)))
        output = term if output is None else output + term
    for s in range(samples):
        at = slice(s * part, (s + 1) * part)
        wide = acts_ref[at, :].astype(f32)
        updated_ref[at, :] = (wide + output[at]).astype(bf16)
        whitened, inv_std = norm_parts(wide)
        grad = grad_normed[at]
        products = grad * whitened
        scaled = grad * (1.0 + mod_ref[s : s + 1, :width])
        moved = scaled - jnp.mean(scaled, axis=1, keepdims=True)
        moved = moved - whitened * jnp.mean(scaled * whitened, axis=1, keepdims=True)
        grad_ref[at, :] = (cots_ref[at, :].astype(f32) + inv_std * moved).astype(bf16)
        for index, array in enumerate((products, grad)):
            total = jnp.sum(array, axis=0, keepdims=True)
            for k in range(2):
                row = 4 * s + 2 * index + k
                table_ref[row : row + 1, :] = total[:, k * half : (k + 1) * half]


def weights_kernel(
    keep_ref,
    got_ref,
    own_normed_ref,
    other_normed_ref,
    own_cots_ref,
    other_cots_ref,
    payload_ref,
    stage,
    stage_out,
    sems,
):
    width = own_normed_ref.shape[1]
    half = width // 2
    groups, depth = stage.shape[1:3]
    gated = jnp.concatenate([keep_ref[0], got_ref[0]], axis=1)
    cots = jnp.concatenate([own_cots_ref[...], other_cots_ref[...]], axis=0)
    out_grad = dot(gated, cots, ((1,), (0,))).astype(bf16)
    for d in range(4 * groups):
        if d < half // 8:
            block = out_grad[16 * (d // 2) : 16 * (d // 2 + 1), half * (d % 2) : half * (d % 2 + 1)]
        else:
            block = jnp.zeros((16, half), bf16)
        stage_out[d // 4, d % 4] = block
    copies = [pltpu.make_async_copy(stage_out, payload_ref.at[:, :, depth:, :], sems.at[4])]
    copies[0].start()
    normed_t = jnp.concatenate([own_normed_ref[...], other_normed_ref[...]], axis=0).T
    for index in range(4):
        grad = jnp.concatenate([keep_ref[index + 1], got_ref[index + 1]], axis=1).T
        weight_grad = dot(normed_t, grad, ((1,), (0,))).astype(bf16)
        for a in range(groups):
            stage[index, a] = weight_grad[depth * a : depth * (a + 1)]
        copy = pltpu.make_async_copy(
            stage.at[index], payload_ref.at[:, index, :depth, :], sems.at[index]
        )
        copy.start()
        copies.append(copy)
    for copy in copies:
        copy.wait()


def weight_payload(*operands):
    rows, width = operands[2].shape
    half = width // 2
    vmem = pl.BlockSpec(memory_space=pltpu.VMEM)
    return pl.pallas_call(
        weights_kernel,
        in_specs=[vmem] * len(operands),
        out_specs=pl.BlockSpec(memory_space=pl.ANY),
        out_shape=jax.ShapeDtypeStruct((16, 4, 64, half), bf16),
        scratch_shapes=[
            pltpu.VMEM((4, 16, 48, half), bf16),
            pltpu.VMEM((16, 4, 16, half), bf16),
            pltpu.SemaphoreType.DMA((5,)),
        ],
        compiler_params=pltpu.CompilerParams(vmem_limit_bytes=vmem_bytes),
        cost_estimate=pl.CostEstimate(
            flops=10 * rows * width * width,
            bytes_accessed=8 * 1024 * 1024,
            transcendentals=0,
        ),
    )(*operands)


def assemble_kernel(place_ref, block_ref, *refs):
    input_ref, output_ref, blocks, stage, stage_out, in_sems, sems = refs[-7:]
    half = blocks.shape[2]
    depth = 48
    groups = in_sems.shape[0]
    chips = blocks.shape[0]
    size = chips // groups
    place = place_ref[0]
    arrivals = []
    for g in range(groups):
        at = slice(size * g, size * (g + 1))
        arrivals.append(pltpu.make_async_copy(block_ref.at[at], blocks.at[at], in_sems.at[g]))
        arrivals[-1].start()
    copies = []
    for g in range(groups):
        arrivals[g].wait()
        for b in range(4):
            for a in range(size // 4 * g, size // 4 * (g + 1)):
                stage[b, depth * a : depth * (a + 1), :] = blocks[4 * a + b, :depth, :].astype(f32)
            rows = slice(size // 4 * depth * g, size // 4 * depth * (g + 1))
            at = pl.multiple_of((2 * b + place) * half, 128)
            copies.append(
                pltpu.make_async_copy(
                    stage.at[b, rows, :],
                    input_ref.at[rows, pl.ds(at, half)],
                    sems.at[len(copies)],
                )
            )
            copies[-1].start()
    for d in range(half // 8):
        stage_out[16 * (d // 2) : 16 * (d // 2 + 1), half * (d % 2) : half * (d % 2 + 1)] = blocks[
            d, depth : depth + 16, :
        ].astype(f32)
    copies.append(pltpu.make_async_copy(stage_out, output_ref.at[place], sems.at[len(copies)]))
    copies[-1].start()
    for copy in copies:
        copy.wait()


def assemble(place, gathered, earlier):
    chips, depth, half = gathered.shape
    width = 2 * half
    groups = 4
    anywhere = pl.BlockSpec(memory_space=pl.ANY)
    return pl.pallas_call(
        assemble_kernel,
        in_specs=[pl.BlockSpec(memory_space=pltpu.SMEM), anywhere] + [anywhere] * len(earlier),
        out_specs=[anywhere, anywhere],
        out_shape=[
            jax.ShapeDtypeStruct((width, 4 * width), f32),
            jax.ShapeDtypeStruct((2, half, width), f32),
        ],
        scratch_shapes=[
            pltpu.VMEM((chips, depth, half), bf16),
            pltpu.VMEM((4, width, half), f32),
            pltpu.VMEM((half, width), f32),
            pltpu.SemaphoreType.DMA((groups,)),
            pltpu.SemaphoreType.DMA((4 * groups + 1,)),
        ],
        input_output_aliases={2 + k: k for k in range(len(earlier))},
        compiler_params=pltpu.CompilerParams(vmem_limit_bytes=vmem_bytes),
        cost_estimate=pl.CostEstimate(
            flops=0, bytes_accessed=10 * 1024 * 1024, transcendentals=0
        ),
    )(place, gathered, *earlier)


def total_kernel(parts_ref, small_ref, out_ref):
    chips, depth, _ = parts_ref.shape
    total = parts_ref[0].astype(f32)
    for p in range(1, chips):
        total = total + parts_ref[p].astype(f32)
    total = total.astype(bf16)
    small = small_ref[...].astype(bf16)
    for p in range(out_ref.shape[0]):
        out_ref[p, :depth, :] = total
        out_ref[p, depth:, :] = small


def gather_small_kernel(block_ref, out_ref):
    zy = out_ref.shape[0]
    blocks = block_ref.shape[0] // zy
    for p in range(zy):
        for parity in range(2):
            total = None
            for t in range(blocks):
                if t // 2 % 2 == parity:
                    term = block_ref[blocks * p + t]
                    total = term if total is None else total + term
            out_ref[p, parity] = total


def finish_small_kernel(sharers, mine_ref, other_ref, table_ref, pair_ref, cross_ref):
    zy, _, rows, half = mine_ref.shape
    levels = table_ref.shape[0]
    heads, lanes = pair_ref.shape
    refs = (mine_ref, other_ref)
    values = jnp.concatenate([ref[...].reshape(zy * 2 * rows, half) for ref in refs], axis=0)
    high = values.astype(bf16)
    low = (values - high.astype(f32)).astype(bf16)
    row = lax.broadcasted_iota(jnp.int32, (rows, 1), 0)
    at = lax.broadcasted_iota(jnp.int32, (rows, levels), 1).astype(f32)
    same = []
    for ref in refs:
        for p in range(zy):
            for parity in range(2):
                lane = 2 * lanes + 2 * heads + parity
                level = ref[p, parity, 6:7, lane : lane + 1] * (1.0 / sharers)
                same.append(level == at)
    for r in range(4):
        hot = jnp.concatenate([jnp.where(s & (row == r), 1.0, 0.0) for s in same], axis=0)
        hot = hot.astype(bf16)
        table_ref[:, r * half : (r + 1) * half] = dot(hot, high, ((0,), (0,))) + dot(
            hot, low, ((0,), (0,))
        )
    sums = jnp.sum(mine_ref[...], axis=0) + jnp.sum(other_ref[...], axis=0)
    per_row = half // lanes
    pair = []
    for h in range(heads):
        parity, j = h // (heads // 2), h % (heads // 2)
        at_row, at_lane = 4 + j // per_row, j % per_row * lanes
        pair.append(sums[parity, at_row : at_row + 1, at_lane : at_lane + lanes])
    pair_ref[...] = jnp.concatenate(pair, axis=0)
    last = sums[0, 6:7, 2 * lanes :] + sums[1, 6:7, 2 * lanes :]
    cross_ref[...] = last[:, :heads] + last[:, heads : 2 * heads]


def ring(array, shift):
    return lax.ppermute(array, "y", [(i, (i + shift) % 4) for i in range(4)])


def spread_bias(near):
    above = ring(near, 3)
    below = ring(near, 1)
    return [near, above, below, ring(below[:, :1], 1), ring(above[:, 1:], 3)]


def sum_bias(near, above, far, below):
    arrived = [near, ring(above, 1), ring(far, 2), ring(below, 3)]
    total = sum(a.astype(f32) for a in arrived)
    return total[0] + swap(total[1].astype(bf16)).astype(f32)


def swap(array):
    return lax.ppermute(array, "core", [(0, 1), (1, 0)])


def exchange(array, axes):
    return lax.all_to_all(array, axes, 0, 0, tiled=True)


def shards(
    activations,
    levels,
    ada_table,
    input_weight,
    output_matrix,
    pair_feats,
    pair_weight,
    cross_bias,
    chains,
    cotangent,
):
    own_samples, row_count, width = activations.shape
    heads = pair_weight.shape[1]
    size = width // heads
    col_count = pair_feats.shape[1]
    level_count = ada_table.shape[0]
    factor = 1.0 / math.sqrt(size)
    core = lax.axis_index("core")
    blocks = lax.axis_size("x") * lax.axis_size("z_hi")
    zy_count = lax.axis_size("z_lo") * lax.axis_size("y")
    chip_count = blocks * zy_count
    half = width // 2

    pair_part = jnp.einsum("ijc,ch->hji", pair_feats, pair_weight, preferred_element_type=f32)
    shift = jnp.max(pair_part, axis=1, keepdims=True).astype(bf16)
    moved = (pair_part - shift.astype(f32)).astype(bf16)
    bias_sent = jnp.concatenate(
        [moved, jnp.broadcast_to(shift, (heads, 16, row_count))], axis=1
    )
    bias_got = exchange(bias_sent, head_axes)

    core_at = jnp.reshape(core, (1,)).astype(jnp.int32)
    acts = activations.reshape(-1, width)
    cots = cotangent.reshape(-1, width)
    onehot = (
        levels[:, None] == lax.broadcasted_iota(jnp.int32, (own_samples, level_count), 1)
    ).astype(bf16)
    modulation = jnp.dot(onehot, ada_table, preferred_element_type=f32)
    sent, gate_open, grad_gated, normed = before(
        acts, cots, modulation, input_weight, output_matrix, heads, factor
    )
    count = chains.shape[0]
    chain_col = jnp.broadcast_to(chains[:, None], (count, 128))
    chain_row = jnp.broadcast_to(chains[None, :], (8, count))
    sent, bias_got = lax.optimization_barrier((sent, bias_got))
    bias_own = jnp.concatenate(
        [
            bias_got[:, :col_count].reshape(2, blocks * col_count, row_count),
            bias_got[:, col_count].reshape(2, blocks, row_count),
            bias_got[:, col_count].reshape(2, blocks, row_count),
        ],
        axis=1,
    )
    near = jnp.stack([bias_own, swap(bias_own)])
    sent, near = lax.optimization_barrier((sent, near))
    biases = spread_bias(near)
    biases[3], chain_col, chain_row = lax.optimization_barrier((biases[3], chain_col, chain_row))
    head_rows = exchange(sent, head_axes)
    y_at = lax.axis_index("y")
    base = jnp.stack(
        [
            ((p % 2) * 4 + (y_at + p // 2) % 4) * 2 + (core + p // 8) % 2
            for p in range(16)
        ]
    ).astype(jnp.int32)
    head = lax.axis_index(head_axes)
    own_cross = lax.dynamic_slice_in_dim(cross_bias, head, 1)
    other_normed = swap(normed)
    other_cots = swap(cots)
    head_grads, grad_biases, cross_sum = attend(
        base, head_rows, biases, own_cross, (chain_col, chain_row), factor
    )

    back = exchange(head_grads, head_axes)
    half_shape = ((5, half, acts.shape[0]), bf16)
    keep, send = in_vmem(
        gate_kernel, [half_shape] * 2, (core_at, back, gate_open, grad_gated), 0, 1
    )
    got = swap(send)
    updated, grad_tokens, table_rows = in_vmem(
        rows_kernel,
        [(acts.shape, bf16), (acts.shape, bf16), ((8, half), f32)],
        (core_at, keep, send, acts, cots, modulation, input_weight, output_matrix),
        10 * acts.size * width,
        1,
    )
    updated = updated.reshape(activations.shape)
    grad_tokens = grad_tokens.reshape(activations.shape)
    payload = weight_payload(keep, got, normed, other_normed, cots, other_cots)
    payload = payload.reshape(chip_count, -1, half)

    bias_sum = sum_bias(*grad_biases).astype(bf16)
    grad_bias_half = exchange(bias_sum.reshape(heads, col_count, row_count), head_axes)
    grad_pair = jnp.einsum(
        "hji,ch->ijc", grad_bias_half, pair_weight, preferred_element_type=f32
    ).astype(bf16)
    grad_pair_part = jnp.einsum(
        "ijc,hji->hc", pair_feats, grad_bias_half, preferred_element_type=f32
    )

    parts = exchange(payload, chip_axes)
    cross_part = jnp.sum(cross_sum[0])
    cross_high = cross_part.astype(bf16).astype(f32)
    at_head = (jnp.arange(heads) == head).astype(f32)
    last = jnp.concatenate(
        [at_head * cross_high, at_head * (cross_part - cross_high), levels.astype(f32)]
    )
    halves = jnp.concatenate(
        [table_rows.reshape(2, -1), grad_pair_part.reshape(2, -1)], axis=1
    )
    odd = lax.axis_index("x") % 2
    pick = lambda index: lax.dynamic_index_in_dim(halves, index, 0, keepdims=False)
    shared = pick(odd) + lax.ppermute(pick(1 - odd), "x", [(i, i ^ 1) for i in range(4)])
    flat = jnp.concatenate([shared, last])
    small_depth = 8
    small = jnp.pad(flat, (0, small_depth * half - flat.size)).reshape(small_depth, half)
    (block,) = in_vmem(
        total_kernel,
        [((chip_count, parts.shape[1] + small_depth, half), bf16)],
        (parts, small),
        parts.size,
    )
    gathered = exchange(block, chip_axes)
    pair_shape = grad_pair.shape
    gathered, updated, grad_tokens, grad_pair = lax.optimization_barrier(
        (gathered, updated, grad_tokens, grad_pair.reshape(-1, pair_shape[2]))
    )
    grad_pair = grad_pair.reshape(pair_shape)
    (mine_small,) = in_vmem(
        gather_small_kernel,
        [((zy_count, 2, small_depth, half), f32)],
        (gathered[:, -small_depth:].astype(f32),),
        0,
    )
    other = swap(gathered)
    other_small = swap(mine_small)
    earlier = assemble(core_at, gathered, ())
    input_weight_grad, output_weight_grad = assemble(1 - core_at, other, earlier)
    output_weight_grad = output_weight_grad.reshape(width, width)
    grad_table, grad_pair_weight, grad_cross = in_vmem(
        functools.partial(finish_small_kernel, blocks // 2),
        [((level_count, 4 * half), f32), (pair_weight.shape[::-1], f32), ((1, heads), f32)],
        (mine_small, other_small),
        0,
    )
    grad_pair_weight = grad_pair_weight.T
    grad_cross = grad_cross.reshape(heads)
    return (
        updated,
        grad_tokens,
        grad_pair,
        input_weight_grad,
        output_weight_grad,
        grad_pair_weight,
        grad_cross,
        grad_table,
    )


def solution(mesh):
    fine = Mesh(mesh.devices.reshape(2, 4, 2, 4, 2), ("z_lo", "y", "core", "x", "z_hi"))
    sample = ("z_lo", "y", "core")
    token = ("x", "z_hi")
    placed = (
        P(sample, token, None),
        P(sample),
        P(),
        P(),
        P(),
        P(token, sample, None),
        P(),
        P(),
        P(),
        P(sample, token, None),
    )
    return jax.shard_map(
        shards,
        mesh=fine,
        in_specs=placed,
        out_specs=(
            P(sample, token, None),
            P(sample, token, None),
            P(token, sample, None),
            P(),
            P(),
            P(),
            P(),
            P(),
        ),
        check_vma=False,
    )
```

```python
import functools
import math

import jax
import jax.numpy as jnp
from jax import lax
from jax.experimental import pallas as pl
from jax.experimental.pallas import tpu as pltpu
from jax.sharding import Mesh, PartitionSpec as P

norm_epsilon = 1e-05
bf16 = jnp.bfloat16
f32 = jnp.float32
token_axes = ("x", "z_hi")
head_axes = ("z_lo", "x", "z_hi")
column_axes = ("z_lo", "y")
chip_axes = ("z_lo", "y", "x", "z_hi")
vmem_bytes = 60 * 1024 * 1024


def dot(a, b, dims):
    return lax.dot_general(a, b, (dims, ((), ())), preferred_element_type=f32)


def attend_places(refs):
    near, above, below, first, second = refs

    def find(place, part):
        dcore, dy = place // 4, place % 4
        if dy == 2:
            return (first, second)[part], (dcore, 0)
        return (near, above, None, below)[dy], (dcore, part)

    return find


def rows_of(base_ref, index, part):
    return pl.ds(pl.multiple_of(base_ref[index] * part, part), part)


def attend_kernel(factor, part, base_ref, cross_ref, chain_col_ref, chain_row_ref, rows_ref, *refs):
    bias_at, out_ref, grad_refs, cross_sum_ref = attend_places(refs[:5]), refs[5], refs[6:10], refs[10]
    bias_full, logits, exp_half, grad_half, grad_sum = refs[11:]
    blocks, width, lanes = rows_ref.shape
    size = width // 4
    count = blocks * lanes
    chunk = 256

    @pl.when(pl.program_id(0) == 0)
    def _():
        cross = cross_ref[0]
        for p in range(count // part):
            at = rows_of(base_ref, p, part)
            ref, lead = bias_at(p // 2, p % 2)
            moved = jnp.concatenate(
                [ref[(*lead, slice(part * t, part * (t + 1)))].astype(f32) for t in range(blocks)], axis=1
            )
            shifts = ref[(*lead, slice(part * blocks, part * blocks + 16))].astype(f32)
            shift = jnp.concatenate([shifts[t : t + 1] for t in range(blocks)], axis=1)
            differ = chain_col_ref[at, 0:1] != chain_row_ref[0:1, :]
            bias_full[at, :] = (moved + shift) + jnp.where(differ, cross, 0.0)
            grad_sum[at, :] = jnp.zeros((part, count), f32)

    def take(index):
        return jnp.concatenate(
            [rows_ref[t, index * size : (index + 1) * size, :] for t in range(blocks)], axis=1
        )

    query_t, key_t, value_t, grad_t = take(0), take(1), take(2), take(3)
    key = key_t.T
    value = value_t.T
    query = query_t.T
    peak = jnp.full((1, count), -jnp.inf, f32)
    for p in range(count // chunk):
        at = pl.ds(chunk * p, chunk)
        scores = dot(key[chunk * p : chunk * (p + 1)], query_t, ((1,), (0,))) + bias_full[at, :]
        logits[at, :] = scores
        peak = jnp.maximum(peak, jnp.max(scores, axis=0, keepdims=True))
    for p in range(count // chunk):
        at = pl.ds(chunk * p, chunk)
        exp_half[at, :] = jnp.exp(logits[at, :] - peak).astype(bf16)
    value_ones = jnp.concatenate([value_t, jnp.ones((16, count), bf16)], axis=0)
    summed = dot(value_ones, exp_half[...], ((1,), (0,)))
    inverse = 1.0 / summed[size : size + 1]
    attended_t = summed[:size] * inverse
    scaled_t = (grad_t.astype(f32) * inverse).astype(bf16)
    scaled = scaled_t.T
    delta = jnp.sum(scaled_t.astype(f32) * attended_t, axis=0, keepdims=True)
    key_grad = []
    value_grad = []
    for p in range(count // chunk):
        at = pl.ds(chunk * p, chunk)
        weights = dot(value[chunk * p : chunk * (p + 1)], scaled_t, ((1,), (0,)))
        terms = exp_half[at, :]
        grad = terms.astype(f32) * (weights - delta)
        half = grad.astype(bf16)
        grad_half[at, :] = half
        grad_sum[at, :] += grad
        key_grad.append(dot(half, query, ((1,), (0,))))
        value_grad.append(dot(terms, scaled, ((1,), (0,))))
    query_grad_t = dot(key_t, grad_half[...], ((1,), (0,))) * factor
    key_grad_t = jnp.concatenate(key_grad, axis=0).T
    value_grad_t = jnp.concatenate(value_grad, axis=0).T
    for index, array in enumerate((attended_t, query_grad_t, key_grad_t, value_grad_t)):
        array = array.astype(bf16)
        for t in range(blocks):
            out_ref[t, index * size : (index + 1) * size, :] = array[:, t * lanes : (t + 1) * lanes]

    @pl.when(pl.program_id(0) == pl.num_programs(0) - 1)
    def _():
        cross_sum = jnp.zeros((1, count), f32)
        for p in range(count // part):
            at = rows_of(base_ref, p, part)
            block = grad_sum[at, :]
            differ = chain_col_ref[at, 0:1] != chain_row_ref[0:1, :]
            cross_sum += jnp.sum(jnp.where(differ, block, 0.0), axis=0, keepdims=True)
            half = block.astype(bf16)
            for t in range(blocks):
                grad_refs[p // 2 % 4][p // 8, p % 2, t] = half[:, t * lanes : (t + 1) * lanes]
        cross_sum_ref[...] = jnp.broadcast_to(cross_sum, cross_sum_ref.shape)


def attend(base, rows, biases, cross, chains, factor):
    sources, width, total = rows.shape
    lanes = 128
    blocks = sources // 2
    own = total // lanes
    samples = 2 * own
    count = blocks * lanes
    chain_col, chain_row = chains
    part = (biases[0].shape[2] - 16) // blocks
    once = lambda shape: pl.BlockSpec(
        shape, lambda s: (0,) * len(shape), pipeline_mode=pl.Buffered(1)
    )
    smem = pl.BlockSpec(memory_space=pltpu.SMEM)
    by_sample = pl.BlockSpec((blocks, width, lanes), lambda s: (s // own, 0, s % own))
    block_shape = (2, 2, blocks, part, lanes)
    head_grads, *grad_biases, cross_sum = pl.pallas_call(
        functools.partial(attend_kernel, factor, part),
        grid=(samples,),
        in_specs=[smem, smem, once(chain_col.shape), once(chain_row.shape), by_sample]
        + [once(bias.shape) for bias in biases],
        out_specs=[by_sample] + [once(block_shape)] * 4 + [once((8, count))],
        out_shape=[jax.ShapeDtypeStruct(rows.shape, bf16)]
        + [jax.ShapeDtypeStruct(block_shape, bf16)] * 4
        + [jax.ShapeDtypeStruct((8, count), f32)],
        scratch_shapes=[
            pltpu.VMEM((count, count), f32),
            pltpu.VMEM((count, count), f32),
            pltpu.VMEM((count, count), bf16),
            pltpu.VMEM((count, count), bf16),
            pltpu.VMEM((count, count), f32),
        ],
        compiler_params=pltpu.CompilerParams(vmem_limit_bytes=vmem_bytes),
        cost_estimate=pl.CostEstimate(
            flops=12 * samples * count * count * 48,
            bytes_accessed=16 * 1024 * 1024,
            transcendentals=samples * count * count,
        ),
    )(base, cross, chain_col, chain_row, rows, *biases)
    return head_grads, grad_biases, cross_sum


def norm_parts(wide):
    centred = wide - jnp.mean(wide, axis=1, keepdims=True)
    inv_std = lax.rsqrt(jnp.mean(centred * centred, axis=1, keepdims=True) + norm_epsilon)
    return centred * inv_std, inv_std


def before_kernel(
    factor,
    acts_ref,
    cots_ref,
    mod_ref,
    weight_ref,
    out_weight_ref,
    sent_ref,
    gate_ref,
    grad_gated_ref,
    normed_ref,
):
    rows, width = acts_ref.shape
    heads = sent_ref.shape[0]
    size = sent_ref.shape[1] // 4
    samples = mod_ref.shape[0]
    part = rows // samples
    for s in range(samples):
        at = slice(s * part, (s + 1) * part)
        whitened, _ = norm_parts(acts_ref[at, :].astype(f32))
        scale = 1.0 + mod_ref[s : s + 1, :width]
        shift = mod_ref[s : s + 1, width:]
        normed_ref[at, :] = (whitened * scale + shift).astype(bf16)
    normed = normed_ref[...]

    def project(index):
        return dot(normed, weight_ref[:, index * width : (index + 1) * width], ((1,), (0,)))

    def put(index, array):
        for h in range(heads):
            sent_ref[h, index * size : (index + 1) * size, :] = array[h * size : (h + 1) * size]

    put(0, (project(0) * factor).T.astype(bf16))
    put(1, project(1).T.astype(bf16))
    put(2, project(2).T.astype(bf16))
    gate = jax.nn.sigmoid(project(3)).T
    gate_ref[...] = gate
    grad_gated = dot(cots_ref[...], out_weight_ref[...], ((1,), (1,))).T
    grad_gated_ref[...] = grad_gated
    put(3, (grad_gated * gate).astype(bf16))


def in_vmem(kernel, shapes, operands, flops, smem=0):
    vmem = pl.BlockSpec(memory_space=pltpu.VMEM)
    scalars = [pl.BlockSpec(memory_space=pltpu.SMEM)] * smem
    size = sum(a.size * a.dtype.itemsize for a in operands)
    return pl.pallas_call(
        kernel,
        in_specs=scalars + [vmem] * (len(operands) - smem),
        out_specs=[vmem] * len(shapes),
        out_shape=[jax.ShapeDtypeStruct(shape, kind) for shape, kind in shapes],
        compiler_params=pltpu.CompilerParams(vmem_limit_bytes=vmem_bytes),
        cost_estimate=pl.CostEstimate(flops=flops, bytes_accessed=size, transcendentals=0),
    )(*operands)


def before(acts, cots, modulation, input_weight, output_matrix, heads, factor):
    rows, width = acts.shape
    shapes = [
        ((heads, 4 * width // heads, rows), bf16),
        ((width, rows), f32),
        ((width, rows), f32),
        ((rows, width), bf16),
    ]
    return in_vmem(
        functools.partial(before_kernel, factor),
        shapes,
        (acts, cots, modulation, input_weight, output_matrix),
        10 * rows * width * width,
    )


def gate_kernel(core_ref, back_ref, gate_ref, grad_gated_ref, keep_ref, send_ref):
    heads = back_ref.shape[0]
    size = back_ref.shape[1] // 4
    half = heads * size // 2

    def take(index, side):
        return jnp.concatenate(
            [
                back_ref[h, index * size : (index + 1) * size, :]
                for h in range(side * heads // 2, (side + 1) * heads // 2)
            ],
            axis=0,
        )

    def write(side, ref):
        at = slice(side * half, (side + 1) * half)
        gate = gate_ref[at, :]
        gated = gate * take(0, side).astype(f32)
        ref[0] = gated.astype(bf16)
        for index in (1, 2, 3):
            ref[index] = take(index, side)
        ref[4] = (grad_gated_ref[at, :] * gated * (1.0 - gate)).astype(bf16)

    @pl.when(core_ref[0] == 0)
    def _():
        write(0, keep_ref)
        write(1, send_ref)

    @pl.when(core_ref[0] == 1)
    def _():
        write(1, keep_ref)
        write(0, send_ref)


def rows_kernel(
    core_ref,
    keep_ref,
    send_ref,
    acts_ref,
    cots_ref,
    mod_ref,
    weight_ref,
    out_weight_ref,
    updated_ref,
    grad_ref,
    table_ref,
):
    rows, width = acts_ref.shape
    half = width // 2
    samples = mod_ref.shape[0]
    part = rows // samples
    grad_normed = None
    output = None
    for side, ref in ((core_ref[0], keep_ref), (1 - core_ref[0], send_ref)):
        for index in range(4):
            at = pl.multiple_of((2 * index + side) * half, 128)
            term = dot(ref[index + 1].T, weight_ref[:, pl.ds(at, half)], ((1,), (1,)))
            grad_normed = term if grad_normed is None else grad_normed + term
        at = pl.multiple_of(side * half, 128)
        term = dot(ref[0].T, out_weight_ref[pl.ds(at, half), :], ((1,), (0,)))
        output = term if output is None else output + term
    for s in range(samples):
        at = slice(s * part, (s + 1) * part)
        wide = acts_ref[at, :].astype(f32)
        updated_ref[at, :] = (wide + output[at]).astype(bf16)
        whitened, inv_std = norm_parts(wide)
        grad = grad_normed[at]
        products = grad * whitened
        scaled = grad * (1.0 + mod_ref[s : s + 1, :width])
        moved = scaled - jnp.mean(scaled, axis=1, keepdims=True)
        moved = moved - whitened * jnp.mean(scaled * whitened, axis=1, keepdims=True)
        grad_ref[at, :] = (cots_ref[at, :].astype(f32) + inv_std * moved).astype(bf16)
        for index, array in enumerate((products, grad)):
            total = jnp.sum(array, axis=0, keepdims=True)
            for k in range(2):
                row = 4 * s + 2 * index + k
                table_ref[row : row + 1, :] = total[:, k * half : (k + 1) * half]


def weights_kernel(
    keep_ref,
    got_ref,
    own_normed_ref,
    other_normed_ref,
    own_cots_ref,
    other_cots_ref,
    payload_ref,
    stage,
    stage_out,
    sems,
):
    width = own_normed_ref.shape[1]
    half = width // 2
    groups, depth = stage.shape[1:3]
    gated = jnp.concatenate([keep_ref[0], got_ref[0]], axis=1)
    cots = jnp.concatenate([own_cots_ref[...], other_cots_ref[...]], axis=0)
    out_grad = dot(gated, cots, ((1,), (0,))).astype(bf16)
    for d in range(4 * groups):
        if d < half // 8:
            block = out_grad[16 * (d // 2) : 16 * (d // 2 + 1), half * (d % 2) : half * (d % 2 + 1)]
        else:
            block = jnp.zeros((16, half), bf16)
        stage_out[d // 4, d % 4] = block
    copies = [pltpu.make_async_copy(stage_out, payload_ref.at[:, :, depth:, :], sems.at[4])]
    copies[0].start()
    normed_t = jnp.concatenate([own_normed_ref[...], other_normed_ref[...]], axis=0).T
    for index in range(4):
        grad = jnp.concatenate([keep_ref[index + 1], got_ref[index + 1]], axis=1).T
        weight_grad = dot(normed_t, grad, ((1,), (0,))).astype(bf16)
        for a in range(groups):
            stage[index, a] = weight_grad[depth * a : depth * (a + 1)]
        copy = pltpu.make_async_copy(
            stage.at[index], payload_ref.at[:, index, :depth, :], sems.at[index]
        )
        copy.start()
        copies.append(copy)
    for copy in copies:
        copy.wait()


def weight_payload(*operands):
    rows, width = operands[2].shape
    half = width // 2
    vmem = pl.BlockSpec(memory_space=pltpu.VMEM)
    return pl.pallas_call(
        weights_kernel,
        in_specs=[vmem] * len(operands),
        out_specs=pl.BlockSpec(memory_space=pl.ANY),
        out_shape=jax.ShapeDtypeStruct((16, 4, 64, half), bf16),
        scratch_shapes=[
            pltpu.VMEM((4, 16, 48, half), bf16),
            pltpu.VMEM((16, 4, 16, half), bf16),
            pltpu.SemaphoreType.DMA((5,)),
        ],
        compiler_params=pltpu.CompilerParams(vmem_limit_bytes=vmem_bytes),
        cost_estimate=pl.CostEstimate(
            flops=10 * rows * width * width,
            bytes_accessed=8 * 1024 * 1024,
            transcendentals=0,
        ),
    )(*operands)


def assemble_kernel(place_ref, block_ref, *refs):
    input_ref, output_ref, blocks, stage, stage_out, in_sems, sems = refs[-7:]
    half = blocks.shape[2]
    depth = 48
    groups = in_sems.shape[0]
    chips = blocks.shape[0]
    size = chips // groups
    place = place_ref[0]
    arrivals = []
    for g in range(groups):
        at = slice(size * g, size * (g + 1))
        arrivals.append(pltpu.make_async_copy(block_ref.at[at], blocks.at[at], in_sems.at[g]))
        arrivals[-1].start()
    copies = []
    for g in range(groups):
        arrivals[g].wait()
        for b in range(4):
            for a in range(size // 4 * g, size // 4 * (g + 1)):
                stage[b, depth * a : depth * (a + 1), :] = blocks[4 * a + b, :depth, :].astype(f32)
            rows = slice(size // 4 * depth * g, size // 4 * depth * (g + 1))
            at = pl.multiple_of((2 * b + place) * half, 128)
            copies.append(
                pltpu.make_async_copy(
                    stage.at[b, rows, :],
                    input_ref.at[rows, pl.ds(at, half)],
                    sems.at[len(copies)],
                )
            )
            copies[-1].start()
    for d in range(half // 8):
        stage_out[16 * (d // 2) : 16 * (d // 2 + 1), half * (d % 2) : half * (d % 2 + 1)] = blocks[
            d, depth : depth + 16, :
        ].astype(f32)
    copies.append(pltpu.make_async_copy(stage_out, output_ref.at[place], sems.at[len(copies)]))
    copies[-1].start()
    for copy in copies:
        copy.wait()


def assemble(place, gathered, earlier):
    chips, depth, half = gathered.shape
    width = 2 * half
    groups = 4
    anywhere = pl.BlockSpec(memory_space=pl.ANY)
    return pl.pallas_call(
        assemble_kernel,
        in_specs=[pl.BlockSpec(memory_space=pltpu.SMEM), anywhere] + [anywhere] * len(earlier),
        out_specs=[anywhere, anywhere],
        out_shape=[
            jax.ShapeDtypeStruct((width, 4 * width), f32),
            jax.ShapeDtypeStruct((2, half, width), f32),
        ],
        scratch_shapes=[
            pltpu.VMEM((chips, depth, half), bf16),
            pltpu.VMEM((4, width, half), f32),
            pltpu.VMEM((half, width), f32),
            pltpu.SemaphoreType.DMA((groups,)),
            pltpu.SemaphoreType.DMA((4 * groups + 1,)),
        ],
        input_output_aliases={2 + k: k for k in range(len(earlier))},
        compiler_params=pltpu.CompilerParams(vmem_limit_bytes=vmem_bytes),
        cost_estimate=pl.CostEstimate(
            flops=0, bytes_accessed=10 * 1024 * 1024, transcendentals=0
        ),
    )(place, gathered, *earlier)


def total_kernel(parts_ref, small_ref, out_ref):
    chips, depth, _ = parts_ref.shape
    total = parts_ref[0].astype(f32)
    for p in range(1, chips):
        total = total + parts_ref[p].astype(f32)
    total = total.astype(bf16)
    small = small_ref[...].astype(bf16)
    for p in range(out_ref.shape[0]):
        out_ref[p, :depth, :] = total
        out_ref[p, depth:, :] = small


def gather_small_kernel(block_ref, out_ref):
    zy = out_ref.shape[0]
    blocks = block_ref.shape[0] // zy
    for p in range(zy):
        for parity in range(2):
            total = None
            for t in range(blocks):
                if t // 2 % 2 == parity:
                    term = block_ref[blocks * p + t]
                    total = term if total is None else total + term
            out_ref[p, parity] = total


def finish_small_kernel(sharers, mine_ref, other_ref, table_ref, pair_ref, cross_ref):
    zy, _, rows, half = mine_ref.shape
    levels = table_ref.shape[0]
    heads, lanes = pair_ref.shape
    refs = (mine_ref, other_ref)
    values = jnp.concatenate([ref[...].reshape(zy * 2 * rows, half) for ref in refs], axis=0)
    high = values.astype(bf16)
    low = (values - high.astype(f32)).astype(bf16)
    row = lax.broadcasted_iota(jnp.int32, (rows, 1), 0)
    at = lax.broadcasted_iota(jnp.int32, (rows, levels), 1).astype(f32)
    same = []
    for ref in refs:
        for p in range(zy):
            for parity in range(2):
                lane = 2 * lanes + 2 * heads + parity
                level = ref[p, parity, 6:7, lane : lane + 1] * (1.0 / sharers)
                same.append(level == at)
    for r in range(4):
        hot = jnp.concatenate([jnp.where(s & (row == r), 1.0, 0.0) for s in same], axis=0)
        hot = hot.astype(bf16)
        table_ref[:, r * half : (r + 1) * half] = dot(hot, high, ((0,), (0,))) + dot(
            hot, low, ((0,), (0,))
        )
    sums = jnp.sum(mine_ref[...], axis=0) + jnp.sum(other_ref[...], axis=0)
    per_row = half // lanes
    pair = []
    for h in range(heads):
        parity, j = h // (heads // 2), h % (heads // 2)
        at_row, at_lane = 4 + j // per_row, j % per_row * lanes
        pair.append(sums[parity, at_row : at_row + 1, at_lane : at_lane + lanes])
    pair_ref[...] = jnp.concatenate(pair, axis=0)
    last = sums[0, 6:7, 2 * lanes :] + sums[1, 6:7, 2 * lanes :]
    cross_ref[...] = last[:, :heads] + last[:, heads : 2 * heads]


def ring(array, shift):
    return lax.ppermute(array, "y", [(i, (i + shift) % 4) for i in range(4)])


def spread_bias(near):
    above = ring(near, 3)
    below = ring(near, 1)
    return [near, above, below, ring(below[:, :1], 1), ring(above[:, 1:], 3)]


def sum_bias(near, above, far, below):
    arrived = [near, ring(above, 1), ring(far, 2), ring(below, 3)]
    total = sum(a.astype(f32) for a in arrived)
    return total[0] + swap(total[1].astype(bf16)).astype(f32)


def swap(array):
    return lax.ppermute(array, "core", [(0, 1), (1, 0)])


def exchange(array, axes):
    return lax.all_to_all(array, axes, 0, 0, tiled=True)


def shards(
    activations,
    levels,
    ada_table,
    input_weight,
    output_matrix,
    pair_feats,
    pair_weight,
    cross_bias,
    chains,
    cotangent,
):
    own_samples, row_count, width = activations.shape
    heads = pair_weight.shape[1]
    size = width // heads
    col_count = pair_feats.shape[1]
    level_count = ada_table.shape[0]
    factor = 1.0 / math.sqrt(size)
    core = lax.axis_index("core")
    blocks = lax.axis_size("x") * lax.axis_size("z_hi")
    zy_count = lax.axis_size("z_lo") * lax.axis_size("y")
    chip_count = blocks * zy_count
    half = width // 2

    pair_part = jnp.einsum("ijc,ch->hji", pair_feats, pair_weight, preferred_element_type=f32)
    shift = jnp.max(pair_part, axis=1, keepdims=True).astype(bf16)
    moved = (pair_part - shift.astype(f32)).astype(bf16)
    bias_sent = jnp.concatenate(
        [moved, jnp.broadcast_to(shift, (heads, 16, row_count))], axis=1
    )
    bias_got = exchange(bias_sent, head_axes)

    core_at = jnp.reshape(core, (1,)).astype(jnp.int32)
    acts = activations.reshape(-1, width)
    cots = cotangent.reshape(-1, width)
    onehot = (
        levels[:, None] == lax.broadcasted_iota(jnp.int32, (own_samples, level_count), 1)
    ).astype(bf16)
    modulation = jnp.dot(onehot, ada_table, preferred_element_type=f32)
    sent, gate_open, grad_gated, normed = before(
        acts, cots, modulation, input_weight, output_matrix, heads, factor
    )
    count = chains.shape[0]
    chain_col = jnp.broadcast_to(chains[:, None], (count, 128))
    chain_row = jnp.broadcast_to(chains[None, :], (8, count))
    sent, bias_got = lax.optimization_barrier((sent, bias_got))
    bias_own = jnp.concatenate(
        [
            bias_got[:, :col_count].reshape(2, blocks * col_count, row_count),
            bias_got[:, col_count].reshape(2, blocks, row_count),
            bias_got[:, col_count].reshape(2, blocks, row_count),
        ],
        axis=1,
    )
    near = jnp.stack([bias_own, swap(bias_own)])
    sent, near = lax.optimization_barrier((sent, near))
    biases = spread_bias(near)
    biases[1], chain_col, chain_row = lax.optimization_barrier((biases[1], chain_col, chain_row))
    head_rows = exchange(sent, head_axes)
    y_at = lax.axis_index("y")
    base = jnp.stack(
        [
            ((p % 2) * 4 + (y_at + p // 2) % 4) * 2 + (core + p // 8) % 2
            for p in range(16)
        ]
    ).astype(jnp.int32)
    head = lax.axis_index(head_axes)
    own_cross = lax.dynamic_slice_in_dim(cross_bias, head, 1)
    other_normed = swap(normed)
    other_cots = swap(cots)
    head_grads, grad_biases, cross_sum = attend(
        base, head_rows, biases, own_cross, (chain_col, chain_row), factor
    )

    back = exchange(head_grads, head_axes)
    half_shape = ((5, half, acts.shape[0]), bf16)
    keep, send = in_vmem(
        gate_kernel, [half_shape] * 2, (core_at, back, gate_open, grad_gated), 0, 1
    )
    got = swap(send)
    updated, grad_tokens, table_rows = in_vmem(
        rows_kernel,
        [(acts.shape, bf16), (acts.shape, bf16), ((8, half), f32)],
        (core_at, keep, send, acts, cots, modulation, input_weight, output_matrix),
        10 * acts.size * width,
        1,
    )
    updated = updated.reshape(activations.shape)
    grad_tokens = grad_tokens.reshape(activations.shape)
    payload = weight_payload(keep, got, normed, other_normed, cots, other_cots)
    payload = payload.reshape(chip_count, -1, half)

    bias_sum = sum_bias(*grad_biases).astype(bf16)
    grad_bias_half = exchange(bias_sum.reshape(heads, col_count, row_count), head_axes)
    grad_pair = jnp.einsum(
        "hji,ch->ijc", grad_bias_half, pair_weight, preferred_element_type=f32
    ).astype(bf16)
    grad_pair_part = jnp.einsum(
        "ijc,hji->hc", pair_feats, grad_bias_half, preferred_element_type=f32
    )

    parts = exchange(payload, chip_axes)
    cross_part = jnp.sum(cross_sum[0])
    cross_high = cross_part.astype(bf16).astype(f32)
    at_head = (jnp.arange(heads) == head).astype(f32)
    last = jnp.concatenate(
        [at_head * cross_high, at_head * (cross_part - cross_high), levels.astype(f32)]
    )
    halves = jnp.concatenate(
        [table_rows.reshape(2, -1), grad_pair_part.reshape(2, -1)], axis=1
    )
    odd = lax.axis_index("x") % 2
    pick = lambda index: lax.dynamic_index_in_dim(halves, index, 0, keepdims=False)
    shared = pick(odd) + lax.ppermute(pick(1 - odd), "x", [(i, i ^ 1) for i in range(4)])
    flat = jnp.concatenate([shared, last])
    small_depth = 8
    small = jnp.pad(flat, (0, small_depth * half - flat.size)).reshape(small_depth, half)
    (block,) = in_vmem(
        total_kernel,
        [((chip_count, parts.shape[1] + small_depth, half), bf16)],
        (parts, small),
        parts.size,
    )
    gathered = exchange(block, chip_axes)
    pair_shape = grad_pair.shape
    gathered, updated, grad_tokens, grad_pair = lax.optimization_barrier(
        (gathered, updated, grad_tokens, grad_pair.reshape(-1, pair_shape[2]))
    )
    grad_pair = grad_pair.reshape(pair_shape)
    (mine_small,) = in_vmem(
        gather_small_kernel,
        [((zy_count, 2, small_depth, half), f32)],
        (gathered[:, -small_depth:].astype(f32),),
        0,
    )
    other = swap(gathered)
    other_small = swap(mine_small)
    earlier = assemble(core_at, gathered, ())
    input_weight_grad, output_weight_grad = assemble(1 - core_at, other, earlier)
    output_weight_grad = output_weight_grad.reshape(width, width)
    grad_table, grad_pair_weight, grad_cross = in_vmem(
        functools.partial(finish_small_kernel, blocks // 2),
        [((level_count, 4 * half), f32), (pair_weight.shape[::-1], f32), ((1, heads), f32)],
        (mine_small, other_small),
        0,
    )
    grad_pair_weight = grad_pair_weight.T
    grad_cross = grad_cross.reshape(heads)
    return (
        updated,
        grad_tokens,
        grad_pair,
        input_weight_grad,
        output_weight_grad,
        grad_pair_weight,
        grad_cross,
        grad_table,
    )


def solution(mesh):
    fine = Mesh(mesh.devices.reshape(2, 4, 2, 4, 2), ("z_lo", "y", "core", "x", "z_hi"))
    sample = ("z_lo", "y", "core")
    token = ("x", "z_hi")
    placed = (
        P(sample, token, None),
        P(sample),
        P(),
        P(),
        P(),
        P(token, sample, None),
        P(),
        P(),
        P(),
        P(sample, token, None),
    )
    return jax.shard_map(
        shards,
        mesh=fine,
        in_specs=placed,
        out_specs=(
            P(sample, token, None),
            P(sample, token, None),
            P(token, sample, None),
            P(),
            P(),
            P(),
            P(),
            P(),
        ),
        check_vma=False,
    )
```
